32 devices in a mesh: row: 8 (over z, core), col: 4 (over y, x).
Axes of the slice: x: 2, y: 2, z: 4, core: 2. Of those that a mesh axis runs over, the one named last changes fastest.
Arguments:
- tokens: bfloat16 [4, 16, 4, 73728], P(None, 'row', 'col'), may hold values from -6 to 6
- conditioning: float32 [4, 1152], P(None, 'row'), may hold values from -6 to 6
- ada_weight: bfloat16 [2, 8, 4, 248832], P(None, 'row', 'col'), may hold values from -0.1875 to 0.1875
- ada_bias: float32 [2, 6, 1152], P(None, None, 'col'), may hold values from -3 to 3
- qkv_weight: bfloat16 [2, 8, 4, 124416], P(None, 'row', 'col'), may hold values from -1 to 1
- attn_bias: float32 [2, 2, 1152], P(None, None, 'col'), may hold values from -3 to 3
- mixing_weight: bfloat16 [2, 4, 8, 41472], P(None, 'col', 'row'), may hold values from -0.5 to 0.5
- mixing_bias: float32 [2, 1152], P(None, 'col'), may hold values from -3 to 3
- hidden_weight: bfloat16 [2, 8, 4, 165888], P(None, 'row', 'col'), may hold values from -1 to 1
- hidden_bias: float32 [2, 4608], P(None, 'col'), may hold values from -3 to 3
- output_weight: bfloat16 [2, 4, 8, 165888], P(None, 'col', 'row'), may hold values from -0.09375 to 0.09375
- output_bias: float32 [2, 1152], P(None, 'col'), may hold values from -3 to 3
- cotangent: bfloat16 [4, 16, 4, 73728], P(None, None, 'col', 'row'), may hold values from -6 to 6
Outputs:
- result: bfloat16 [4, 16, 4, 73728], P(None, None, 'col', 'row')
- tokens_gradient: float32 [4, 16, 4, 73728], P(None, 'row', 'col')
- conditioning_gradient: float32 [4, 1152], P(None, 'row')
- ada_weight_grad: float32 [2, 8, 4, 248832], P(None, 'row', 'col')
- ada_bias_grad: float32 [2, 6, 1152], P(None, None, 'col')
- qkv_weight_grad: float32 [2, 8, 4, 124416], P(None, 'row', 'col')
- attn_bias_grad: float32 [2, 2, 1152], P(None, None, 'col')
- mixing_weight_grad: float32 [2, 4, 8, 41472], P(None, 'col', 'row')
- mixing_bias_grad: float32 [2, 1152], P(None, 'col')
- hidden_weight_grad: float32 [2, 8, 4, 165888], P(None, 'row', 'col')
- hidden_bias_grad: float32 [2, 4608], P(None, 'col')
- output_weight_grad: float32 [2, 4, 8, 165888], P(None, 'col', 'row')
- output_bias_grad: float32 [2, 1152], P(None, 'col')
The draws below stay inside these ranges and needn't reach their ends.
All inputs are finite; a program needn't handle non-finite values.
Results may differ from the reference program's by a relative error of at most 0.035.
Values may be sent and summed in bfloat16 or wider, within the bound.
No kernel may reach another device: no remote copies, remote signals or barrier semaphores. Data moves between devices by JAX's collectives and lax.ppermute only.
A program may use at most 448 MiB of HBM per device.

```python
import jax
import jax.numpy as jnp
from jax import lax

D = 1152
HEADS = 16
FF = 4608
FRAMES = 16
PLACES = 256
LAYERS = 2
CLIPS = 4
HEAD_DIM = 72
N_ROW = 8
N_COL = 4


def shared_rows(key, plain_shape):
    first, second = jax.random.split(key)
    spread_factor = D ** (-0.5)
    fresh = jax.random.truncated_normal(first, -4.0, 4.0, plain_shape, jnp.float32) * spread_factor
    common_shape = (plain_shape[0], 1) + plain_shape[2:]
    common = jax.random.truncated_normal(second, -4.0, 4.0, common_shape, jnp.float32) * (0.5 * spread_factor)
    return fresh + common


def draw_qkv_weight(key, part):
    drawn = shared_rows(key, (LAYERS, D, 3, D))
    blocked = drawn.reshape(LAYERS, N_ROW, D // N_ROW, 3, N_COL, D // N_COL)
    blocked = jnp.moveaxis(blocked, 4, 2)
    return blocked.reshape(LAYERS, N_ROW, N_COL, D // N_ROW * 3 * (D // N_COL)).astype(jnp.bfloat16)


def draw_hidden_weight(key, part):
    drawn = shared_rows(key, (LAYERS, D, FF))
    blocked = drawn.reshape(LAYERS, N_ROW, D // N_ROW, N_COL, FF // N_COL)
    blocked = jnp.moveaxis(blocked, 3, 2)
    return blocked.reshape(LAYERS, N_ROW, N_COL, D // N_ROW * (FF // N_COL)).astype(jnp.bfloat16)


def block_scale(own_key, shape, cuts, smallest, largest):
    def one(position, shards_of):
        draws = jax.random.uniform(jax.random.fold_in(jax.random.fold_in(own_key, 6), position), (shards_of,), jnp.float32, smallest / len(cuts), largest / len(cuts))
        return jnp.repeat(jnp.exp(draws), shape[position] // shards_of).reshape((-1,) + (1,) * (len(shape) - position - 1))

    loudness = one(*cuts[0])
    for cut in cuts[1:]:
        loudness = loudness * one(*cut)
    return loudness


def normal_values(stream_key, extent, scale, reach, cuts=(), dtype=jnp.bfloat16):
    drawn = scale * jax.random.normal(stream_key, extent, jnp.float32)
    if cuts:
        drawn = drawn * block_scale(stream_key, extent, cuts, -0.22, 0.18)
    return jnp.clip(drawn, -reach, reach).astype(dtype)


def setup_inputs(seed: int = 0) -> dict:
    seeds = jax.random.split(jax.random.key(seed), 14)
    tokens = normal_values(seeds[0], (CLIPS, FRAMES, N_COL, PLACES * (D // N_COL)), 1.0, 6.0, ((1, 8), (2, 4)))
    conditioning = normal_values(seeds[1], (CLIPS, D), 1.0, 6.0, ((1, 8),), jnp.float32)
    ada_weight = normal_values(seeds[2], (LAYERS, N_ROW, N_COL, (D // N_ROW) * 6 * (D // N_COL)), D ** -0.5, 0.1875, ((1, 8), (2, 4)))
    ada_bias = normal_values(seeds[3], (LAYERS, 6, D), 0.5, 3.0, ((2, 4),), jnp.float32)
    qkv_weight = draw_qkv_weight(jax.random.fold_in(seeds[13], 71), 0)
    attn_bias = normal_values(seeds[5], (LAYERS, 2, D), 0.5, 3.0, ((2, 4),), jnp.float32)
    mixing_weight = normal_values(seeds[6], (LAYERS, N_COL, N_ROW, (D // N_COL) * (D // N_ROW)), (D // 9) ** -0.5, 0.5, ((1, 4), (2, 8)))
    mixing_bias = normal_values(seeds[7], (LAYERS, D), 0.5, 3.0, ((1, 4),), jnp.float32)
    hidden_weight = draw_hidden_weight(jax.random.fold_in(seeds[13], 71), 0)
    hidden_bias = normal_values(seeds[9], (LAYERS, FF), 0.5, 3.0, ((1, 4),), jnp.float32)
    output_weight = normal_values(seeds[10], (LAYERS, N_COL, N_ROW, (FF // N_COL) * (D // N_ROW)), FF ** -0.5, 0.09375, ((1, 4), (2, 8)))
    output_bias = normal_values(seeds[11], (LAYERS, D), 0.5, 3.0, ((1, 4),), jnp.float32)
    cotangent = normal_values(seeds[12], (CLIPS, FRAMES, N_COL, PLACES * (D // N_COL)), 1.0, 6.0, ((2, 4), (3, 8)))
    return {"tokens": tokens, "conditioning": conditioning, "ada_weight": ada_weight, "ada_bias": ada_bias, "qkv_weight": qkv_weight, "attn_bias": attn_bias, "mixing_weight": mixing_weight, "mixing_bias": mixing_bias, "hidden_weight": hidden_weight, "hidden_bias": hidden_bias, "output_weight": output_weight, "output_bias": output_bias, "cotangent": cotangent}


@jax.custom_vjp
def low(v):
    return lax.optimization_barrier(v.astype(jnp.bfloat16)).astype(jnp.float32)

@jax.custom_vjp
def low_back(v):
    return v

def low_keep(v):
    return (low(v), None)

def low_pass(kept, grad):
    return (grad,)

def back_keep(v):
    return (v, None)

def back_low(kept, grad):
    return (low(grad),)
low.defvjp(low_keep, low_pass)
low_back.defvjp(back_keep, back_low)
epsilon = 1e-06
highest = lax.Precision.HIGHEST

def product(pattern, left, right):
    return jnp.einsum(pattern, left, right, precision=highest)

def unblock(blocked, first, middle_value, last):
    layers, outer_first, outer_second = blocked.shape[:3]
    spread_out = blocked.reshape((layers, outer_first, outer_second, first) + middle_value + (last,))
    spread_out = jnp.moveaxis(spread_out, 2, 3 + len(middle_value))
    return spread_out.reshape((layers, outer_first * first) + middle_value + (outer_second * last,))

def rebuild_block(plain_layout, outer_first, outer_second, middle_value):
    layers = plain_layout.shape[0]
    first = plain_layout.shape[1] // outer_first
    last = plain_layout.shape[-1] // outer_second
    split_up = plain_layout.reshape((layers, outer_first, first) + middle_value + (outer_second, last))
    split_up = jnp.moveaxis(split_up, 3 + len(middle_value), 2)
    return split_up.reshape((layers, outer_first, outer_second, -1))

def unblock_tokens(blocked):
    clips, frames, groups, merged = blocked.shape
    width = merged // PLACES
    spread_out = blocked.reshape(clips, frames, groups, PLACES, width)
    return jnp.moveaxis(spread_out, 2, 3).reshape(clips, frames, PLACES, groups * width)

def rebuild_block_tokens(plain_layout):
    clips, frames, places, width = plain_layout.shape
    split_up = plain_layout.reshape(clips, frames, places, N_COL, width // N_COL)
    return jnp.moveaxis(split_up, 3, 2).reshape(clips, frames, N_COL, places * (width // N_COL))

def normalize(stream):
    average = lax.optimization_barrier(jnp.mean(stream, -1, keepdims=True))
    variance = lax.optimization_barrier(jnp.mean((stream - average) ** 2, -1, keepdims=True))
    return (stream - average) * lax.rsqrt(variance + epsilon)

def attend(queries, key_rows, value_rows, spatial):
    shape = queries.shape[:-1] + (HEADS, HEAD_DIM)
    if spatial:
        patterns = ('fqhe,fkhe->fhqk', 'fhqk,fkhe->fqhe')
    else:
        patterns = ('qphe,kphe->phqk', 'phqk,kphe->qphe')
    softmax_scale = HEAD_DIM ** (-0.5)
    scores = low_back(softmax_scale * product(patterns[0], queries.reshape(shape), key_rows.reshape(shape)))
    probs = low(jax.nn.softmax(scores, axis=-1))
    mixed = product(patterns[1], probs, value_rows.reshape(shape))
    return mixed.reshape(queries.shape)

def residual_block(stream, modulation, qkv_full, attn_full, mixing_full, mixing_add, hidden_full, hidden_add, output_full, output_add, spatial):
    input_attn = low(normalize(stream) * (1.0 + modulation[1]) + modulation[0])
    qkv_rows = product('fpd,dsk->fpsk', input_attn, qkv_full)
    queries = low_back(low(qkv_rows[:, :, 0] + attn_full[0]))
    key_rows = low_back(low(qkv_rows[:, :, 1]))
    value_rows = low_back(low(qkv_rows[:, :, 2] + attn_full[1]))
    heads_out = low_back(low(attend(queries, key_rows, value_rows, spatial)))
    attn_out = low_back(product('fpk,kd->fpd', heads_out, mixing_full) + mixing_add)
    stream_mid = stream + modulation[2] * attn_out
    input_mlp = low(normalize(stream_mid) * (1.0 + modulation[4]) + modulation[3])
    pre_gelu = low_back(product('fpd,de->fpe', input_mlp, hidden_full) + hidden_add)
    activated = low(jax.nn.gelu(pre_gelu, approximate=True))
    mlp_out = low_back(product('fpe,ed->fpd', activated, output_full) + output_add)
    return stream_mid + modulation[5] * mlp_out

def clip_forward(clip_tokens, clip_cond, params):
    ada_full, ada_add, qkv_full, attn_full, mixing_full, mixing_add, hidden_full, hidden_add, output_full, output_add = params
    cond_act = low(jax.nn.silu(clip_cond))
    modulation = product('d,ldsk->lsk', cond_act, ada_full) + ada_add
    stream = residual_block(clip_tokens, modulation[0], qkv_full[0], attn_full[0], mixing_full[0], mixing_add[0], hidden_full[0], hidden_add[0], output_full[0], output_add[0], True)
    stream = low_back(low(stream))
    stream = residual_block(stream, modulation[1], qkv_full[1], attn_full[1], mixing_full[1], mixing_add[1], hidden_full[1], hidden_add[1], output_full[1], output_add[1], False)
    return stream

def reference(tokens, conditioning, ada_weight, ada_bias, qkv_weight, attn_bias, mixing_weight, mixing_bias, hidden_weight, hidden_bias, output_weight, output_bias, cotangent):
    row_part = D // N_ROW
    col_part = D // N_COL
    params = (unblock(ada_weight.astype(jnp.float32), row_part, (6,), col_part), ada_bias.astype(jnp.float32), unblock(qkv_weight.astype(jnp.float32), row_part, (3,), col_part), attn_bias.astype(jnp.float32), unblock(mixing_weight.astype(jnp.float32), col_part, (), row_part), mixing_bias.astype(jnp.float32), unblock(hidden_weight.astype(jnp.float32), row_part, (), FF // N_COL), hidden_bias.astype(jnp.float32), unblock(output_weight.astype(jnp.float32), FF // N_COL, (), row_part), output_bias.astype(jnp.float32))
    empty_sums = tuple((jnp.zeros(entry.shape, jnp.float32) for entry in params))
    plain_tokens = unblock_tokens(tokens)
    plain_cotangent = unblock_tokens(cotangent)

    def clip_step(running_total, clip_data):
        clip_tokens, clip_cond, clip_cotangent = clip_data
        stream, pullback = jax.vjp(clip_forward, clip_tokens.astype(jnp.float32), clip_cond.astype(jnp.float32), params)
        tokens_part, cond_part, param_parts = pullback(clip_cotangent.astype(jnp.float32))
        running_total = tuple((first + second for first, second in zip(running_total, param_parts)))
        return (running_total, (stream.astype(jnp.bfloat16), tokens_part, cond_part))
    running_total, (result, tokens_gradient, conditioning_gradient) = lax.scan(clip_step, empty_sums, (plain_tokens, conditioning, plain_cotangent))
    return (rebuild_block_tokens(result), rebuild_block_tokens(tokens_gradient), conditioning_gradient, rebuild_block(running_total[0], N_ROW, N_COL, (6,)), running_total[1], rebuild_block(running_total[2], N_ROW, N_COL, (3,)), running_total[3], rebuild_block(running_total[4], N_COL, N_ROW, ()), running_total[5], rebuild_block(running_total[6], N_ROW, N_COL, ()), running_total[7], rebuild_block(running_total[8], N_COL, N_ROW, ()), running_total[9])
```

```python
import jax
import jax.numpy as jnp
from jax import lax
from jax.sharding import PartitionSpec as P

HEAD_DIM = 72


epsilon = 1e-06
highest = lax.Precision.HIGHEST
spatial_forms = ("caqhe,cakhe->cahqk", "cahqk,cakhe->caqhe", "cahqk,caqhe->cakhe")
temporal_forms = ("cqbhe,ckbhe->cbhqk", "cbhqk,ckbhe->cqbhe", "cbhqk,cqbhe->ckbhe")


def matmul(pattern, left, right):
    return jnp.einsum(pattern, left, right, preferred_element_type=jnp.float32)


def split_heads(values):
    return values.reshape(values.shape[:-1] + (values.shape[-1] // HEAD_DIM, HEAD_DIM))


def merge_heads(values):
    return values.reshape(values.shape[:-2] + (values.shape[-2] * values.shape[-1],))


def gelu_tanh(values):
    return jax.nn.gelu(values, approximate=True)


def open_tokens(blocked, width):
    return blocked.reshape(blocked.shape[0], blocked.shape[1], blocked.shape[3] // width, width)


def close_tokens(plain_layout):
    return plain_layout.reshape(
        plain_layout.shape[0],
        plain_layout.shape[1],
        1,
        plain_layout.shape[2] * plain_layout.shape[3],
    )


def close_weight(plain_layout):
    return plain_layout.reshape(plain_layout.shape[0], 1, 1, -1)


def normalize(stream):
    feature_count = stream.shape[-1] * lax.axis_size("col")
    row_total, squares = lax.psum((jnp.sum(stream, -1), jnp.sum(stream * stream, -1)), "col")
    average = row_total / feature_count
    variance = squares / feature_count - average * average
    inverse = lax.rsqrt(variance + epsilon)
    return ((stream - average[..., None]) * inverse[..., None], inverse)


def normalize_back(grad_normed, normed, inverse):
    feature_count = grad_normed.shape[-1] * lax.axis_size("col")
    first, second = lax.psum((jnp.sum(grad_normed, -1), jnp.sum(grad_normed * normed, -1)), "col")
    return inverse[..., None] * (
        grad_normed - first[..., None] / feature_count - normed * second[..., None] / feature_count
    )


def spread(values):
    return lax.all_gather(values, "col", axis=3, tiled=True)


def collect(terms):
    return lax.psum_scatter(
        terms.astype(jnp.bfloat16), "col", scatter_dimension=3, tiled=True
    ).astype(jnp.float32)


def spread_grad(values):
    return lax.all_gather(values, "col", axis=3, tiled=True)


def collect_grad(terms):
    return lax.psum_scatter(
        terms.astype(jnp.bfloat16), "col", scatter_dimension=3, tiled=True
    ).astype(jnp.float32)


def fetch_weights(qkv_weight, mixing_weight, hidden_weight, output_weight, depth):
    return (
        lax.all_gather(qkv_weight[depth], "row", axis=0, tiled=True),
        lax.all_gather(mixing_weight[depth], "row", axis=1, tiled=True),
        lax.all_gather(hidden_weight[depth], "row", axis=0, tiled=True),
        lax.all_gather(output_weight[depth], "row", axis=1, tiled=True),
    )


def attend(queries, key_rows, value_rows, forms):
    softmax_scale = HEAD_DIM ** (-0.5)
    scores = matmul(forms[0], split_heads(queries), split_heads(key_rows)) * softmax_scale
    largest = jnp.max(scores, -1, keepdims=True)
    weights = jnp.exp(scores - largest)
    totals = jnp.sum(weights, -1, keepdims=True)
    probs = (weights / totals).astype(jnp.bfloat16)
    mixed = matmul(forms[1], probs, split_heads(value_rows))
    return (merge_heads(mixed).astype(jnp.bfloat16), largest + jnp.log(totals))


def attend_back(queries, key_rows, value_rows, grad_heads, log_totals, forms):
    softmax_scale = HEAD_DIM ** (-0.5)
    query_split = split_heads(queries)
    key_split = split_heads(key_rows)
    value_split = split_heads(value_rows)
    grad_split = split_heads(grad_heads)
    scores = matmul(forms[0], query_split, key_split) * softmax_scale
    probs = jnp.exp(scores - log_totals)
    grad_values = matmul(forms[2], probs.astype(jnp.bfloat16), grad_split)
    grad_probs = matmul(forms[0], grad_split, value_split)
    row_delta = jnp.sum(probs * grad_probs, -1, keepdims=True)
    grad_scores = (probs * (grad_probs - row_delta)).astype(jnp.bfloat16)
    grad_queries = matmul(forms[1], grad_scores, key_split) * softmax_scale
    grad_keys = matmul(forms[2], grad_scores, query_split) * softmax_scale
    return tuple(
        (
            merge_heads(part_grad).astype(jnp.bfloat16)
            for part_grad in (grad_queries, grad_keys, grad_values)
        )
    )


def residual_forward(stream, modulation, weights, biases, forms):
    qkv_full, mixing_full, hidden_full, output_full = weights
    attn_add, mixing_add, hidden_add, output_add = biases

    def piece_of(column):
        return modulation[:, column][:, None, None, :]

    normed_attn, inv_attn = normalize(stream)
    input_attn = spread((normed_attn * (1.0 + piece_of(1)) + piece_of(0)).astype(jnp.bfloat16))
    qkv_rows = matmul("cabd,dsk->cabsk", input_attn, qkv_full)
    queries = (qkv_rows[..., 0, :] + attn_add[0]).astype(jnp.bfloat16)
    key_rows = qkv_rows[..., 1, :].astype(jnp.bfloat16)
    value_rows = (qkv_rows[..., 2, :] + attn_add[1]).astype(jnp.bfloat16)
    heads_out, log_totals = attend(queries, key_rows, value_rows, forms)
    attn_out = collect(matmul("cabk,kd->cabd", heads_out, mixing_full)) + mixing_add
    stream_mid = stream + piece_of(2) * attn_out
    normed_mlp, inv_mlp = normalize(stream_mid)
    input_mlp = spread((normed_mlp * (1.0 + piece_of(4)) + piece_of(3)).astype(jnp.bfloat16))
    pre_gelu = matmul("cabd,df->cabf", input_mlp, hidden_full) + hidden_add
    activated = gelu_tanh(pre_gelu).astype(jnp.bfloat16)
    mlp_out = collect(matmul("cabf,fd->cabd", activated, output_full)) + output_add
    stream_out = stream_mid + piece_of(5) * mlp_out
    saved = (
        normed_attn,
        inv_attn,
        input_attn,
        queries,
        key_rows,
        value_rows,
        heads_out,
        log_totals,
        attn_out,
        normed_mlp,
        inv_mlp,
        input_mlp,
        pre_gelu,
        activated,
        mlp_out,
    )
    return (stream_out, saved)


def residual_backward(grad_stream, saved, modulation, weights, forms):
    (
        normed_attn,
        inv_attn,
        input_attn,
        queries,
        key_rows,
        value_rows,
        heads_out,
        log_totals,
        attn_out,
        normed_mlp,
        inv_mlp,
        input_mlp,
        pre_gelu,
        activated,
        mlp_out,
    ) = saved
    qkv_full, mixing_full, hidden_full, output_full = weights

    def piece_of(column):
        return modulation[:, column][:, None, None, :]

    grad_mlp = (grad_stream * piece_of(5)).astype(jnp.bfloat16)
    gate_mlp_grad = jnp.sum(grad_stream * mlp_out, (1, 2))
    grad_mlp_all = spread_grad(grad_mlp)
    output_weight_term = matmul("cabf,cabd->fd", activated, grad_mlp_all)
    grad_act = matmul("cabd,fd->cabf", grad_mlp_all, output_full)
    grad_pre = jax.vjp(gelu_tanh, pre_gelu)[1](grad_act)[0].astype(jnp.bfloat16)
    hidden_weight_term = matmul("cabd,cabf->df", input_mlp, grad_pre)
    grad_input_mlp = collect_grad(matmul("cabf,df->cabd", grad_pre, hidden_full))
    shift_mlp_grad = jnp.sum(grad_input_mlp, (1, 2))
    scale_mlp_grad = jnp.sum(grad_input_mlp * normed_mlp, (1, 2))
    grad_mid = grad_stream + normalize_back(
        grad_input_mlp * (1.0 + piece_of(4)), normed_mlp, inv_mlp
    )
    grad_attn = (grad_mid * piece_of(2)).astype(jnp.bfloat16)
    gate_attn_grad = jnp.sum(grad_mid * attn_out, (1, 2))
    grad_attn_all = spread_grad(grad_attn)
    mixing_weight_term = matmul("cabk,cabd->kd", heads_out, grad_attn_all)
    grad_heads = matmul("cabd,kd->cabk", grad_attn_all, mixing_full).astype(jnp.bfloat16)
    grad_queries, grad_keys, grad_values = attend_back(
        queries, key_rows, value_rows, grad_heads, log_totals, forms
    )
    grad_qkv = jnp.stack((grad_queries, grad_keys, grad_values), 3)
    qkv_weight_term = matmul("cabd,cabsk->dsk", input_attn, grad_qkv)
    grad_input_attn = collect_grad(matmul("cabsk,dsk->cabd", grad_qkv, qkv_full))
    shift_attn_grad = jnp.sum(grad_input_attn, (1, 2))
    scale_attn_grad = jnp.sum(grad_input_attn * normed_attn, (1, 2))
    grad_input = grad_mid + normalize_back(
        grad_input_attn * (1.0 + piece_of(1)), normed_attn, inv_attn
    )
    weight_terms = (
        lax.psum_scatter(
            qkv_weight_term.astype(jnp.bfloat16), "row", scatter_dimension=0, tiled=True
        ).astype(jnp.float32),
        lax.psum_scatter(
            mixing_weight_term.astype(jnp.bfloat16), "row", scatter_dimension=1, tiled=True
        ).astype(jnp.float32),
        lax.psum_scatter(
            hidden_weight_term.astype(jnp.bfloat16), "row", scatter_dimension=0, tiled=True
        ).astype(jnp.float32),
        lax.psum_scatter(
            output_weight_term.astype(jnp.bfloat16), "row", scatter_dimension=1, tiled=True
        ).astype(jnp.float32),
    )
    modulation_grad = jnp.stack(
        (
            shift_attn_grad,
            scale_attn_grad,
            gate_attn_grad,
            shift_mlp_grad,
            scale_mlp_grad,
            gate_mlp_grad,
        ),
        1,
    )
    attn_bias_term = jnp.stack(
        (
            jnp.sum(grad_queries.astype(jnp.float32), (0, 1, 2)),
            jnp.sum(grad_values.astype(jnp.float32), (0, 1, 2)),
        )
    )
    bias_terms = (
        attn_bias_term,
        jnp.sum(grad_attn.astype(jnp.float32), (0, 1, 2)),
        jnp.sum(grad_pre.astype(jnp.float32), (0, 1, 2)),
        jnp.sum(grad_mlp.astype(jnp.float32), (0, 1, 2)),
    )
    return (grad_input, weight_terms, modulation_grad, bias_terms)


def tensor_parallel(
    tokens,
    conditioning,
    ada_weight,
    ada_bias,
    qkv_weight,
    attn_bias,
    mixing_weight,
    mixing_bias,
    hidden_weight,
    hidden_bias,
    output_weight,
    output_bias,
    cotangent,
):
    col_width = ada_bias.shape[2]
    row_width = conditioning.shape[1]
    hidden_width = hidden_bias.shape[1]
    layer_count = ada_bias.shape[0]
    ada_weight = ada_weight.reshape(layer_count, row_width, 6, col_width)
    qkv_weight = qkv_weight.reshape(layer_count, row_width, 3, col_width)
    mixing_weight = mixing_weight.reshape(layer_count, col_width, row_width)
    hidden_weight = hidden_weight.reshape(layer_count, row_width, hidden_width)
    output_weight = output_weight.reshape(layer_count, hidden_width, row_width)
    tokens = open_tokens(tokens, col_width)
    cotangent = open_tokens(cotangent, col_width)
    cond_act = jax.nn.silu(conditioning).astype(jnp.bfloat16)
    modulation = lax.psum(
        (
            matmul("cr,rsk->csk", cond_act, ada_weight[0]),
            matmul("cr,rsk->csk", cond_act, ada_weight[1]),
        ),
        "row",
    )
    modulation = (modulation[0] + ada_bias[0][None], modulation[1] + ada_bias[1][None])

    def biases_of(depth):
        return (attn_bias[depth], mixing_bias[depth], hidden_bias[depth], output_bias[depth])

    stream_first = tokens.astype(jnp.float32)
    weights_first = fetch_weights(qkv_weight, mixing_weight, hidden_weight, output_weight, 0)
    output_first, saved_first = residual_forward(
        stream_first, modulation[0], weights_first, biases_of(0), spatial_forms
    )
    moved = lax.all_to_all(
        output_first.astype(jnp.bfloat16), "row", split_axis=2, concat_axis=1, tiled=True
    )
    stream_second = moved.astype(jnp.float32)
    weights_second = fetch_weights(qkv_weight, mixing_weight, hidden_weight, output_weight, 1)
    output_second, saved_second = residual_forward(
        stream_second, modulation[1], weights_second, biases_of(1), temporal_forms
    )
    result = output_second.astype(jnp.bfloat16)
    weights_second = fetch_weights(qkv_weight, mixing_weight, hidden_weight, output_weight, 1)
    saved_second = residual_forward(
        stream_second, modulation[1], weights_second, biases_of(1), temporal_forms
    )[1]
    grad_second, terms_second, modgrad_second, biasgrad_second = residual_backward(
        cotangent.astype(jnp.float32), saved_second, modulation[1], weights_second, temporal_forms
    )
    returned = lax.all_to_all(
        grad_second.astype(jnp.bfloat16), "row", split_axis=1, concat_axis=2, tiled=True
    )
    weights_first = fetch_weights(qkv_weight, mixing_weight, hidden_weight, output_weight, 0)
    saved_first = residual_forward(
        stream_first, modulation[0], weights_first, biases_of(0), spatial_forms
    )[1]
    grad_first, terms_first, modgrad_first, biasgrad_first = residual_backward(
        returned.astype(jnp.float32), saved_first, modulation[0], weights_first, spatial_forms
    )
    summed = (
        lax.psum(jnp.stack((modgrad_first, modgrad_second)).astype(jnp.bfloat16), "row").astype(
            jnp.float32
        ),
        lax.psum(
            jnp.stack((biasgrad_first[0], biasgrad_second[0])).astype(jnp.bfloat16), "row"
        ).astype(jnp.float32),
        lax.psum(
            jnp.stack((biasgrad_first[1], biasgrad_second[1])).astype(jnp.bfloat16), "row"
        ).astype(jnp.float32),
        lax.psum(
            jnp.stack((biasgrad_first[2], biasgrad_second[2])).astype(jnp.bfloat16), "row"
        ).astype(jnp.float32),
        lax.psum(
            jnp.stack((biasgrad_first[3], biasgrad_second[3])).astype(jnp.bfloat16), "row"
        ).astype(jnp.float32),
    )
    modulation_grad = summed[0]
    ada_bias_grad = jnp.sum(modulation_grad, 1)
    ada_weight_grad = jnp.einsum(
        "cr,lcsk->lrsk", cond_act.astype(jnp.float32), modulation_grad, precision=highest
    )
    cond_part = jnp.einsum(
        "lcsk,lrsk->cr", modulation_grad, ada_weight.astype(jnp.float32), precision=highest
    )
    cond_part = lax.psum(cond_part, "col")
    conditioning_gradient = jax.vjp(jax.nn.silu, conditioning)[1](cond_part)[0]
    qkv_weight_grad = jnp.stack((terms_first[0], terms_second[0]))
    mixing_weight_grad = jnp.stack((terms_first[1], terms_second[1]))
    hidden_weight_grad = jnp.stack((terms_first[2], terms_second[2]))
    output_weight_grad = jnp.stack((terms_first[3], terms_second[3]))
    return (
        close_tokens(result),
        close_tokens(grad_first),
        conditioning_gradient,
        close_weight(ada_weight_grad),
        ada_bias_grad,
        close_weight(qkv_weight_grad),
        summed[1],
        close_weight(mixing_weight_grad),
        summed[2],
        close_weight(hidden_weight_grad),
        summed[3],
        close_weight(output_weight_grad),
        summed[4],
    )


def exchange(values, axis, mask):
    count = lax.axis_size(axis)
    return lax.ppermute(values, axis, [(index, index ^ mask) for index in range(count)])


def ordered(mine, theirs, upper):
    return jnp.where(
        upper, jnp.concatenate((theirs, mine), 0), jnp.concatenate((mine, theirs), 0)
    )


def add_low(first, second):
    return (first.astype(jnp.float32) + second.astype(jnp.float32)).astype(jnp.bfloat16)


def gather_weight(shard, place):
    held = shard
    for mask in place.depth_masks:
        held = ordered(held, exchange(held, "row", mask), (place.row & mask) != 0)
    half = held.shape[0] // 2
    across = exchange(held, "col", 1)
    above = exchange(held, "col", 2)
    opposite = jnp.concatenate(
        (exchange(across[:half], "col", 2), exchange(above[half:], "col", 1)), 0
    )
    own = (held, across, above, opposite)
    return (own, tuple(exchange(block, "row", 1) for block in own))


def scatter_weight(own, other, place):
    held, across, above, opposite = (
        add_low(mine, exchange(theirs, "row", 1)) for mine, theirs in zip(own, other)
    )
    half = held.shape[0] // 2
    upper = exchange(opposite[:half], "col", 2)
    lower = exchange(opposite[half:], "col", 1)
    across = jnp.concatenate((add_low(across[:half], upper), across[half:]), 0)
    above = jnp.concatenate((above[:half], add_low(above[half:], lower)), 0)
    total = held.astype(jnp.float32) + exchange(across, "col", 1).astype(jnp.float32)
    total = total + exchange(above, "col", 2).astype(jnp.float32)
    for mask in reversed(place.depth_masks):
        half = total.shape[0] // 2
        total = total.astype(jnp.bfloat16)
        upper = (place.row & mask) != 0
        kept = jnp.where(upper, total[half:], total[:half])
        sent = jnp.where(upper, total[:half], total[half:])
        total = kept.astype(jnp.float32) + exchange(sent, "row", mask).astype(jnp.float32)
    return total


class Place:
    def __init__(self):
        self.row = lax.axis_index("row")
        self.col = lax.axis_index("col")
        self.row_count = lax.axis_size("row")
        self.col_count = lax.axis_size("col")
        self.core = self.row & 1
        self.depth_masks = []
        mask = 2
        while mask < self.row_count:
            self.depth_masks.append(mask)
            mask *= 2


def mine_first(halves, place, axis):
    return jnp.where(place.core == 1, jnp.flip(halves, axis), halves)


def to_halves(features, place):
    width = features.shape[-1]
    lead = features.shape[:-1]
    split_up = features.reshape(lead + (place.row_count // 2, 2, width // place.row_count))
    halves = jnp.swapaxes(split_up, -3, -2).reshape(lead + (2, width // 2))
    return mine_first(halves, place, len(lead))


def from_halves(halves, place):
    lead = halves.shape[:-2]
    half = halves.shape[-1]
    halves = mine_first(halves, place, len(lead))
    split_up = halves.reshape(lead + (2, place.row_count // 2, half // (place.row_count // 2)))
    return jnp.swapaxes(split_up, -3, -2).reshape(lead + (2 * half,))


def relative(stacked, place):
    return [
        lax.dynamic_index_in_dim(stacked, place.col ^ step, 0, keepdims=False)
        for step in range(place.col_count)
    ]


def absolute(blocks, place):
    return jnp.stack(relative(jnp.stack(blocks), place))


def trade(blocks):
    return [
        block if step == 0 else exchange(block, "col", step) for step, block in enumerate(blocks)
    ]


def placing(width, place):
    block = width // place.col_count
    part = width // place.row_count
    feature = lax.broadcasted_iota(jnp.int32, (block, width // 2), 0)
    target = lax.broadcasted_iota(jnp.int32, (block, width // 2), 1)

    def one(step, half):
        whole = feature + (place.col ^ step) * block
        row = whole // part
        matches = ((row & 1) == (place.core ^ half)) & (
            (row // 2) * part + whole % part == target
        )
        return matches.astype(jnp.bfloat16)

    return [[one(step, half) for half in range(2)] for step in range(place.col_count)]


def enter(blocks, placement):
    return jnp.stack(
        [
            sum(matmul("ti,io->to", block, pair[half]) for block, pair in zip(blocks, placement))
            for half in range(2)
        ]
    )


def leave(halves, placement):
    return [
        sum(matmul("to,io->ti", halves[half], pair[half]) for half in range(2)).astype(
            jnp.bfloat16
        )
        for pair in placement
    ]


def norm(stream):
    count = stream.shape[0] * stream.shape[2]
    average = jnp.sum(stream, (0, 2), keepdims=True) / count
    centred = stream - average
    variance = jnp.sum(centred * centred, (0, 2), keepdims=True) / count
    inverse = lax.rsqrt(variance + epsilon)
    return (centred * inverse, inverse)


def norm_back(grad_normed, normed, inverse):
    count = normed.shape[0] * normed.shape[2]
    first = jnp.sum(grad_normed, (0, 2), keepdims=True) / count
    second = jnp.sum(grad_normed * normed, (0, 2), keepdims=True) / count
    return inverse * (grad_normed - first - normed * second)


def inward(halves, own, other):
    return matmul("td,dn->tn", halves[0], own) + matmul("td,dn->tn", halves[1], other)


def outward(blocks, weight):
    return jnp.stack(
        [
            sum(matmul("tn,dn->td", block, part) for block, part in zip(blocks, half))
            for half in weight
        ]
    )


def weight_terms(halves, blocks):
    return tuple(
        tuple(matmul("td,tn->dn", halves[half], block).astype(jnp.bfloat16) for block in blocks)
        for half in range(2)
    )


def block_forward(stream, modulation, weights, biases, group, forms):
    qkv, mixing, hidden, output = weights
    attn_add, mixing_add, hidden_add, output_add = biases

    def piece(column):
        return modulation[column][:, None, :]

    normed_attn, inv_attn = norm(stream)
    input_attn = (normed_attn * (1.0 + piece(1)) + piece(0)).astype(jnp.bfloat16)
    queries, keys, values, heads, logs = ([], [], [], [], [])
    for step in range(len(qkv[0])):
        rows = inward(input_attn, qkv[0][step], qkv[1][step])
        width = rows.shape[1] // 3
        query = (rows[:, :width] + attn_add[step][0]).astype(jnp.bfloat16).reshape((1,) + group + (width,))
        key = rows[:, width : 2 * width].astype(jnp.bfloat16).reshape((1,) + group + (width,))
        value = (rows[:, 2 * width :] + attn_add[step][1]).astype(jnp.bfloat16)
        value = value.reshape((1,) + group + (width,))
        out, log_total = attend(query, key, value, forms)
        queries.append(query)
        keys.append(key)
        values.append(value)
        heads.append(out.reshape(-1, width))
        logs.append(log_total)
    attn_out = outward(heads, mixing) + mixing_add[:, None, :]
    mid = stream + piece(2) * attn_out
    normed_mlp, inv_mlp = norm(mid)
    input_mlp = (normed_mlp * (1.0 + piece(4)) + piece(3)).astype(jnp.bfloat16)
    pre = [
        inward(input_mlp, own, other) + added
        for own, other, added in zip(hidden[0], hidden[1], hidden_add)
    ]
    active = [gelu_tanh(values_in).astype(jnp.bfloat16) for values_in in pre]
    mlp_out = outward(active, output) + output_add[:, None, :]
    saved = (
        normed_attn,
        inv_attn,
        input_attn,
        queries,
        keys,
        values,
        heads,
        logs,
        attn_out,
        normed_mlp,
        inv_mlp,
        input_mlp,
        pre,
        active,
        mlp_out,
    )
    return (mid + piece(5) * mlp_out, saved)


def block_backward(grad, saved, modulation, weights, group, forms):
    (
        normed_attn,
        inv_attn,
        input_attn,
        queries,
        keys,
        values,
        heads,
        logs,
        attn_out,
        normed_mlp,
        inv_mlp,
        input_mlp,
        pre,
        active,
        mlp_out,
    ) = saved
    qkv, mixing, hidden, output = weights

    def piece(column):
        return modulation[column][:, None, :]

    grad_mlp = (piece(5) * grad).astype(jnp.bfloat16)
    gate_mlp = jnp.sum(grad * mlp_out, 1)
    output_terms = weight_terms(grad_mlp, active)
    grad_pre = []
    for own, other, before in zip(output[0], output[1], pre):
        grad_act = inward(grad_mlp, own, other)
        grad_pre.append(jax.vjp(gelu_tanh, before)[1](grad_act)[0].astype(jnp.bfloat16))
    hidden_terms = weight_terms(input_mlp, grad_pre)
    grad_input = outward(grad_pre, hidden)
    shift_mlp = jnp.sum(grad_input, 1)
    scale_mlp = jnp.sum(grad_input * normed_mlp, 1)
    grad_mid = grad + norm_back(grad_input * (1.0 + piece(4)), normed_mlp, inv_mlp)
    grad_attn = (piece(2) * grad_mid).astype(jnp.bfloat16)
    gate_attn = jnp.sum(grad_mid * attn_out, 1)
    mixing_terms = weight_terms(grad_attn, heads)
    grad_qkv = []
    for step in range(len(qkv[0])):
        grad_heads = inward(grad_attn, mixing[0][step], mixing[1][step]).astype(jnp.bfloat16)
        width = grad_heads.shape[1]
        parts = attend_back(
            queries[step],
            keys[step],
            values[step],
            grad_heads.reshape((1,) + group + (width,)),
            logs[step],
            forms,
        )
        grad_qkv.append(jnp.concatenate([part.reshape(-1, width) for part in parts], 1))
    qkv_terms = weight_terms(input_attn, grad_qkv)
    grad_input = outward(grad_qkv, qkv)
    shift_attn = jnp.sum(grad_input, 1)
    scale_attn = jnp.sum(grad_input * normed_attn, 1)
    grad_in = grad_mid + norm_back(grad_input * (1.0 + piece(1)), normed_attn, inv_attn)
    modulation_grad = jnp.stack(
        (shift_attn, scale_attn, gate_attn, shift_mlp, scale_mlp, gate_mlp)
    )

    def total(blocks):
        return [jnp.sum(block.astype(jnp.float32), 0) for block in blocks]

    bias_grads = (
        total(grad_qkv),
        jnp.sum(grad_attn.astype(jnp.float32), 1),
        total(grad_pre),
        jnp.sum(grad_mlp.astype(jnp.float32), 1),
    )
    return (grad_in, (qkv_terms, mixing_terms, hidden_terms, output_terms), modulation_grad, bias_grads)


def token_parallel(
    tokens,
    conditioning,
    ada_weight,
    ada_bias,
    qkv_weight,
    attn_bias,
    mixing_weight,
    mixing_bias,
    hidden_weight,
    hidden_bias,
    output_weight,
    output_bias,
    cotangent,
):
    place = Place()
    col_width = ada_bias.shape[2]
    row_width = conditioning.shape[1]
    hidden_width = hidden_bias.shape[1]
    layer_count = ada_bias.shape[0]
    clip_count = conditioning.shape[0]
    width = col_width * place.col_count
    ada_weight = ada_weight.reshape(layer_count, row_width, 6, col_width)
    qkv_weight = qkv_weight.reshape(layer_count, row_width, 3 * col_width)
    mixing_weight = jnp.swapaxes(mixing_weight.reshape(layer_count, col_width, row_width), 1, 2)
    hidden_weight = hidden_weight.reshape(layer_count, row_width, hidden_width)
    output_weight = jnp.swapaxes(output_weight.reshape(layer_count, hidden_width, row_width), 1, 2)
    tokens = open_tokens(tokens, col_width)
    cotangent = open_tokens(cotangent, col_width)
    first_group = tokens.shape[1:3]
    second_group = cotangent.shape[1:3]
    placement = placing(width, place)

    def arrive(held):
        flat = held.reshape(clip_count, -1, col_width)
        return enter(trade(relative(flat, place)), placement)

    def depart(halves, group):
        blocks = trade(leave(halves.astype(jnp.bfloat16), placement))
        return absolute(blocks, place).reshape((clip_count,) + group + (col_width,))

    stream_first = arrive(tokens)
    cond_act = jax.nn.silu(conditioning).astype(jnp.bfloat16)
    modulation = jnp.stack(
        [matmul("cr,rsk->csk", cond_act, ada_weight[depth]) for depth in range(layer_count)], 1
    )
    modulation = modulation + jnp.where(place.row == 0, ada_bias, 0.0)[None]
    modulation = modulation.reshape(clip_count, -1)
    vectors = jnp.concatenate(
        [value.reshape(-1) for value in (attn_bias, hidden_bias, mixing_bias, output_bias)]
    )
    met = trade([jnp.concatenate((mine, vectors)) for mine in relative(modulation, place)])
    cut = modulation.shape[1]
    modulation = jnp.stack([block[:cut] for block in met])
    mask = 1
    while mask < place.row_count:
        modulation = modulation + exchange(modulation, "row", mask)
        mask *= 2
    modulation = jnp.stack(relative(modulation, place)).reshape(-1, layer_count, 6, col_width)
    modulation = jnp.moveaxis(modulation, 0, 2).reshape(layer_count, 6, width)
    modulation = to_halves(modulation, place)
    attn_add, hidden_add, mixing_add, output_add = ([], [], [], [])
    for block in met:
        rest = block[cut:]
        for kept, value in (
            (attn_add, attn_bias),
            (hidden_add, hidden_bias),
            (mixing_add, mixing_bias),
            (output_add, output_bias),
        ):
            kept.append(rest[: value.size].reshape(value.shape))
            rest = rest[value.size :]

    def whole_vector(blocks):
        joined = jnp.moveaxis(absolute(blocks, place), 0, 1).reshape(layer_count, width)
        return to_halves(joined, place)

    mixing_add = whole_vector(mixing_add)
    output_add = whole_vector(output_add)

    def biases_of(depth):
        return (
            [block[depth] for block in attn_add],
            mixing_add[depth],
            [block[depth] for block in hidden_add],
            output_add[depth],
        )

    weights = [
        tuple(
            gather_weight(shard[depth], place)
            for shard in (qkv_weight, mixing_weight, hidden_weight, output_weight)
        )
        for depth in range(layer_count)
    ]
    output_first, saved_first = block_forward(
        stream_first, modulation[0], weights[0], biases_of(0), first_group, spatial_forms
    )
    moving = mine_first(output_first.astype(jnp.bfloat16), place, 0)
    moving = moving.reshape((2,) + first_group + (width // 2,))
    moved = lax.all_to_all(moving, "row", split_axis=2, concat_axis=1, tiled=True)
    stream_second = mine_first(moved, place, 0).astype(jnp.float32).reshape(2, -1, width // 2)
    output_second, saved_second = block_forward(
        stream_second, modulation[1], weights[1], biases_of(1), second_group, temporal_forms
    )
    result = depart(output_second, second_group)
    grad_second, terms_second, modgrad_second, biasgrad_second = block_backward(
        arrive(cotangent), saved_second, modulation[1], weights[1], second_group, temporal_forms
    )
    moving = mine_first(grad_second.astype(jnp.bfloat16), place, 0)
    moving = moving.reshape((2,) + second_group + (width // 2,))
    moved = lax.all_to_all(moving, "row", split_axis=1, concat_axis=2, tiled=True)
    returned = mine_first(moved, place, 0).astype(jnp.float32).reshape(2, -1, width // 2)
    sums_second = [scatter_weight(own, other, place) for own, other in terms_second]
    grad_first, terms_first, modgrad_first, biasgrad_first = block_backward(
        returned, saved_first, modulation[0], weights[0], first_group, spatial_forms
    )
    tokens_gradient = depart(grad_first, first_group).astype(jnp.float32)
    sums_first = [scatter_weight(own, other, place) for own, other in terms_first]

    def by_block(halves):
        features = from_halves(halves, place)
        features = features.reshape(features.shape[:-1] + (place.col_count, col_width))
        return relative(jnp.moveaxis(features, -2, 0), place)

    modgrad = by_block(jnp.stack((modgrad_first, modgrad_second)))
    mixgrad = by_block(jnp.stack((biasgrad_first[1], biasgrad_second[1])))
    outgrad = by_block(jnp.stack((biasgrad_first[3], biasgrad_second[3])))
    sending = []
    for step in range(place.col_count):
        pieces = [modgrad[step].reshape(-1)]
        for grads in (biasgrad_first, biasgrad_second):
            pieces.append(grads[0][step][:col_width])
            pieces.append(grads[0][step][2 * col_width :])
        for grads in (biasgrad_first, biasgrad_second):
            pieces.append(grads[2][step])
        pieces.append(mixgrad[step].reshape(-1))
        pieces.append(outgrad[step].reshape(-1))
        sending.append(jnp.concatenate(pieces))
    met = trade(sending)
    modgrad = jnp.concatenate([block[:cut] for block in met])
    biasgrad = sum(block[cut:] for block in met)
    small = jnp.concatenate((modgrad, biasgrad))
    mask = 1
    while mask < place.row_count:
        small = small + exchange(small, "row", mask)
        mask *= 2
    modgrad = small[: cut * clip_count].reshape(clip_count, layer_count, 6, col_width)
    modgrad = jnp.moveaxis(jnp.stack(relative(modgrad, place)), 1, 0)
    rest = small[cut * clip_count :]
    bias_grads = []
    for value in (attn_bias, hidden_bias, mixing_bias, output_bias):
        bias_grads.append(rest[: value.size].reshape(value.shape))
        rest = rest[value.size :]
    ada_bias_grad = jnp.sum(modgrad, 1)
    ada_weight_grad = jnp.einsum(
        "cr,lcsk->lrsk", cond_act.astype(jnp.float32), modgrad, precision=highest
    )
    cond_part = jnp.einsum(
        "lcsk,lrsk->cr", modgrad, ada_weight.astype(jnp.float32), precision=highest
    )
    for mask in (1, 2):
        cond_part = cond_part + exchange(cond_part, "col", mask)
    conditioning_gradient = jax.vjp(jax.nn.silu, conditioning)[1](cond_part)[0]

    def both(index, flip):
        pair = jnp.stack((sums_first[index], sums_second[index]))
        return close_weight(jnp.swapaxes(pair, 1, 2) if flip else pair)

    return (
        close_tokens(result),
        close_tokens(tokens_gradient),
        conditioning_gradient,
        close_weight(ada_weight_grad),
        ada_bias_grad,
        both(0, False),
        bias_grads[0],
        both(1, True),
        bias_grads[2],
        both(2, False),
        bias_grads[1],
        both(3, True),
        bias_grads[3],
    )


def suits_tokens(mesh):
    rows, cols = (mesh.shape["row"], mesh.shape["col"])
    return cols == 4 and rows >= 2 and rows & (rows - 1) == 0


def solution(mesh):
    placed = (
        P(None, "row", "col", None),
        P(None, "row"),
        P(None, "row", "col", None),
        P(None, None, "col"),
        P(None, "row", "col", None),
        P(None, None, "col"),
        P(None, "col", "row", None),
        P(None, "col"),
        P(None, "row", "col", None),
        P(None, "col"),
        P(None, "col", "row", None),
        P(None, "col"),
        P(None, None, "col", "row"),
    )
    return jax.shard_map(
        token_parallel if suits_tokens(mesh) else tensor_parallel,
        mesh=mesh,
        in_specs=placed,
        out_specs=(
            P(None, None, "col", "row"),
            P(None, "row", "col", None),
            P(None, "row"),
            P(None, "row", "col", None),
            P(None, None, "col"),
            P(None, "row", "col", None),
            P(None, None, "col"),
            P(None, "col", "row", None),
            P(None, "col"),
            P(None, "row", "col", None),
            P(None, "col"),
            P(None, "col", "row", None),
            P(None, "col"),
        ),
        check_vma=False,
    )
```

```python
import functools

import jax
import jax.numpy as jnp
from jax import lax
from jax.experimental import pallas as pl
from jax.experimental.pallas import tpu as pltpu
from jax.sharding import PartitionSpec as P

HEAD_DIM = 72


epsilon = 1e-06
highest = lax.Precision.HIGHEST
spatial_forms = ("caqhe,cakhe->cahqk", "cahqk,cakhe->caqhe", "cahqk,caqhe->cakhe")
temporal_forms = ("cqbhe,ckbhe->cbhqk", "cbhqk,ckbhe->cqbhe", "cbhqk,cqbhe->ckbhe")


def matmul(pattern, left, right):
    return jnp.einsum(pattern, left, right, preferred_element_type=jnp.float32)


def split_heads(values):
    return values.reshape(values.shape[:-1] + (values.shape[-1] // HEAD_DIM, HEAD_DIM))


def merge_heads(values):
    return values.reshape(values.shape[:-2] + (values.shape[-2] * values.shape[-1],))


def gelu_tanh(values):
    return jax.nn.gelu(values, approximate=True)


def open_tokens(blocked, width):
    return blocked.reshape(blocked.shape[0], blocked.shape[1], blocked.shape[3] // width, width)


def close_tokens(plain_layout):
    return plain_layout.reshape(
        plain_layout.shape[0],
        plain_layout.shape[1],
        1,
        plain_layout.shape[2] * plain_layout.shape[3],
    )


def close_weight(plain_layout):
    return plain_layout.reshape(plain_layout.shape[0], 1, 1, -1)


def normalize(stream):
    feature_count = stream.shape[-1] * lax.axis_size("col")
    row_total, squares = lax.psum((jnp.sum(stream, -1), jnp.sum(stream * stream, -1)), "col")
    average = row_total / feature_count
    variance = squares / feature_count - average * average
    inverse = lax.rsqrt(variance + epsilon)
    return ((stream - average[..., None]) * inverse[..., None], inverse)


def normalize_back(grad_normed, normed, inverse):
    feature_count = grad_normed.shape[-1] * lax.axis_size("col")
    first, second = lax.psum((jnp.sum(grad_normed, -1), jnp.sum(grad_normed * normed, -1)), "col")
    return inverse[..., None] * (
        grad_normed - first[..., None] / feature_count - normed * second[..., None] / feature_count
    )


def spread(values):
    return lax.all_gather(values, "col", axis=3, tiled=True)


def collect(terms):
    return lax.psum_scatter(
        terms.astype(jnp.bfloat16), "col", scatter_dimension=3, tiled=True
    ).astype(jnp.float32)


def spread_grad(values):
    return lax.all_gather(values, "col", axis=3, tiled=True)


def collect_grad(terms):
    return lax.psum_scatter(
        terms.astype(jnp.bfloat16), "col", scatter_dimension=3, tiled=True
    ).astype(jnp.float32)


def fetch_weights(qkv_weight, mixing_weight, hidden_weight, output_weight, depth):
    return (
        lax.all_gather(qkv_weight[depth], "row", axis=0, tiled=True),
        lax.all_gather(mixing_weight[depth], "row", axis=1, tiled=True),
        lax.all_gather(hidden_weight[depth], "row", axis=0, tiled=True),
        lax.all_gather(output_weight[depth], "row", axis=1, tiled=True),
    )


def attend(queries, key_rows, value_rows, forms):
    softmax_scale = HEAD_DIM ** (-0.5)
    scores = matmul(forms[0], split_heads(queries), split_heads(key_rows)) * softmax_scale
    largest = jnp.max(scores, -1, keepdims=True)
    weights = jnp.exp(scores - largest)
    totals = jnp.sum(weights, -1, keepdims=True)
    probs = (weights / totals).astype(jnp.bfloat16)
    mixed = matmul(forms[1], probs, split_heads(value_rows))
    return (merge_heads(mixed).astype(jnp.bfloat16), largest + jnp.log(totals))


def attend_back(queries, key_rows, value_rows, grad_heads, log_totals, forms):
    softmax_scale = HEAD_DIM ** (-0.5)
    query_split = split_heads(queries)
    key_split = split_heads(key_rows)
    value_split = split_heads(value_rows)
    grad_split = split_heads(grad_heads)
    scores = matmul(forms[0], query_split, key_split) * softmax_scale
    probs = jnp.exp(scores - log_totals)
    grad_values = matmul(forms[2], probs.astype(jnp.bfloat16), grad_split)
    grad_probs = matmul(forms[0], grad_split, value_split)
    row_delta = jnp.sum(probs * grad_probs, -1, keepdims=True)
    grad_scores = (probs * (grad_probs - row_delta)).astype(jnp.bfloat16)
    grad_queries = matmul(forms[1], grad_scores, key_split) * softmax_scale
    grad_keys = matmul(forms[2], grad_scores, query_split) * softmax_scale
    return tuple(
        (
            merge_heads(part_grad).astype(jnp.bfloat16)
            for part_grad in (grad_queries, grad_keys, grad_values)
        )
    )


def residual_forward(stream, modulation, weights, biases, forms):
    qkv_full, mixing_full, hidden_full, output_full = weights
    attn_add, mixing_add, hidden_add, output_add = biases

    def piece_of(column):
        return modulation[:, column][:, None, None, :]

    normed_attn, inv_attn = normalize(stream)
    input_attn = spread((normed_attn * (1.0 + piece_of(1)) + piece_of(0)).astype(jnp.bfloat16))
    qkv_rows = matmul("cabd,dsk->cabsk", input_attn, qkv_full)
    queries = (qkv_rows[..., 0, :] + attn_add[0]).astype(jnp.bfloat16)
    key_rows = qkv_rows[..., 1, :].astype(jnp.bfloat16)
    value_rows = (qkv_rows[..., 2, :] + attn_add[1]).astype(jnp.bfloat16)
    heads_out, log_totals = attend(queries, key_rows, value_rows, forms)
    attn_out = collect(matmul("cabk,kd->cabd", heads_out, mixing_full)) + mixing_add
    stream_mid = stream + piece_of(2) * attn_out
    normed_mlp, inv_mlp = normalize(stream_mid)
    input_mlp = spread((normed_mlp * (1.0 + piece_of(4)) + piece_of(3)).astype(jnp.bfloat16))
    pre_gelu = matmul("cabd,df->cabf", input_mlp, hidden_full) + hidden_add
    activated = gelu_tanh(pre_gelu).astype(jnp.bfloat16)
    mlp_out = collect(matmul("cabf,fd->cabd", activated, output_full)) + output_add
    stream_out = stream_mid + piece_of(5) * mlp_out
    saved = (
        normed_attn,
        inv_attn,
        input_attn,
        queries,
        key_rows,
        value_rows,
        heads_out,
        log_totals,
        attn_out,
        normed_mlp,
        inv_mlp,
        input_mlp,
        pre_gelu,
        activated,
        mlp_out,
    )
    return (stream_out, saved)


def residual_backward(grad_stream, saved, modulation, weights, forms):
    (
        normed_attn,
        inv_attn,
        input_attn,
        queries,
        key_rows,
        value_rows,
        heads_out,
        log_totals,
        attn_out,
        normed_mlp,
        inv_mlp,
        input_mlp,
        pre_gelu,
        activated,
        mlp_out,
    ) = saved
    qkv_full, mixing_full, hidden_full, output_full = weights

    def piece_of(column):
        return modulation[:, column][:, None, None, :]

    grad_mlp = (grad_stream * piece_of(5)).astype(jnp.bfloat16)
    gate_mlp_grad = jnp.sum(grad_stream * mlp_out, (1, 2))
    grad_mlp_all = spread_grad(grad_mlp)
    output_weight_term = matmul("cabf,cabd->fd", activated, grad_mlp_all)
    grad_act = matmul("cabd,fd->cabf", grad_mlp_all, output_full)
    grad_pre = jax.vjp(gelu_tanh, pre_gelu)[1](grad_act)[0].astype(jnp.bfloat16)
    hidden_weight_term = matmul("cabd,cabf->df", input_mlp, grad_pre)
    grad_input_mlp = collect_grad(matmul("cabf,df->cabd", grad_pre, hidden_full))
    shift_mlp_grad = jnp.sum(grad_input_mlp, (1, 2))
    scale_mlp_grad = jnp.sum(grad_input_mlp * normed_mlp, (1, 2))
    grad_mid = grad_stream + normalize_back(
        grad_input_mlp * (1.0 + piece_of(4)), normed_mlp, inv_mlp
    )
    grad_attn = (grad_mid * piece_of(2)).astype(jnp.bfloat16)
    gate_attn_grad = jnp.sum(grad_mid * attn_out, (1, 2))
    grad_attn_all = spread_grad(grad_attn)
    mixing_weight_term = matmul("cabk,cabd->kd", heads_out, grad_attn_all)
    grad_heads = matmul("cabd,kd->cabk", grad_attn_all, mixing_full).astype(jnp.bfloat16)
    grad_queries, grad_keys, grad_values = attend_back(
        queries, key_rows, value_rows, grad_heads, log_totals, forms
    )
    grad_qkv = jnp.stack((grad_queries, grad_keys, grad_values), 3)
    qkv_weight_term = matmul("cabd,cabsk->dsk", input_attn, grad_qkv)
    grad_input_attn = collect_grad(matmul("cabsk,dsk->cabd", grad_qkv, qkv_full))
    shift_attn_grad = jnp.sum(grad_input_attn, (1, 2))
    scale_attn_grad = jnp.sum(grad_input_attn * normed_attn, (1, 2))
    grad_input = grad_mid + normalize_back(
        grad_input_attn * (1.0 + piece_of(1)), normed_attn, inv_attn
    )
    weight_terms = (
        lax.psum_scatter(
            qkv_weight_term.astype(jnp.bfloat16), "row", scatter_dimension=0, tiled=True
        ).astype(jnp.float32),
        lax.psum_scatter(
            mixing_weight_term.astype(jnp.bfloat16), "row", scatter_dimension=1, tiled=True
        ).astype(jnp.float32),
        lax.psum_scatter(
            hidden_weight_term.astype(jnp.bfloat16), "row", scatter_dimension=0, tiled=True
        ).astype(jnp.float32),
        lax.psum_scatter(
            output_weight_term.astype(jnp.bfloat16), "row", scatter_dimension=1, tiled=True
        ).astype(jnp.float32),
    )
    modulation_grad = jnp.stack(
        (
            shift_attn_grad,
            scale_attn_grad,
            gate_attn_grad,
            shift_mlp_grad,
            scale_mlp_grad,
            gate_mlp_grad,
        ),
        1,
    )
    attn_bias_term = jnp.stack(
        (
            jnp.sum(grad_queries.astype(jnp.float32), (0, 1, 2)),
            jnp.sum(grad_values.astype(jnp.float32), (0, 1, 2)),
        )
    )
    bias_terms = (
        attn_bias_term,
        jnp.sum(grad_attn.astype(jnp.float32), (0, 1, 2)),
        jnp.sum(grad_pre.astype(jnp.float32), (0, 1, 2)),
        jnp.sum(grad_mlp.astype(jnp.float32), (0, 1, 2)),
    )
    return (grad_input, weight_terms, modulation_grad, bias_terms)


def tensor_parallel(
    tokens,
    conditioning,
    ada_weight,
    ada_bias,
    qkv_weight,
    attn_bias,
    mixing_weight,
    mixing_bias,
    hidden_weight,
    hidden_bias,
    output_weight,
    output_bias,
    cotangent,
):
    col_width = ada_bias.shape[2]
    row_width = conditioning.shape[1]
    hidden_width = hidden_bias.shape[1]
    layer_count = ada_bias.shape[0]
    ada_weight = ada_weight.reshape(layer_count, row_width, 6, col_width)
    qkv_weight = qkv_weight.reshape(layer_count, row_width, 3, col_width)
    mixing_weight = mixing_weight.reshape(layer_count, col_width, row_width)
    hidden_weight = hidden_weight.reshape(layer_count, row_width, hidden_width)
    output_weight = output_weight.reshape(layer_count, hidden_width, row_width)
    tokens = open_tokens(tokens, col_width)
    cotangent = open_tokens(cotangent, col_width)
    cond_act = jax.nn.silu(conditioning).astype(jnp.bfloat16)
    modulation = lax.psum(
        (
            matmul("cr,rsk->csk", cond_act, ada_weight[0]),
            matmul("cr,rsk->csk", cond_act, ada_weight[1]),
        ),
        "row",
    )
    modulation = (modulation[0] + ada_bias[0][None], modulation[1] + ada_bias[1][None])

    def biases_of(depth):
        return (attn_bias[depth], mixing_bias[depth], hidden_bias[depth], output_bias[depth])

    stream_first = tokens.astype(jnp.float32)
    weights_first = fetch_weights(qkv_weight, mixing_weight, hidden_weight, output_weight, 0)
    output_first, saved_first = residual_forward(
        stream_first, modulation[0], weights_first, biases_of(0), spatial_forms
    )
    moved = lax.all_to_all(
        output_first.astype(jnp.bfloat16), "row", split_axis=2, concat_axis=1, tiled=True
    )
    stream_second = moved.astype(jnp.float32)
    weights_second = fetch_weights(qkv_weight, mixing_weight, hidden_weight, output_weight, 1)
    output_second, saved_second = residual_forward(
        stream_second, modulation[1], weights_second, biases_of(1), temporal_forms
    )
    result = output_second.astype(jnp.bfloat16)
    weights_second = fetch_weights(qkv_weight, mixing_weight, hidden_weight, output_weight, 1)
    saved_second = residual_forward(
        stream_second, modulation[1], weights_second, biases_of(1), temporal_forms
    )[1]
    grad_second, terms_second, modgrad_second, biasgrad_second = residual_backward(
        cotangent.astype(jnp.float32), saved_second, modulation[1], weights_second, temporal_forms
    )
    returned = lax.all_to_all(
        grad_second.astype(jnp.bfloat16), "row", split_axis=1, concat_axis=2, tiled=True
    )
    weights_first = fetch_weights(qkv_weight, mixing_weight, hidden_weight, output_weight, 0)
    saved_first = residual_forward(
        stream_first, modulation[0], weights_first, biases_of(0), spatial_forms
    )[1]
    grad_first, terms_first, modgrad_first, biasgrad_first = residual_backward(
        returned.astype(jnp.float32), saved_first, modulation[0], weights_first, spatial_forms
    )
    summed = (
        lax.psum(jnp.stack((modgrad_first, modgrad_second)).astype(jnp.bfloat16), "row").astype(
            jnp.float32
        ),
        lax.psum(
            jnp.stack((biasgrad_first[0], biasgrad_second[0])).astype(jnp.bfloat16), "row"
        ).astype(jnp.float32),
        lax.psum(
            jnp.stack((biasgrad_first[1], biasgrad_second[1])).astype(jnp.bfloat16), "row"
        ).astype(jnp.float32),
        lax.psum(
            jnp.stack((biasgrad_first[2], biasgrad_second[2])).astype(jnp.bfloat16), "row"
        ).astype(jnp.float32),
        lax.psum(
            jnp.stack((biasgrad_first[3], biasgrad_second[3])).astype(jnp.bfloat16), "row"
        ).astype(jnp.float32),
    )
    modulation_grad = summed[0]
    ada_bias_grad = jnp.sum(modulation_grad, 1)
    ada_weight_grad = jnp.einsum(
        "cr,lcsk->lrsk", cond_act.astype(jnp.float32), modulation_grad, precision=highest
    )
    cond_part = jnp.einsum(
        "lcsk,lrsk->cr", modulation_grad, ada_weight.astype(jnp.float32), precision=highest
    )
    cond_part = lax.psum(cond_part, "col")
    conditioning_gradient = jax.vjp(jax.nn.silu, conditioning)[1](cond_part)[0]
    qkv_weight_grad = jnp.stack((terms_first[0], terms_second[0]))
    mixing_weight_grad = jnp.stack((terms_first[1], terms_second[1]))
    hidden_weight_grad = jnp.stack((terms_first[2], terms_second[2]))
    output_weight_grad = jnp.stack((terms_first[3], terms_second[3]))
    return (
        close_tokens(result),
        close_tokens(grad_first),
        conditioning_gradient,
        close_weight(ada_weight_grad),
        ada_bias_grad,
        close_weight(qkv_weight_grad),
        summed[1],
        close_weight(mixing_weight_grad),
        summed[2],
        close_weight(hidden_weight_grad),
        summed[3],
        close_weight(output_weight_grad),
        summed[4],
    )


def exchange(values, axis, mask):
    count = lax.axis_size(axis)
    return lax.ppermute(values, axis, [(index, index ^ mask) for index in range(count)])


def add_low(first, second):
    return (first.astype(jnp.float32) + second.astype(jnp.float32)).astype(jnp.bfloat16)


def after(values, *others):
    return lax.optimization_barrier((values,) + others)[0]


def together(*values):
    return lax.optimization_barrier(values)


def over_depth(values, place):
    groups = [list(range(core, place.row_count, 2)) for core in range(2)]
    return lax.all_to_all(
        values, "row", split_axis=0, concat_axis=0, tiled=True, axis_index_groups=groups
    )


def swap(values):
    return exchange(values, "row", 1)


class Gathering:
    def __init__(self, place):
        self.place = place
        self.held = ()
        self.plane = ()
        self.corner = ()
        self.sent = ()
        self.done = []

    def step(self, shard, *gates):
        groups = (self.held, self.plane, self.corner)
        values = list(together(*[value for group in groups for value in group], *gates))
        held, plane, corner = [[values.pop(0) for _ in group] for group in groups]
        across, above = ([], [])
        if held:
            across.append(held[0])
            above.append(held[0])
        if plane:
            size = plane[0].shape[0]
            across.append(plane[2][size // 2 : size])
            above.append(plane[1][: size // 2])
        across = [jnp.concatenate(across, 0)] if across else []
        above = [jnp.concatenate(above, 0)] if above else []
        self.sent = tuple(across + above)
        self.held = ()
        if shard is not None:
            self.held = (over_depth(after(shard, *self.sent), self.place),)
        if corner:
            own = pack_blocks(after(corner, *self.sent))
            self.done.append((own, swap(own)))
        met = tuple(
            exchange(value[0], "col", mask) for mask, value in ((1, across), (2, above)) if value
        )
        self.corner = tuple(plane) + met if plane else ()
        self.plane = tuple(held) + met if held else ()


def scatter_corner(blocks):
    held, across_upper, across_first, above_first, above_lower = blocks
    return (
        held,
        across_upper,
        exchange(across_first, "col", 1),
        exchange(above_first, "col", 2),
        above_lower,
    )


def scatter_sides(blocks):
    held, across_upper, across_first, above_first, above_lower = blocks
    half = across_upper.shape[0]
    return (
        add_low(across_upper, above_first[half:]),
        add_low(above_lower, across_first[half:]),
    )


def scatter_plane(blocks, sides):
    held, _, across_first, above_first, _ = blocks
    across, above = sides
    return (held, exchange(across, "col", 1), across_first, above_first, exchange(above, "col", 2))


def add_all(pieces, place):
    count = place.row_count // 2
    pieces = pieces.reshape((count, -1) + pieces.shape[1:])
    return jnp.sum(pieces.astype(jnp.float32), 0)


class Place:
    def __init__(self):
        self.row = lax.axis_index("row")
        self.col = lax.axis_index("col")
        self.row_count = lax.axis_size("row")
        self.col_count = lax.axis_size("col")
        self.core = self.row & 1
        self.depth_masks = []
        mask = 2
        while mask < self.row_count:
            self.depth_masks.append(mask)
            mask *= 2


def mine_first(halves, place, axis):
    return jnp.where(place.core == 1, jnp.flip(halves, axis), halves)


def to_halves(features, place):
    width = features.shape[-1]
    lead = features.shape[:-1]
    split_up = features.reshape(lead + (place.row_count // 2, 2, width // place.row_count))
    halves = jnp.swapaxes(split_up, -3, -2).reshape(lead + (2, width // 2))
    return mine_first(halves, place, len(lead))


def from_halves(halves, place):
    lead = halves.shape[:-2]
    half = halves.shape[-1]
    halves = mine_first(halves, place, len(lead))
    split_up = halves.reshape(lead + (2, place.row_count // 2, half // (place.row_count // 2)))
    return jnp.swapaxes(split_up, -3, -2).reshape(lead + (2 * half,))


def relative(stacked, place):
    return [
        lax.dynamic_index_in_dim(stacked, place.col ^ step, 0, keepdims=False)
        for step in range(place.col_count)
    ]


def absolute(blocks, place):
    return jnp.stack(relative(jnp.stack(blocks), place))


def trade(blocks):
    return [
        block if step == 0 else exchange(block, "col", step) for step, block in enumerate(blocks)
    ]


PLAIN = ((1,), (0,))
TURNED = ((1,), (1,))
SUMMED = ((0,), (0,))
VMEM_BYTES = 58 * 1024 * 1024
LANES = 128
IN_HBM = pl.BlockSpec(memory_space=pl.ANY)
SMALL_COST = pl.CostEstimate(flops=0, bytes_accessed=0, transcendentals=0)


def dot(left, right, dims):
    return lax.dot_general(left, right, (dims, ((), ())), preferred_element_type=jnp.float32)


def round_up(value):
    return -(-value // LANES) * LANES


def whole(shape):
    return pl.BlockSpec(shape, lambda step: (0,) * len(shape))


def stepped(shape):
    return pl.BlockSpec((1,) + shape, lambda step: (step,) + (0,) * len(shape))


def of(shape, dtype):
    return jax.ShapeDtypeStruct(shape, dtype)


def norm_parts(stream_ref):
    first, second = (stream_ref[0], stream_ref[1])
    count = 2 * first.shape[1]
    average = (jnp.sum(first, 1, keepdims=True) + jnp.sum(second, 1, keepdims=True)) / count
    first, second = (first - average, second - average)
    variance = (
        jnp.sum(first * first, 1, keepdims=True) + jnp.sum(second * second, 1, keepdims=True)
    ) / count
    inverse = lax.rsqrt(variance + epsilon)
    return (first * inverse, second * inverse, inverse)


def norm_grads(stream_ref, acc, mod_ref, scale_row, grad_ref, out_ref, small_ref):
    normed = norm_parts(stream_ref)
    inverse = normed[2]
    count = 2 * normed[0].shape[1]
    weighted = []
    for half in range(2):
        grad_input = acc[half]
        small_ref[half, 0:1, :] = jnp.sum(grad_input, 0, keepdims=True)
        small_ref[half, 1:2, :] = jnp.sum(grad_input * normed[half], 0, keepdims=True)
        weighted.append(grad_input * (1.0 + mod_ref[half, scale_row : scale_row + 1, :]))
    first = sum(jnp.sum(value, 1, keepdims=True) for value in weighted) / count
    second = (
        sum(jnp.sum(value * normed[half], 1, keepdims=True) for half, value in enumerate(weighted))
        / count
    )
    for half in range(2):
        out_ref[half] = grad_ref[half] + inverse * (
            weighted[half] - first - normed[half] * second
        )


def same_place(size, period):
    row = lax.broadcasted_iota(jnp.int32, (size, size), 0)
    column = lax.broadcasted_iota(jnp.int32, (size, size), 1)
    return (row % period) == (column % period)


def attention_kernel(size, period, steps, *refs):
    stream_ref, mod_ref, bias_ref, added_ref = refs[:4]
    weights = refs[4:6]
    mid_ref, mine_ref, other_ref, qkv_ref, heads_ref, log_ref, out_ref, acc = refs[6:]
    input_refs = (mine_ref, other_ref)
    step = pl.program_id(0)
    tokens = stream_ref.shape[1]
    used = qkv_ref.shape[2]
    padded = heads_ref.shape[2]
    columns = weights[0].shape[2]
    width = columns // 4
    count = width // HEAD_DIM
    scale = HEAD_DIM ** (-0.5)

    @pl.when(step == 0)
    def _():
        normed = norm_parts(stream_ref)
        for half in range(2):
            input_refs[half][...] = (
                normed[half] * (1.0 + mod_ref[half, 1:2, :]) + mod_ref[half, 0:1, :]
            ).astype(jnp.bfloat16)
        acc[...] = jnp.zeros_like(acc)

    rows = dot(input_refs[0][...], weights[0][0, :, :used], PLAIN)
    rows = rows + dot(input_refs[1][...], weights[1][0, :, :used], PLAIN) + bias_ref[0]
    lane = lax.broadcasted_iota(jnp.int32, rows.shape, 1)
    qkv_ref[0] = jnp.where(lane < 3 * width, rows, 0.0).astype(jnp.bfloat16)
    log_lane = lax.broadcasted_iota(jnp.int32, (size, LANES), 1)
    for group in range(tokens // size):
        block = qkv_ref[0, group * size : (group + 1) * size, :]
        outs = [jnp.zeros((size, padded - width), jnp.float32)]
        logs = jnp.zeros((size, LANES), jnp.float32)
        for head in range(count):
            start = head * HEAD_DIM
            query = block[:, start : start + HEAD_DIM]
            key = block[:, width + start : width + start + HEAD_DIM]
            value = block[:, 2 * width + start : 2 * width + start + HEAD_DIM]
            scores = dot(query, key, TURNED) * scale
            if period:
                scores = jnp.where(same_place(size, period), scores, -1e30)
            largest = jnp.max(scores, 1, keepdims=True)
            weight = jnp.exp(scores - largest)
            total = jnp.sum(weight, 1, keepdims=True)
            probs = (weight * (1.0 / total)).astype(jnp.bfloat16)
            outs.append(dot(probs, value, PLAIN))
            logs = jnp.where(log_lane == head, largest + jnp.log(total), logs)
        heads_ref[0, group * size : (group + 1) * size, :] = jnp.concatenate(outs, 1).astype(
            jnp.bfloat16
        )
        log_ref[0, group * size : (group + 1) * size, :] = logs
    for half in range(2):
        acc[half] += dot(heads_ref[0], weights[half][0, :, columns - padded :], TURNED)

    @pl.when(step == steps - 1)
    def _():
        for half in range(2):
            total = acc[half] + added_ref[half]
            out_ref[half] = total.astype(jnp.bfloat16)
            mid_ref[half] = stream_ref[half] + mod_ref[half, 2:3, :] * total


def attention_forward(stream, modulation, weights, bias, added, size, period):
    steps = weights[0].shape[0]
    _, tokens, half = stream.shape
    columns = weights[0].shape[2]
    used = round_up(3 * columns // 4)
    padded = columns - (3 * columns // 4) // LANES * LANES
    bf16, f32 = (jnp.bfloat16, jnp.float32)
    return pl.pallas_call(
        functools.partial(attention_kernel, size, period, steps),
        grid=(steps,),
        in_specs=[
            whole(stream.shape),
            whole(modulation.shape),
            stepped((1, used)),
            whole(added.shape),
        ]
        + [stepped((half, columns))] * 2,
        out_specs=[
            whole(stream.shape),
            whole((tokens, half)),
            whole((tokens, half)),
            stepped((tokens, used)),
            stepped((tokens, padded)),
            stepped((tokens, LANES)),
            whole(stream.shape),
        ],
        out_shape=[
            of(stream.shape, f32),
            of((tokens, half), bf16),
            of((tokens, half), bf16),
            of((steps, tokens, used), bf16),
            of((steps, tokens, padded), bf16),
            of((steps, tokens, LANES), f32),
            of(stream.shape, bf16),
        ],
        scratch_shapes=[
            pltpu.VMEM(stream.shape, f32),
        ],
        compiler_params=pltpu.CompilerParams(vmem_limit_bytes=VMEM_BYTES),
        cost_estimate=SMALL_COST,
        name="attention_forward",
    )(stream, modulation, bias, added, *weights)


def mlp_kernel(steps, *refs):
    mid_ref, mod_ref, bias_ref, added_ref = refs[:4]
    hidden, output = (refs[4:6], refs[6:8])
    stream_ref, mine_ref, other_ref, active_ref, slope_ref, out_ref, acc = refs[8:]
    input_refs = (mine_ref, other_ref)
    step = pl.program_id(0)

    @pl.when(step == 0)
    def _():
        normed = norm_parts(mid_ref)
        for half in range(2):
            input_refs[half][...] = (
                normed[half] * (1.0 + mod_ref[half, 4:5, :]) + mod_ref[half, 3:4, :]
            ).astype(jnp.bfloat16)
        acc[...] = jnp.zeros_like(acc)

    pre = dot(input_refs[0][...], hidden[0][0], PLAIN)
    pre = pre + dot(input_refs[1][...], hidden[1][0], PLAIN) + bias_ref[0]
    root = (2.0 / jnp.pi) ** 0.5
    square = pre * pre
    bend = jnp.tanh(pre * (root + root * 0.044715 * square))
    active_ref[0] = (0.5 * pre * (1.0 + bend)).astype(jnp.bfloat16)
    slope_ref[0] = (
        0.5 * (1.0 + bend)
        + 0.5 * pre * (1.0 - bend * bend) * (root + 3.0 * root * 0.044715 * square)
    ).astype(jnp.bfloat16)
    for half in range(2):
        acc[half] += dot(active_ref[0], output[half][0], TURNED)

    @pl.when(step == steps - 1)
    def _():
        for half in range(2):
            total = acc[half] + added_ref[half]
            out_ref[half] = total.astype(jnp.bfloat16)
            stream_ref[half] = mid_ref[half] + mod_ref[half, 5:6, :] * total


def mlp_forward(mid, modulation, hidden, output, bias, added):
    steps = hidden[0].shape[0]
    _, tokens, half = mid.shape
    columns = hidden[0].shape[2]
    bf16, f32 = (jnp.bfloat16, jnp.float32)
    return pl.pallas_call(
        functools.partial(mlp_kernel, steps),
        grid=(steps,),
        in_specs=[
            whole(mid.shape),
            whole(modulation.shape),
            stepped((1, columns)),
            whole(added.shape),
        ]
        + [stepped((half, columns))] * 4,
        out_specs=[
            whole(mid.shape),
            whole((tokens, half)),
            whole((tokens, half)),
            stepped((tokens, columns)),
            stepped((tokens, columns)),
            whole(mid.shape),
        ],
        out_shape=[
            of(mid.shape, f32),
            of((tokens, half), bf16),
            of((tokens, half), bf16),
            of((steps, tokens, columns), bf16),
            of((steps, tokens, columns), bf16),
            of(mid.shape, bf16),
        ],
        scratch_shapes=[
            pltpu.VMEM(mid.shape, f32),
        ],
        compiler_params=pltpu.CompilerParams(vmem_limit_bytes=VMEM_BYTES),
        cost_estimate=SMALL_COST,
        name="mlp_forward",
    )(mid, modulation, bias, added, *hidden, *output)


def mlp_back_kernel(steps, *refs):
    grad_ref, mid_ref, out_ref, slope_ref, mod_ref = refs[:5]
    hidden, output = (refs[5:7], refs[7:9])
    grad_mid_ref, mine_ref, other_ref, grad_pre_ref, small_ref, sum_ref, acc = refs[9:]
    grad_mlp_refs = (mine_ref, other_ref)
    step = pl.program_id(0)

    @pl.when(step == 0)
    def _():
        for half in range(2):
            grad = grad_ref[half]
            scaled = (grad * mod_ref[half, 5:6, :]).astype(jnp.bfloat16)
            grad_mlp_refs[half][...] = scaled
            small_ref[half, 2:3, :] = jnp.sum(
                grad * out_ref[half].astype(jnp.float32), 0, keepdims=True
            )
            small_ref[half, 3:4, :] = jnp.sum(scaled.astype(jnp.float32), 0, keepdims=True)
        acc[...] = jnp.zeros_like(acc)

    grad_act = dot(grad_mlp_refs[0][...], output[0][0], PLAIN)
    grad_act = grad_act + dot(grad_mlp_refs[1][...], output[1][0], PLAIN)
    grad_pre = (grad_act * slope_ref[0].astype(jnp.float32)).astype(jnp.bfloat16)
    grad_pre_ref[0] = grad_pre
    sum_ref[0] = jnp.sum(grad_pre.astype(jnp.float32), 0, keepdims=True)
    for half in range(2):
        acc[half] += dot(grad_pre, hidden[half][0], TURNED)

    @pl.when(step == steps - 1)
    def _():
        norm_grads(mid_ref, acc, mod_ref, 4, grad_ref, grad_mid_ref, small_ref)


def mlp_backward(grad, mid, out, slope, modulation, hidden, output):
    steps = hidden[0].shape[0]
    _, tokens, half = mid.shape
    columns = hidden[0].shape[2]
    bf16, f32 = (jnp.bfloat16, jnp.float32)
    return pl.pallas_call(
        functools.partial(mlp_back_kernel, steps),
        grid=(steps,),
        in_specs=[
            whole(mid.shape),
            whole(mid.shape),
            whole(mid.shape),
            stepped((tokens, columns)),
            whole(modulation.shape),
        ]
        + [stepped((half, columns))] * 4,
        out_specs=[
            whole(mid.shape),
            whole((tokens, half)),
            whole((tokens, half)),
            stepped((tokens, columns)),
            whole((2, 8, half)),
            stepped((1, columns)),
        ],
        out_shape=[
            of(mid.shape, f32),
            of((tokens, half), bf16),
            of((tokens, half), bf16),
            of((steps, tokens, columns), bf16),
            of((2, 8, half), f32),
            of((steps, 1, columns), f32),
        ],
        scratch_shapes=[
            pltpu.VMEM(mid.shape, f32),
        ],
        compiler_params=pltpu.CompilerParams(vmem_limit_bytes=VMEM_BYTES),
        cost_estimate=SMALL_COST,
        name="mlp_backward",
    )(grad, mid, out, slope, modulation, *hidden, *output)


def attention_back_kernel(size, period, steps, *refs):
    grad_ref, stream_ref, out_ref, qkv_ref, log_ref, mod_ref = refs[:6]
    weights = refs[6:8]
    grad_in_ref, mine_ref, other_ref, grad_qkv_ref, small_ref, sum_ref, acc = refs[8:]
    grad_attn_refs = (mine_ref, other_ref)
    step = pl.program_id(0)
    tokens = stream_ref.shape[1]
    used = qkv_ref.shape[2]
    columns = weights[0].shape[2]
    width = columns // 4
    padded = columns - (3 * width) // LANES * LANES
    count = width // HEAD_DIM
    scale = HEAD_DIM ** (-0.5)

    @pl.when(step == 0)
    def _():
        for half in range(2):
            grad = grad_ref[half]
            scaled = (grad * mod_ref[half, 2:3, :]).astype(jnp.bfloat16)
            grad_attn_refs[half][...] = scaled
            small_ref[half, 2:3, :] = jnp.sum(
                grad * out_ref[half].astype(jnp.float32), 0, keepdims=True
            )
            small_ref[half, 3:4, :] = jnp.sum(scaled.astype(jnp.float32), 0, keepdims=True)
        acc[...] = jnp.zeros_like(acc)

    grad_heads = dot(grad_attn_refs[0][...], weights[0][0, :, columns - padded :], PLAIN)
    grad_heads = grad_heads + dot(grad_attn_refs[1][...], weights[1][0, :, columns - padded :], PLAIN)
    grad_heads = grad_heads.astype(jnp.bfloat16)
    total = jnp.zeros((1, used), jnp.float32)
    for group in range(tokens // size):
        rows = slice(group * size, (group + 1) * size)
        block = qkv_ref[0, rows, :]
        logs = log_ref[0, rows, :]
        grad_queries, grad_keys, grad_values = ([], [], [])
        for head in range(count):
            start = head * HEAD_DIM
            query = block[:, start : start + HEAD_DIM]
            key = block[:, width + start : width + start + HEAD_DIM]
            value = block[:, 2 * width + start : 2 * width + start + HEAD_DIM]
            start = padded - width + head * HEAD_DIM
            grad_out = grad_heads[rows, start : start + HEAD_DIM]
            scores = dot(query, key, TURNED) * scale - logs[:, head : head + 1]
            if period:
                scores = jnp.where(same_place(size, period), scores, -1e30)
            probs = jnp.exp(scores)
            grad_probs = dot(grad_out, value, TURNED)
            delta = jnp.sum(probs * grad_probs, 1, keepdims=True)
            grad_scores = (probs * (grad_probs - delta)).astype(jnp.bfloat16)
            grad_values.append(dot(probs.astype(jnp.bfloat16), grad_out, SUMMED))
            grad_queries.append(dot(grad_scores, key, PLAIN) * scale)
            grad_keys.append(dot(grad_scores, query, SUMMED) * scale)
        rest = [jnp.zeros((size, used - 3 * width), jnp.float32)]
        joined = jnp.concatenate(grad_queries + grad_keys + grad_values + rest, 1)
        joined = joined.astype(jnp.bfloat16)
        grad_qkv_ref[0, rows, :] = joined
        total = total + jnp.sum(joined.astype(jnp.float32), 0, keepdims=True)
    sum_ref[0] = total
    for half in range(2):
        acc[half] += dot(grad_qkv_ref[0], weights[half][0, :, :used], TURNED)

    @pl.when(step == steps - 1)
    def _():
        norm_grads(stream_ref, acc, mod_ref, 1, grad_ref, grad_in_ref, small_ref)


def attention_backward(grad, stream, out, qkv, logs, modulation, weights, size, period):
    steps = weights[0].shape[0]
    _, tokens, half = stream.shape
    columns = weights[0].shape[2]
    used = qkv.shape[2]
    bf16, f32 = (jnp.bfloat16, jnp.float32)
    return pl.pallas_call(
        functools.partial(attention_back_kernel, size, period, steps),
        grid=(steps,),
        in_specs=[
            whole(stream.shape),
            whole(stream.shape),
            whole(stream.shape),
            stepped((tokens, used)),
            stepped((tokens, LANES)),
            whole(modulation.shape),
        ]
        + [stepped((half, columns))] * 2,
        out_specs=[
            whole(stream.shape),
            whole((tokens, half)),
            whole((tokens, half)),
            stepped((tokens, used)),
            whole((2, 8, half)),
            stepped((1, used)),
        ],
        out_shape=[
            of(stream.shape, f32),
            of((tokens, half), bf16),
            of((tokens, half), bf16),
            of((steps, tokens, used), bf16),
            of((2, 8, half), f32),
            of((steps, 1, used), f32),
        ],
        scratch_shapes=[
            pltpu.VMEM(stream.shape, f32),
        ],
        compiler_params=pltpu.CompilerParams(vmem_limit_bytes=VMEM_BYTES),
        cost_estimate=SMALL_COST,
        name="attention_backward",
    )(grad, stream, out, qkv, logs, modulation, *weights)


def weight_kernel(pairs, overlap, steps, *refs):
    inputs = refs[: 4 * pairs]
    outs = refs[4 * pairs : 4 * pairs + 5]
    turned = refs[4 * pairs + 5 : 6 * pairs + 5]
    buffer, sems = refs[6 * pairs + 5 :]
    step = pl.program_id(0)
    slot = step % 2
    for pair in range(pairs):
        mine, theirs, _, _ = inputs[4 * pair : 4 * pair + 4]

        @pl.when(step == 0)
        def _():
            turned[2 * pair][...] = mine[...].T
            turned[2 * pair + 1][...] = theirs[...].T

    @pl.when(step >= 2)
    def _():
        pltpu.make_async_copy(buffer.at[slot], outs[0], sems.at[slot]).wait()

    sums = []
    for pair in range(pairs):
        _, _, mine, theirs = inputs[4 * pair : 4 * pair + 4]
        total = dot(turned[2 * pair][...], mine[0], PLAIN)
        sums.append(total + dot(turned[2 * pair + 1][...], theirs[0], PLAIN))
    if pairs == 1:
        buffer[slot] = sums[0].astype(jnp.bfloat16)
    else:
        first = sums[0].shape[1] - overlap
        buffer[slot, :, :first] = sums[0][:, :first].astype(jnp.bfloat16)
        buffer[slot, :, first : first + overlap] = (
            sums[0][:, first:] + sums[1][:, :overlap]
        ).astype(jnp.bfloat16)
        buffer[slot, :, first + overlap :] = sums[1][:, overlap:].astype(jnp.bfloat16)
    for index in range(steps):

        @pl.when(step == index)
        def _():
            source = buffer.at[index % 2]
            sem = sems.at[index % 2]
            if index == 0:
                pltpu.make_async_copy(source, outs[0], sem).start()
            else:
                rows = outs[1].shape[0]
                upper, lower = (
                    (outs[1], outs[2].at[:rows]),
                    (outs[3].at[:rows], outs[4]),
                    (outs[3].at[rows:], outs[2].at[rows:]),
                )[index - 1]
                pltpu.make_async_copy(source.at[:rows], upper, sem).start()
                pltpu.make_async_copy(source.at[rows:], lower, sem).start()

    @pl.when(step == steps - 1)
    def _():
        for index in range(2):
            pltpu.make_async_copy(buffer.at[index], outs[0], sems.at[index]).wait()


def weight_grads(columns, overlap, *pairs, flops=0):
    steps, tokens, _ = pairs[0][2].shape
    half = pairs[0][1].shape[1]
    bf16 = jnp.bfloat16
    specs, values, turned = ([], [], [])
    for mine, theirs, blocks, their_blocks in pairs:
        specs += [
            whole(mine.shape),
            whole(theirs.shape),
            stepped(blocks.shape[1:]),
            stepped(blocks.shape[1:]),
        ]
        values += [mine, theirs, blocks, their_blocks]
        turned += [pltpu.VMEM((half, tokens), bf16)] * 2
    return pl.pallas_call(
        functools.partial(weight_kernel, len(pairs), overlap, steps),
        grid=(steps,),
        in_specs=specs,
        out_specs=[IN_HBM] * 5,
        out_shape=[
            of((rows, columns), bf16) for rows in (half, half // 2, half, half, half // 2)
        ],
        scratch_shapes=turned
        + [pltpu.VMEM((2, half, columns), bf16), pltpu.SemaphoreType.DMA((2,))],
        compiler_params=pltpu.CompilerParams(vmem_limit_bytes=VMEM_BYTES),
        cost_estimate=pl.CostEstimate(flops=flops, bytes_accessed=0, transcendentals=0),
        name="weight_grads",
    )(*values)


def pack_kernel(held, across, above, lower, upper, out, buffer, sems):
    size = held.shape[0]
    half = size // 2
    corner = pl.ds(lower.shape[0] - half, half)
    incoming = [
        pltpu.make_async_copy(source, target, sems.at[index])
        for index, (source, target) in enumerate(
            (
                (held, buffer.at[0]),
                (across.at[:size], buffer.at[1]),
                (above.at[:size], buffer.at[2]),
                (upper.at[corner], buffer.at[3, :half]),
                (lower.at[corner], buffer.at[3, half:]),
            )
        )
    ]
    outgoing = [
        pltpu.make_async_copy(buffer.at[index], out.at[index], sems.at[5 + index])
        for index in range(4)
    ]
    for copy in incoming:
        copy.start()
    for index in range(3):
        incoming[index].wait()
        outgoing[index].start()
    incoming[3].wait()
    incoming[4].wait()
    outgoing[3].start()
    for copy in outgoing:
        copy.wait()


def pack_blocks(blocks):
    shape = (4,) + blocks[0].shape
    return pl.pallas_call(
        pack_kernel,
        in_specs=[IN_HBM] * 5,
        out_specs=IN_HBM,
        out_shape=of(shape, jnp.bfloat16),
        scratch_shapes=[pltpu.VMEM(shape, jnp.bfloat16), pltpu.SemaphoreType.DMA((9,))],
        compiler_params=pltpu.CompilerParams(vmem_limit_bytes=VMEM_BYTES // 4),
        cost_estimate=SMALL_COST,
        name="pack_blocks",
    )(*blocks)


def placing_matrix(core, part, block, half, shape):
    feature = lax.broadcasted_iota(jnp.int32, shape, 0) + block * shape[0]
    target = lax.broadcasted_iota(jnp.int32, shape, 1)
    row = feature // part
    match = (row & 1) == (core ^ half)
    match &= (row // 2) * part + (feature - row * part) == target
    return jnp.where(match, 1.0, 0.0).astype(jnp.bfloat16)


def enter_kernel(part, where_ref, *refs):
    *blocks, out_ref = refs
    shape = (blocks[0].shape[1], out_ref.shape[2])
    for half in range(2):
        total = None
        for step, block in enumerate(blocks):
            matrix = placing_matrix(where_ref[0], part, where_ref[1] ^ step, half, shape)
            term = dot(block[...], matrix, PLAIN)
            total = term if total is None else total + term
        out_ref[half] = total


def leave_kernel(part, where_ref, halves_ref, *outs):
    shape = (outs[0].shape[1], halves_ref.shape[2])
    halves = [halves_ref[half].astype(jnp.bfloat16) for half in range(2)]
    for step, out in enumerate(outs):
        total = None
        for half in range(2):
            matrix = placing_matrix(where_ref[0], part, where_ref[1] ^ step, half, shape)
            term = dot(halves[half], matrix, TURNED)
            total = term if total is None else total + term
        out[...] = total.astype(jnp.bfloat16)


def assemble_kernel(where_ref, *refs):
    *blocks, out_ref = refs
    for step, block in enumerate(blocks):
        out_ref[where_ref[1] ^ step] = block[...].astype(out_ref.dtype)


def reorder(kernel, values, outs, place):
    in_vmem = pl.BlockSpec(memory_space=pltpu.VMEM)
    where = jnp.stack((place.core, place.col)).astype(jnp.int32)
    return pl.pallas_call(
        kernel,
        in_specs=[pl.BlockSpec(memory_space=pltpu.SMEM)] + [in_vmem] * len(values),
        out_specs=[in_vmem] * len(outs),
        out_shape=outs,
        compiler_params=pltpu.CompilerParams(vmem_limit_bytes=VMEM_BYTES // 2),
        cost_estimate=SMALL_COST,
        name="reorder",
    )(where, *values)


def add_kernel(held, across_upper, across_first, above_first, above_lower, out):
    rows = across_upper.shape[0]
    for start, pair in ((0, (across_upper, above_first)), (rows, (across_first, above_lower))):
        total = held[start : start + rows].astype(jnp.float32)
        for value in pair:
            total += value[:rows].astype(jnp.float32)
        out[start : start + rows] = total.astype(jnp.bfloat16)


def add_blocks(blocks):
    in_vmem = pl.BlockSpec(memory_space=pltpu.VMEM)
    return pl.pallas_call(
        add_kernel,
        in_specs=[in_vmem] * 5,
        out_specs=in_vmem,
        out_shape=of(blocks[0].shape, jnp.bfloat16),
        compiler_params=pltpu.CompilerParams(vmem_limit_bytes=VMEM_BYTES // 2),
        cost_estimate=SMALL_COST,
        name="add_blocks",
    )(*blocks)


def token_parallel(
    tokens,
    conditioning,
    ada_weight,
    ada_bias,
    qkv_weight,
    attn_bias,
    mixing_weight,
    mixing_bias,
    hidden_weight,
    hidden_bias,
    output_weight,
    output_bias,
    cotangent,
):
    place = Place()
    col_width = ada_bias.shape[2]
    row_width = conditioning.shape[1]
    hidden_width = hidden_bias.shape[1]
    layer_count = ada_bias.shape[0]
    clip_count = conditioning.shape[0]
    width = col_width * place.col_count

    copies = (place.row_count // 2, 1)

    def attn_shards(*gate):
        first, second = together(qkv_weight, mixing_weight, *gate)[:2]
        return [
            jnp.tile(
                jnp.concatenate(
                    (
                        first[depth].reshape(row_width, 3 * col_width),
                        second[depth].reshape(col_width, row_width).T,
                    ),
                    1,
                ),
                copies,
            )
            for depth in range(layer_count)
        ]

    def hidden_shards(*gate):
        value = after(hidden_weight, *gate)
        return [
            jnp.tile(value[depth].reshape(row_width, hidden_width), copies)
            for depth in range(layer_count)
        ]

    def output_shards(*gate):
        value = after(output_weight, *gate)
        return [
            jnp.tile(value[depth].reshape(hidden_width, row_width).T, copies)
            for depth in range(layer_count)
        ]

    def arriving(held):
        return trade(relative(held.reshape(clip_count, -1, col_width), place))

    def entered(blocks):
        outs = [of((2, blocks[0].shape[0], width // 2), jnp.float32)]
        return reorder(functools.partial(enter_kernel, row_width), blocks, outs, place)[0]

    gathering = Gathering(place)
    attn_ready = attn_shards()
    tokens = after(open_tokens(tokens, col_width), attn_ready[0])
    cotangent = open_tokens(cotangent, col_width)
    gathering.step(attn_ready[0])
    token_blocks = arriving(tokens)
    hidden_ready = hidden_shards(attn_ready[0])
    hidden_ready, attn_ready, token_blocks = together(hidden_ready, attn_ready, token_blocks)
    gathering.step(hidden_ready[0], *token_blocks)
    conditioning, ada_weight, attn_bias, token_blocks, output_gate = after(
        (conditioning, ada_weight, attn_bias, token_blocks, output_weight), *gathering.sent
    )
    output_weight = output_gate
    output_ready = output_shards()
    stream_first = entered(token_blocks)
    ada_weight = ada_weight.reshape(layer_count, row_width, 6, col_width)
    frame_part, places = tokens.shape[1:3]
    frames, place_part = cotangent.shape[1:3]
    period = 16 if place_part % 16 == 0 else place_part
    groups = place_part // period
    first_size = places
    second_size = frames * period

    half = width // 2

    def leaving(halves):
        outs = [of((halves.shape[1], col_width), jnp.bfloat16)] * place.col_count
        return reorder(functools.partial(leave_kernel, row_width), [halves], outs, place)

    def assembled(blocks, dtype):
        outs = [of((len(blocks),) + blocks[0].shape, dtype)]
        return reorder(assemble_kernel, blocks, outs, place)[0]

    cond_act = jax.nn.silu(conditioning).astype(jnp.bfloat16)
    modulation = matmul("cr,lrsk->clsk", cond_act, ada_weight)
    modulation = modulation.reshape(clip_count, -1)
    cut = modulation.shape[1]
    own = [modulation] + [
        value.reshape(clip_count, -1)
        for value in (attn_bias, hidden_bias, mixing_bias, output_bias, ada_bias)
    ]
    met = lax.all_gather(jnp.concatenate(own, 1), ("row", "col"), axis=0)
    met = met.reshape(place.row_count, place.col_count, clip_count, -1)
    modulation = lax.dynamic_index_in_dim(met, place.col, 2, keepdims=False)[:, :, :cut]
    modulation = jnp.sum(modulation, 0).reshape(-1, layer_count, 6, col_width)
    rest = met[0, :, :, cut:]
    vectors = []
    for value in (attn_bias, hidden_bias, mixing_bias, output_bias, ada_bias):
        size = value.size // clip_count
        vectors.append(rest[:, :, :size].reshape((place.col_count,) + value.shape))
        rest = rest[:, :, size:]
    modulation = modulation + vectors.pop()
    modulation = jnp.moveaxis(modulation, 0, 2).reshape(layer_count, 6, width)
    modulation = jnp.swapaxes(to_halves(modulation, place), 1, 2)
    attn_add, hidden_add, mixing_add, output_add = vectors
    attn_add, hidden_add = (relative(value, place) for value in (attn_add, hidden_add))

    def whole_vector(blocks):
        joined = jnp.moveaxis(blocks, 0, 1).reshape(layer_count, width)
        return to_halves(joined, place)

    mixing_add = whole_vector(mixing_add)
    output_add = whole_vector(output_add)

    blank = jnp.zeros((round_up(3 * col_width) - 3 * col_width,), jnp.float32)

    def biases_of(depth):
        attn_rows = [
            jnp.concatenate((block[depth, 0], jnp.zeros_like(block[depth, 0]), block[depth, 1], blank))
            for block in attn_add
        ]
        return (
            jnp.stack(attn_rows)[:, None, :],
            mixing_add[depth][:, None, :],
            jnp.stack([block[depth] for block in hidden_add])[:, None, :],
            output_add[depth][:, None, :],
        )

    attn_biases, mixing_biases, hidden_biases, output_biases = zip(biases_of(0), biases_of(1))
    sizes = (first_size, second_size)
    periods = (0, period)

    def attn_part(depth, stream):
        return attention_forward(
            stream,
            modulation[depth],
            gathering.done[3 * depth],
            attn_biases[depth],
            mixing_biases[depth],
            sizes[depth],
            periods[depth],
        )

    def mlp_part(depth, mid):
        return mlp_forward(
            mid,
            modulation[depth],
            gathering.done[3 * depth + 1],
            gathering.done[3 * depth + 2],
            hidden_biases[depth],
            output_biases[depth],
        )

    def mlp_grads(depth, grad, saved):
        _, mid, _, (_, _, _, slope, mlp_out) = saved
        return mlp_backward(
            grad, mid, mlp_out, slope, modulation[depth], *gathering.done[3 * depth + 1 : 3 * depth + 3]
        )

    def attn_grads(depth, grad_mid, saved):
        stream, _, (_, _, qkv, _, logs, attn_out), _ = saved
        return attention_backward(
            grad_mid,
            stream,
            attn_out,
            qkv,
            logs,
            modulation[depth],
            gathering.done[3 * depth],
            sizes[depth],
            periods[depth],
        )

    def attn_terms(saved, swapped, grad_attn, grad_qkv, received, flops=0):
        input_attn, _, _, heads, _, _ = saved[2]
        columns = 4 * col_width
        return weight_grads(
            columns,
            grad_qkv.shape[2] + heads.shape[2] - columns,
            (input_attn, swapped[0], grad_qkv, received[0]),
            (grad_attn, received[1], heads, swapped[1]),
            flops=flops,
        )

    def output_terms(saved, swapped, grad_mlp, received):
        active = saved[3][2]
        return weight_grads(active.shape[2], 0, (grad_mlp, received, active, swapped[3]))

    def hidden_terms(saved, swapped, grad_pre, received):
        return weight_grads(
            grad_pre.shape[2], 0, (saved[3][0], swapped[2], grad_pre, received)
        )

    gathering.step(output_ready[0], stream_first, *output_ready)
    gathering.step(attn_ready[1], modulation)
    mid_first, *attn_first = attn_part(0, after(stream_first, *gathering.sent))
    gathering.step(hidden_ready[1], mid_first)
    gathering.step(output_ready[1])
    input_attn, heads = after((attn_first[1], attn_first[3]), *gathering.sent)
    swapped_first = [swap(input_attn), swap(heads)]
    output_first, *mlp_first = mlp_part(0, after(mid_first, *gathering.sent))
    saved_first = (stream_first, mid_first, attn_first, mlp_first)
    gathering.step(None, output_first, *swapped_first)
    input_mlp, active, moving = after(
        (mlp_first[1], mlp_first[2], output_first), *gathering.sent
    )
    swapped_first += [swap(input_mlp), swap(active)]
    moving = mine_first(moving.astype(jnp.bfloat16), place, 0)
    moving = moving.reshape(2, frame_part, place.row_count, groups, period, half)
    moving = moving.transpose(0, 2, 3, 1, 4, 5)
    moved = lax.all_to_all(moving, "row", split_axis=1, concat_axis=3, tiled=True)
    gathering.step(None, moved, *swapped_first[2:])
    cotangent, moved = after((cotangent, moved), *gathering.sent)
    cotangent = cotangent.reshape(clip_count, frames, groups, period, col_width)
    gradient_blocks = arriving(jnp.swapaxes(cotangent, 1, 2))
    moved = moved.reshape(2, -1, half)
    stream_second = mine_first(moved, place, 0).astype(jnp.float32)
    mid_second, *attn_second = attn_part(1, stream_second)
    gathering.step(None, mid_second)
    gradient_blocks, mid_second, input_attn, heads = together(
        gradient_blocks, mid_second, attn_second[1], attn_second[3]
    )
    swapped_second = [swap(input_attn), swap(heads)]
    output_second, *mlp_second = mlp_part(1, mid_second)
    saved_second = (stream_second, mid_second, attn_second, mlp_second)
    grad = entered(gradient_blocks)
    grad, swapped_second, input_mlp, active, output_second = together(
        grad, swapped_second, mlp_second[1], mlp_second[2], output_second
    )
    swapped_second += [swap(input_mlp), swap(active)]

    grad_mid, grad_mlp, grad_sent, grad_pre, small_mlp_second, hidden_sum_second = mlp_grads(
        1, grad, saved_second
    )
    grad_mid, grad_mlp, grad_sent, grad_pre, swapped_second, output_second = together(
        grad_mid, grad_mlp, grad_sent, grad_pre, swapped_second, output_second
    )
    received = swap(grad_sent)
    result_blocks = leaving(output_second)
    received, result_blocks, grad_pre = together(received, result_blocks, grad_pre)
    received_pre = swap(grad_pre)
    output_part = output_terms(saved_second, swapped_second, grad_mlp, received)
    output_part, received_pre, grad_mid = together(output_part, received_pre, grad_mid)
    output_part = scatter_corner(output_part)
    hidden_part = hidden_terms(saved_second, swapped_second, grad_pre, received_pre)
    hidden_part, grad_mid = together(hidden_part, grad_mid)
    hidden_part = scatter_corner(hidden_part)
    grad_second, grad_attn, grad_sent, grad_qkv, small_attn_second, qkv_sum_second = attn_grads(
        1, grad_mid, saved_second
    )
    grad_second, grad_attn, grad_sent, grad_qkv, output_part = together(
        grad_second, grad_attn, grad_sent, grad_qkv, output_part
    )
    received = [swap(grad_qkv), swap(grad_sent)]
    sides = scatter_sides(output_part)
    moving = mine_first(grad_second.astype(jnp.bfloat16), place, 0)
    moving = moving.reshape(2, 1, groups, frames, period, half)
    moved = lax.all_to_all(moving, "row", split_axis=3, concat_axis=1, tiled=True)
    received, grad_attn, grad_qkv, sides, moving = together(
        received, grad_attn, grad_qkv, sides, moving
    )
    output_part = scatter_plane(output_part, sides)
    attn_blocks = attn_terms(
        saved_second, swapped_second, grad_attn, grad_qkv, received, 15 * 10**9
    )
    attn_blocks, hidden_part = together(attn_blocks, hidden_part)
    attn_part_second = scatter_corner(attn_blocks)
    sides = scatter_sides(hidden_part)
    output_total = add_blocks(output_part)
    moved, output_total, sides = together(moved, output_total, sides)
    moved = moved.transpose(0, 3, 1, 2, 4, 5).reshape(2, -1, half)
    returned = mine_first(moved, place, 0).astype(jnp.float32)
    output_pieces = over_depth(output_total, place)
    hidden_part = scatter_plane(hidden_part, sides)
    grad_mid, grad_mlp, grad_sent, grad_pre, small_mlp_first, hidden_sum_first = mlp_grads(
        0, returned, saved_first
    )
    grad_mid, grad_mlp, grad_sent, grad_pre, output_pieces, hidden_part = together(
        grad_mid, grad_mlp, grad_sent, grad_pre, output_pieces, hidden_part
    )
    received = swap(grad_sent)
    hidden_total = add_blocks(hidden_part)
    received, hidden_total, grad_pre = together(received, hidden_total, grad_pre)
    hidden_pieces = over_depth(hidden_total, place)
    received_pre = swap(grad_pre)
    output_blocks = output_terms(saved_first, swapped_first, grad_mlp, received)
    output_blocks, received_pre, attn_part_second = together(
        output_blocks, received_pre, attn_part_second
    )
    output_part = scatter_corner(output_blocks)
    sides = scatter_sides(attn_part_second)
    attn_part_second = scatter_plane(attn_part_second, sides)
    received_pre, _ = together(received_pre, sides)
    hidden_blocks = hidden_terms(saved_first, swapped_first, grad_pre, received_pre)
    hidden_blocks, grad_mid = together(hidden_blocks, grad_mid)
    hidden_part = scatter_corner(hidden_blocks)
    grad_first, grad_attn, grad_sent, grad_qkv, small_attn_first, qkv_sum_first = attn_grads(
        0, grad_mid, saved_first
    )
    (
        grad_first,
        grad_attn,
        grad_sent,
        grad_qkv,
        output_part,
        attn_part_second,
        hidden_pieces,
    ) = together(
        grad_first, grad_attn, grad_sent, grad_qkv, output_part, attn_part_second, hidden_pieces
    )
    received = [swap(grad_qkv), swap(grad_sent)]
    sides = scatter_sides(output_part)
    output_part = scatter_plane(output_part, sides)
    attn_total = add_blocks(attn_part_second)
    attn_pieces = over_depth(attn_total, place)
    received, _, grad_attn, grad_qkv = together(
        received, (sides, attn_total), grad_attn, grad_qkv
    )
    attn_blocks = attn_terms(saved_first, swapped_first, grad_attn, grad_qkv, received)
    attn_blocks, output_part, hidden_part, small_mlp_first, grad_first = together(
        attn_blocks, output_part, hidden_part, small_mlp_first, grad_first
    )
    attn_part_first = scatter_corner(attn_blocks)
    sides = scatter_sides(hidden_part)
    output_total = add_blocks(output_part)
    output_total, sides, grad_first, small_attn_first, attn_pieces = together(
        output_total, sides, grad_first, small_attn_first, attn_pieces
    )
    hidden_part = scatter_plane(hidden_part, sides)
    output_first_pieces = over_depth(output_total, place)
    gradient_blocks = leaving(grad_first)

    def small_grads(small_attn, small_mlp, qkv_sum, hidden_sum):
        return (
            jnp.concatenate((small_attn[:, :3], small_mlp[:, :3]), 1),
            (qkv_sum[:, 0], small_attn[:, 3], hidden_sum[:, 0], small_mlp[:, 3]),
        )

    modgrad_first, biasgrad_first = small_grads(
        small_attn_first, small_mlp_first, qkv_sum_first, hidden_sum_first
    )
    modgrad_second, biasgrad_second = small_grads(
        small_attn_second, small_mlp_second, qkv_sum_second, hidden_sum_second
    )
    def by_block(halves):
        features = from_halves(halves, place)
        features = features.reshape(features.shape[:-1] + (place.col_count, col_width))
        return relative(jnp.moveaxis(features, -2, 0), place)

    modgrad = by_block(jnp.swapaxes(jnp.stack((modgrad_first, modgrad_second)), 1, 2))
    mixgrad = by_block(jnp.stack((biasgrad_first[1], biasgrad_second[1])))
    outgrad = by_block(jnp.stack((biasgrad_first[3], biasgrad_second[3])))
    sending = []
    for step in range(place.col_count):
        pieces = [modgrad[step].reshape(-1)]
        for grads in (biasgrad_first, biasgrad_second):
            pieces.append(grads[0][step][:col_width])
            pieces.append(grads[0][step][2 * col_width : 3 * col_width])
        for grads in (biasgrad_first, biasgrad_second):
            pieces.append(grads[2][step])
        pieces.append(mixgrad[step].reshape(-1))
        pieces.append(outgrad[step].reshape(-1))
        sending.append(jnp.concatenate(pieces))
    sending = [value.reshape(-1, LANES) for value in sending]
    attn_part_first, hidden_part, gradient_blocks, sending = together(
        attn_part_first, hidden_part, gradient_blocks, sending
    )
    sides = scatter_sides(attn_part_first)
    hidden_total = add_blocks(hidden_part)
    sides, hidden_total, sending, output_first_pieces = together(
        sides, hidden_total, sending, output_first_pieces
    )
    attn_part_first = scatter_plane(attn_part_first, sides)
    hidden_first_pieces = over_depth(hidden_total, place)
    met = trade(sending)
    sums = [add_all(pieces, place) for pieces in (attn_pieces, hidden_pieces, output_pieces)]
    met, attn_part_first, sums, output_first_pieces = together(
        met, attn_part_first, sums, output_first_pieces
    )
    attn_total = add_blocks(attn_part_first)
    met = [value.reshape(-1) for value in met]
    modgrad = jnp.concatenate([block[:cut] for block in met])
    biasgrad = sum(block[cut:] for block in met)
    small = jnp.concatenate((modgrad, biasgrad))
    small = small + swap(small)
    gradient_blocks, result_blocks, small, _ = together(
        gradient_blocks, result_blocks, small, attn_total
    )
    gradient_blocks = trade(gradient_blocks)
    for mask in place.depth_masks:
        small = small + exchange(small, "row", mask)
    gradient_blocks, hidden_first_pieces, attn_total, small = together(
        gradient_blocks, hidden_first_pieces, attn_total, small
    )
    attn_first_pieces = over_depth(attn_total, place)
    tokens_gradient = assembled(gradient_blocks, jnp.float32)
    tokens_gradient = tokens_gradient.reshape(clip_count, frame_part, places, col_width)
    result = assembled(trade(result_blocks), jnp.bfloat16)
    result = result.reshape(clip_count, groups, frames, period, col_width)
    result = jnp.swapaxes(result, 1, 2).reshape(clip_count, frames, place_part, col_width)
    first_sums = [
        add_all(pieces, place)
        for pieces in (attn_first_pieces, hidden_first_pieces, output_first_pieces)
    ]
    modgrad = small[: cut * clip_count].reshape(clip_count, layer_count, 6, col_width)
    modgrad = jnp.moveaxis(jnp.stack(relative(modgrad, place)), 1, 0)
    rest = small[cut * clip_count :]
    bias_grads = []
    for value in (attn_bias, hidden_bias, mixing_bias, output_bias):
        bias_grads.append(rest[: value.size].reshape(value.shape))
        rest = rest[value.size :]
    ada_bias_grad = jnp.sum(modgrad, 1)
    ada_weight_grad = jnp.einsum(
        "cr,lcsk->lrsk", cond_act.astype(jnp.float32), modgrad, precision=highest
    )
    cond_part = jnp.einsum(
        "lcsk,lrsk->cr", modgrad, ada_weight.astype(jnp.float32), precision=highest
    )
    for mask in (1, 2):
        cond_part = cond_part + exchange(cond_part, "col", mask)
    conditioning_gradient = jax.vjp(jax.nn.silu, conditioning)[1](cond_part)[0]

    attn_sums, hidden_sums, output_sums = (
        jnp.stack((first_sums[index], sums[index])) for index in range(3)
    )
    return (
        close_tokens(result),
        close_tokens(tokens_gradient),
        conditioning_gradient,
        close_weight(ada_weight_grad),
        ada_bias_grad,
        close_weight(attn_sums[:, :, : 3 * col_width]),
        bias_grads[0],
        close_weight(jnp.swapaxes(attn_sums[:, :, 3 * col_width :], 1, 2)),
        bias_grads[2],
        close_weight(hidden_sums),
        bias_grads[1],
        close_weight(jnp.swapaxes(output_sums, 1, 2)),
        bias_grads[3],
    )


def suits_tokens(mesh):
    rows, cols = (mesh.shape["row"], mesh.shape["col"])
    return cols == 4 and rows >= 2 and rows & (rows - 1) == 0


def solution(mesh):
    placed = (
        P(None, "row", "col", None),
        P(None, "row"),
        P(None, "row", "col", None),
        P(None, None, "col"),
        P(None, "row", "col", None),
        P(None, None, "col"),
        P(None, "col", "row", None),
        P(None, "col"),
        P(None, "row", "col", None),
        P(None, "col"),
        P(None, "col", "row", None),
        P(None, "col"),
        P(None, None, "col", "row"),
    )
    return jax.shard_map(
        token_parallel if suits_tokens(mesh) else tensor_parallel,
        mesh=mesh,
        in_specs=placed,
        out_specs=(
            P(None, None, "col", "row"),
            P(None, "row", "col", None),
            P(None, "row"),
            P(None, "row", "col", None),
            P(None, None, "col"),
            P(None, "row", "col", None),
            P(None, None, "col"),
            P(None, "col", "row", None),
            P(None, "col"),
            P(None, "row", "col", None),
            P(None, "col"),
            P(None, "col", "row", None),
            P(None, "col"),
        ),
        check_vma=False,
    )
```

```python
import functools

import jax
import jax.numpy as jnp
from jax import lax
from jax.experimental import pallas as pl
from jax.experimental.pallas import tpu as pltpu
from jax.sharding import PartitionSpec as P

HEAD_DIM = 72


epsilon = 1e-06
highest = lax.Precision.HIGHEST
spatial_forms = ("caqhe,cakhe->cahqk", "cahqk,cakhe->caqhe", "cahqk,caqhe->cakhe")
temporal_forms = ("cqbhe,ckbhe->cbhqk", "cbhqk,ckbhe->cqbhe", "cbhqk,cqbhe->ckbhe")


def matmul(pattern, left, right):
    return jnp.einsum(pattern, left, right, preferred_element_type=jnp.float32)


def split_heads(values):
    return values.reshape(values.shape[:-1] + (values.shape[-1] // HEAD_DIM, HEAD_DIM))


def merge_heads(values):
    return values.reshape(values.shape[:-2] + (values.shape[-2] * values.shape[-1],))


def gelu_tanh(values):
    return jax.nn.gelu(values, approximate=True)


def open_tokens(blocked, width):
    return blocked.reshape(blocked.shape[0], blocked.shape[1], blocked.shape[3] // width, width)


def close_tokens(plain_layout):
    return plain_layout.reshape(
        plain_layout.shape[0],
        plain_layout.shape[1],
        1,
        plain_layout.shape[2] * plain_layout.shape[3],
    )


def close_weight(plain_layout):
    return plain_layout.reshape(plain_layout.shape[0], 1, 1, -1)


def normalize(stream):
    feature_count = stream.shape[-1] * lax.axis_size("col")
    row_total, squares = lax.psum((jnp.sum(stream, -1), jnp.sum(stream * stream, -1)), "col")
    average = row_total / feature_count
    variance = squares / feature_count - average * average
    inverse = lax.rsqrt(variance + epsilon)
    return ((stream - average[..., None]) * inverse[..., None], inverse)


def normalize_back(grad_normed, normed, inverse):
    feature_count = grad_normed.shape[-1] * lax.axis_size("col")
    first, second = lax.psum((jnp.sum(grad_normed, -1), jnp.sum(grad_normed * normed, -1)), "col")
    return inverse[..., None] * (
        grad_normed - first[..., None] / feature_count - normed * second[..., None] / feature_count
    )


def spread(values):
    return lax.all_gather(values, "col", axis=3, tiled=True)


def collect(terms):
    return lax.psum_scatter(
        terms.astype(jnp.bfloat16), "col", scatter_dimension=3, tiled=True
    ).astype(jnp.float32)


def spread_grad(values):
    return lax.all_gather(values, "col", axis=3, tiled=True)


def collect_grad(terms):
    return lax.psum_scatter(
        terms.astype(jnp.bfloat16), "col", scatter_dimension=3, tiled=True
    ).astype(jnp.float32)


def fetch_weights(qkv_weight, mixing_weight, hidden_weight, output_weight, depth):
    return (
        lax.all_gather(qkv_weight[depth], "row", axis=0, tiled=True),
        lax.all_gather(mixing_weight[depth], "row", axis=1, tiled=True),
        lax.all_gather(hidden_weight[depth], "row", axis=0, tiled=True),
        lax.all_gather(output_weight[depth], "row", axis=1, tiled=True),
    )


def attend(queries, key_rows, value_rows, forms):
    softmax_scale = HEAD_DIM ** (-0.5)
    scores = matmul(forms[0], split_heads(queries), split_heads(key_rows)) * softmax_scale
    largest = jnp.max(scores, -1, keepdims=True)
    weights = jnp.exp(scores - largest)
    totals = jnp.sum(weights, -1, keepdims=True)
    probs = (weights / totals).astype(jnp.bfloat16)
    mixed = matmul(forms[1], probs, split_heads(value_rows))
    return (merge_heads(mixed).astype(jnp.bfloat16), largest + jnp.log(totals))


def attend_back(queries, key_rows, value_rows, grad_heads, log_totals, forms):
    softmax_scale = HEAD_DIM ** (-0.5)
    query_split = split_heads(queries)
    key_split = split_heads(key_rows)
    value_split = split_heads(value_rows)
    grad_split = split_heads(grad_heads)
    scores = matmul(forms[0], query_split, key_split) * softmax_scale
    probs = jnp.exp(scores - log_totals)
    grad_values = matmul(forms[2], probs.astype(jnp.bfloat16), grad_split)
    grad_probs = matmul(forms[0], grad_split, value_split)
    row_delta = jnp.sum(probs * grad_probs, -1, keepdims=True)
    grad_scores = (probs * (grad_probs - row_delta)).astype(jnp.bfloat16)
    grad_queries = matmul(forms[1], grad_scores, key_split) * softmax_scale
    grad_keys = matmul(forms[2], grad_scores, query_split) * softmax_scale
    return tuple(
        (
            merge_heads(part_grad).astype(jnp.bfloat16)
            for part_grad in (grad_queries, grad_keys, grad_values)
        )
    )


def residual_forward(stream, modulation, weights, biases, forms):
    qkv_full, mixing_full, hidden_full, output_full = weights
    attn_add, mixing_add, hidden_add, output_add = biases

    def piece_of(column):
        return modulation[:, column][:, None, None, :]

    normed_attn, inv_attn = normalize(stream)
    input_attn = spread((normed_attn * (1.0 + piece_of(1)) + piece_of(0)).astype(jnp.bfloat16))
    qkv_rows = matmul("cabd,dsk->cabsk", input_attn, qkv_full)
    queries = (qkv_rows[..., 0, :] + attn_add[0]).astype(jnp.bfloat16)
    key_rows = qkv_rows[..., 1, :].astype(jnp.bfloat16)
    value_rows = (qkv_rows[..., 2, :] + attn_add[1]).astype(jnp.bfloat16)
    heads_out, log_totals = attend(queries, key_rows, value_rows, forms)
    attn_out = collect(matmul("cabk,kd->cabd", heads_out, mixing_full)) + mixing_add
    stream_mid = stream + piece_of(2) * attn_out
    normed_mlp, inv_mlp = normalize(stream_mid)
    input_mlp = spread((normed_mlp * (1.0 + piece_of(4)) + piece_of(3)).astype(jnp.bfloat16))
    pre_gelu = matmul("cabd,df->cabf", input_mlp, hidden_full) + hidden_add
    activated = gelu_tanh(pre_gelu).astype(jnp.bfloat16)
    mlp_out = collect(matmul("cabf,fd->cabd", activated, output_full)) + output_add
    stream_out = stream_mid + piece_of(5) * mlp_out
    saved = (
        normed_attn,
        inv_attn,
        input_attn,
        queries,
        key_rows,
        value_rows,
        heads_out,
        log_totals,
        attn_out,
        normed_mlp,
        inv_mlp,
        input_mlp,
        pre_gelu,
        activated,
        mlp_out,
    )
    return (stream_out, saved)


def residual_backward(grad_stream, saved, modulation, weights, forms):
    (
        normed_attn,
        inv_attn,
        input_attn,
        queries,
        key_rows,
        value_rows,
        heads_out,
        log_totals,
        attn_out,
        normed_mlp,
        inv_mlp,
        input_mlp,
        pre_gelu,
        activated,
        mlp_out,
    ) = saved
    qkv_full, mixing_full, hidden_full, output_full = weights

    def piece_of(column):
        return modulation[:, column][:, None, None, :]

    grad_mlp = (grad_stream * piece_of(5)).astype(jnp.bfloat16)
    gate_mlp_grad = jnp.sum(grad_stream * mlp_out, (1, 2))
    grad_mlp_all = spread_grad(grad_mlp)
    output_weight_term = matmul("cabf,cabd->fd", activated, grad_mlp_all)
    grad_act = matmul("cabd,fd->cabf", grad_mlp_all, output_full)
    grad_pre = jax.vjp(gelu_tanh, pre_gelu)[1](grad_act)[0].astype(jnp.bfloat16)
    hidden_weight_term = matmul("cabd,cabf->df", input_mlp, grad_pre)
    grad_input_mlp = collect_grad(matmul("cabf,df->cabd", grad_pre, hidden_full))
    shift_mlp_grad = jnp.sum(grad_input_mlp, (1, 2))
    scale_mlp_grad = jnp.sum(grad_input_mlp * normed_mlp, (1, 2))
    grad_mid = grad_stream + normalize_back(
        grad_input_mlp * (1.0 + piece_of(4)), normed_mlp, inv_mlp
    )
    grad_attn = (grad_mid * piece_of(2)).astype(jnp.bfloat16)
    gate_attn_grad = jnp.sum(grad_mid * attn_out, (1, 2))
    grad_attn_all = spread_grad(grad_attn)
    mixing_weight_term = matmul("cabk,cabd->kd", heads_out, grad_attn_all)
    grad_heads = matmul("cabd,kd->cabk", grad_attn_all, mixing_full).astype(jnp.bfloat16)
    grad_queries, grad_keys, grad_values = attend_back(
        queries, key_rows, value_rows, grad_heads, log_totals, forms
    )
    grad_qkv = jnp.stack((grad_queries, grad_keys, grad_values), 3)
    qkv_weight_term = matmul("cabd,cabsk->dsk", input_attn, grad_qkv)
    grad_input_attn = collect_grad(matmul("cabsk,dsk->cabd", grad_qkv, qkv_full))
    shift_attn_grad = jnp.sum(grad_input_attn, (1, 2))
    scale_attn_grad = jnp.sum(grad_input_attn * normed_attn, (1, 2))
    grad_input = grad_mid + normalize_back(
        grad_input_attn * (1.0 + piece_of(1)), normed_attn, inv_attn
    )
    weight_terms = (
        lax.psum_scatter(
            qkv_weight_term.astype(jnp.bfloat16), "row", scatter_dimension=0, tiled=True
        ).astype(jnp.float32),
        lax.psum_scatter(
            mixing_weight_term.astype(jnp.bfloat16), "row", scatter_dimension=1, tiled=True
        ).astype(jnp.float32),
        lax.psum_scatter(
            hidden_weight_term.astype(jnp.bfloat16), "row", scatter_dimension=0, tiled=True
        ).astype(jnp.float32),
        lax.psum_scatter(
            output_weight_term.astype(jnp.bfloat16), "row", scatter_dimension=1, tiled=True
        ).astype(jnp.float32),
    )
    modulation_grad = jnp.stack(
        (
            shift_attn_grad,
            scale_attn_grad,
            gate_attn_grad,
            shift_mlp_grad,
            scale_mlp_grad,
            gate_mlp_grad,
        ),
        1,
    )
    attn_bias_term = jnp.stack(
        (
            jnp.sum(grad_queries.astype(jnp.float32), (0, 1, 2)),
            jnp.sum(grad_values.astype(jnp.float32), (0, 1, 2)),
        )
    )
    bias_terms = (
        attn_bias_term,
        jnp.sum(grad_attn.astype(jnp.float32), (0, 1, 2)),
        jnp.sum(grad_pre.astype(jnp.float32), (0, 1, 2)),
        jnp.sum(grad_mlp.astype(jnp.float32), (0, 1, 2)),
    )
    return (grad_input, weight_terms, modulation_grad, bias_terms)


def tensor_parallel(
    tokens,
    conditioning,
    ada_weight,
    ada_bias,
    qkv_weight,
    attn_bias,
    mixing_weight,
    mixing_bias,
    hidden_weight,
    hidden_bias,
    output_weight,
    output_bias,
    cotangent,
):
    col_width = ada_bias.shape[2]
    row_width = conditioning.shape[1]
    hidden_width = hidden_bias.shape[1]
    layer_count = ada_bias.shape[0]
    ada_weight = ada_weight.reshape(layer_count, row_width, 6, col_width)
    qkv_weight = qkv_weight.reshape(layer_count, row_width, 3, col_width)
    mixing_weight = mixing_weight.reshape(layer_count, col_width, row_width)
    hidden_weight = hidden_weight.reshape(layer_count, row_width, hidden_width)
    output_weight = output_weight.reshape(layer_count, hidden_width, row_width)
    tokens = open_tokens(tokens, col_width)
    cotangent = open_tokens(cotangent, col_width)
    cond_act = jax.nn.silu(conditioning).astype(jnp.bfloat16)
    modulation = lax.psum(
        (
            matmul("cr,rsk->csk", cond_act, ada_weight[0]),
            matmul("cr,rsk->csk", cond_act, ada_weight[1]),
        ),
        "row",
    )
    modulation = (modulation[0] + ada_bias[0][None], modulation[1] + ada_bias[1][None])

    def biases_of(depth):
        return (attn_bias[depth], mixing_bias[depth], hidden_bias[depth], output_bias[depth])

    stream_first = tokens.astype(jnp.float32)
    weights_first = fetch_weights(qkv_weight, mixing_weight, hidden_weight, output_weight, 0)
    output_first, saved_first = residual_forward(
        stream_first, modulation[0], weights_first, biases_of(0), spatial_forms
    )
    moved = lax.all_to_all(
        output_first.astype(jnp.bfloat16), "row", split_axis=2, concat_axis=1, tiled=True
    )
    stream_second = moved.astype(jnp.float32)
    weights_second = fetch_weights(qkv_weight, mixing_weight, hidden_weight, output_weight, 1)
    output_second, saved_second = residual_forward(
        stream_second, modulation[1], weights_second, biases_of(1), temporal_forms
    )
    result = output_second.astype(jnp.bfloat16)
    weights_second = fetch_weights(qkv_weight, mixing_weight, hidden_weight, output_weight, 1)
    saved_second = residual_forward(
        stream_second, modulation[1], weights_second, biases_of(1), temporal_forms
    )[1]
    grad_second, terms_second, modgrad_second, biasgrad_second = residual_backward(
        cotangent.astype(jnp.float32), saved_second, modulation[1], weights_second, temporal_forms
    )
    returned = lax.all_to_all(
        grad_second.astype(jnp.bfloat16), "row", split_axis=1, concat_axis=2, tiled=True
    )
    weights_first = fetch_weights(qkv_weight, mixing_weight, hidden_weight, output_weight, 0)
    saved_first = residual_forward(
        stream_first, modulation[0], weights_first, biases_of(0), spatial_forms
    )[1]
    grad_first, terms_first, modgrad_first, biasgrad_first = residual_backward(
        returned.astype(jnp.float32), saved_first, modulation[0], weights_first, spatial_forms
    )
    summed = (
        lax.psum(jnp.stack((modgrad_first, modgrad_second)).astype(jnp.bfloat16), "row").astype(
            jnp.float32
        ),
        lax.psum(
            jnp.stack((biasgrad_first[0], biasgrad_second[0])).astype(jnp.bfloat16), "row"
        ).astype(jnp.float32),
        lax.psum(
            jnp.stack((biasgrad_first[1], biasgrad_second[1])).astype(jnp.bfloat16), "row"
        ).astype(jnp.float32),
        lax.psum(
            jnp.stack((biasgrad_first[2], biasgrad_second[2])).astype(jnp.bfloat16), "row"
        ).astype(jnp.float32),
        lax.psum(
            jnp.stack((biasgrad_first[3], biasgrad_second[3])).astype(jnp.bfloat16), "row"
        ).astype(jnp.float32),
    )
    modulation_grad = summed[0]
    ada_bias_grad = jnp.sum(modulation_grad, 1)
    ada_weight_grad = jnp.einsum(
        "cr,lcsk->lrsk", cond_act.astype(jnp.float32), modulation_grad, precision=highest
    )
    cond_part = jnp.einsum(
        "lcsk,lrsk->cr", modulation_grad, ada_weight.astype(jnp.float32), precision=highest
    )
    cond_part = lax.psum(cond_part, "col")
    conditioning_gradient = jax.vjp(jax.nn.silu, conditioning)[1](cond_part)[0]
    qkv_weight_grad = jnp.stack((terms_first[0], terms_second[0]))
    mixing_weight_grad = jnp.stack((terms_first[1], terms_second[1]))
    hidden_weight_grad = jnp.stack((terms_first[2], terms_second[2]))
    output_weight_grad = jnp.stack((terms_first[3], terms_second[3]))
    return (
        close_tokens(result),
        close_tokens(grad_first),
        conditioning_gradient,
        close_weight(ada_weight_grad),
        ada_bias_grad,
        close_weight(qkv_weight_grad),
        summed[1],
        close_weight(mixing_weight_grad),
        summed[2],
        close_weight(hidden_weight_grad),
        summed[3],
        close_weight(output_weight_grad),
        summed[4],
    )


def exchange(values, axis, mask):
    count = lax.axis_size(axis)
    return lax.ppermute(values, axis, [(index, index ^ mask) for index in range(count)])


def add_low(first, second):
    return (first.astype(jnp.float32) + second.astype(jnp.float32)).astype(jnp.bfloat16)


def after(values, *others):
    return lax.optimization_barrier((values,) + others)[0]


def together(*values):
    return lax.optimization_barrier(values)


def over_depth(values, place):
    groups = [list(range(core, place.row_count, 2)) for core in range(2)]
    return lax.all_to_all(
        values, "row", split_axis=0, concat_axis=0, tiled=True, axis_index_groups=groups
    )


def swap(values):
    return exchange(values, "row", 1)


class Gathering:
    def __init__(self, place):
        self.place = place
        self.held = ()
        self.plane = ()
        self.corner = ()
        self.sent = ()
        self.done = []

    def step(self, shard, *gates):
        groups = (self.held, self.plane, self.corner)
        values = list(together(*[value for group in groups for value in group], *gates))
        held, plane, corner = [[values.pop(0) for _ in group] for group in groups]
        across, above = ([], [])
        if held:
            across.append(held[0])
            above.append(held[0])
        if plane:
            size = plane[0].shape[0]
            across.append(plane[2][size // 2 : size])
            above.append(plane[1][: size // 2])
        across = [jnp.concatenate(across, 0)] if across else []
        above = [jnp.concatenate(above, 0)] if above else []
        self.sent = tuple(across + above)
        self.held = ()
        if shard is not None:
            self.held = (over_depth(after(shard, *self.sent), self.place),)
        if corner:
            own = pack_blocks(after(corner, *self.sent))
            self.done.append((own, swap(own)))
        met = tuple(
            exchange(value[0], "col", mask) for mask, value in ((1, across), (2, above)) if value
        )
        self.corner = tuple(plane) + met if plane else ()
        self.plane = tuple(held) + met if held else ()


def scatter_corner(blocks):
    held, across_upper, across_first, above_first, above_lower = blocks
    return (
        held,
        across_upper,
        exchange(across_first, "col", 1),
        exchange(above_first, "col", 2),
        above_lower,
    )


def scatter_sides(blocks):
    held, across_upper, across_first, above_first, above_lower = blocks
    half = across_upper.shape[0]
    return (
        add_low(across_upper, above_first[half:]),
        add_low(above_lower, across_first[half:]),
    )


def scatter_plane(blocks, sides):
    held, _, across_first, above_first, _ = blocks
    across, above = sides
    return (held, exchange(across, "col", 1), across_first, above_first, exchange(above, "col", 2))


def add_all(pieces, place):
    count = place.row_count // 2
    pieces = pieces.reshape((count, -1) + pieces.shape[1:])
    return jnp.sum(pieces.astype(jnp.float32), 0)


class Place:
    def __init__(self):
        self.row = lax.axis_index("row")
        self.col = lax.axis_index("col")
        self.row_count = lax.axis_size("row")
        self.col_count = lax.axis_size("col")
        self.core = self.row & 1
        self.depth_masks = []
        mask = 2
        while mask < self.row_count:
            self.depth_masks.append(mask)
            mask *= 2


def mine_first(halves, place, axis):
    return jnp.where(place.core == 1, jnp.flip(halves, axis), halves)


def to_halves(features, place):
    width = features.shape[-1]
    lead = features.shape[:-1]
    split_up = features.reshape(lead + (place.row_count // 2, 2, width // place.row_count))
    halves = jnp.swapaxes(split_up, -3, -2).reshape(lead + (2, width // 2))
    return mine_first(halves, place, len(lead))


def from_halves(halves, place):
    lead = halves.shape[:-2]
    half = halves.shape[-1]
    halves = mine_first(halves, place, len(lead))
    split_up = halves.reshape(lead + (2, place.row_count // 2, half // (place.row_count // 2)))
    return jnp.swapaxes(split_up, -3, -2).reshape(lead + (2 * half,))


def relative(stacked, place):
    return [
        lax.dynamic_index_in_dim(stacked, place.col ^ step, 0, keepdims=False)
        for step in range(place.col_count)
    ]


def absolute(blocks, place):
    return jnp.stack(relative(jnp.stack(blocks), place))


def trade(blocks):
    return [
        block if step == 0 else exchange(block, "col", step) for step, block in enumerate(blocks)
    ]


PLAIN = ((1,), (0,))
TURNED = ((1,), (1,))
SUMMED = ((0,), (0,))
VMEM_BYTES = 58 * 1024 * 1024
LANES = 128
IN_HBM = pl.BlockSpec(memory_space=pl.ANY)
SMALL_COST = pl.CostEstimate(flops=0, bytes_accessed=0, transcendentals=0)


def dot(left, right, dims):
    return lax.dot_general(left, right, (dims, ((), ())), preferred_element_type=jnp.float32)


def round_up(value):
    return -(-value // LANES) * LANES


def whole(shape):
    return pl.BlockSpec(shape, lambda step: (0,) * len(shape))


def stepped(shape):
    return pl.BlockSpec((1,) + shape, lambda step: (step,) + (0,) * len(shape))


def of(shape, dtype):
    return jax.ShapeDtypeStruct(shape, dtype)


def norm_parts(stream_ref):
    first, second = (stream_ref[0], stream_ref[1])
    count = 2 * first.shape[1]
    average = (jnp.sum(first, 1, keepdims=True) + jnp.sum(second, 1, keepdims=True)) / count
    first, second = (first - average, second - average)
    variance = (
        jnp.sum(first * first, 1, keepdims=True) + jnp.sum(second * second, 1, keepdims=True)
    ) / count
    inverse = lax.rsqrt(variance + epsilon)
    return (first * inverse, second * inverse, inverse)


def norm_grads(stream_ref, acc, mod_ref, scale_row, grad_ref, out_ref, small_ref):
    normed = norm_parts(stream_ref)
    inverse = normed[2]
    count = 2 * normed[0].shape[1]
    weighted = []
    for half in range(2):
        grad_input = acc[half]
        small_ref[half, 0:1, :] = jnp.sum(grad_input, 0, keepdims=True)
        small_ref[half, 1:2, :] = jnp.sum(grad_input * normed[half], 0, keepdims=True)
        weighted.append(grad_input * (1.0 + mod_ref[half, scale_row : scale_row + 1, :]))
    first = sum(jnp.sum(value, 1, keepdims=True) for value in weighted) / count
    second = (
        sum(jnp.sum(value * normed[half], 1, keepdims=True) for half, value in enumerate(weighted))
        / count
    )
    for half in range(2):
        out_ref[half] = grad_ref[half] + inverse * (
            weighted[half] - first - normed[half] * second
        )


def same_place(size, period):
    row = lax.broadcasted_iota(jnp.int32, (size, size), 0)
    column = lax.broadcasted_iota(jnp.int32, (size, size), 1)
    return (row % period) == (column % period)


def attention_kernel(size, period, steps, *refs):
    stream_ref, mod_ref, bias_ref, added_ref = refs[:4]
    weights = refs[4:6]
    mid_ref, mine_ref, other_ref, qkv_ref, heads_ref, log_ref, out_ref, acc, kept_ref = refs[6:]
    input_refs = (mine_ref, kept_ref)
    step = pl.program_id(0)
    tokens = stream_ref.shape[1]
    used = qkv_ref.shape[2]
    padded = heads_ref.shape[2]
    columns = weights[0].shape[2]
    width = columns // 4
    count = width // HEAD_DIM
    scale = HEAD_DIM ** (-0.5)

    @pl.when(step == 0)
    def _():
        normed = norm_parts(stream_ref)
        for half in range(2):
            input_refs[half][...] = (
                normed[half] * (1.0 + mod_ref[half, 1:2, :]) + mod_ref[half, 0:1, :]
            ).astype(jnp.bfloat16)
        other_ref[...] = kept_ref[...].T
        acc[...] = jnp.zeros_like(acc)

    rows = dot(input_refs[0][...], weights[0][0, :, :used], PLAIN)
    rows = rows + dot(input_refs[1][...], weights[1][0, :, :used], PLAIN) + bias_ref[0]
    lane = lax.broadcasted_iota(jnp.int32, rows.shape, 1)
    qkv_ref[0] = jnp.where(lane < 3 * width, rows, 0.0).astype(jnp.bfloat16)
    log_lane = lax.broadcasted_iota(jnp.int32, (size, LANES), 1)
    for group in range(tokens // size):
        block = qkv_ref[0, group * size : (group + 1) * size, :]
        outs = [jnp.zeros((size, padded - width), jnp.float32)]
        logs = jnp.zeros((size, LANES), jnp.float32)
        for head in range(count):
            start = head * HEAD_DIM
            query = block[:, start : start + HEAD_DIM]
            key = block[:, width + start : width + start + HEAD_DIM]
            value = block[:, 2 * width + start : 2 * width + start + HEAD_DIM]
            scores = dot(query, key, TURNED) * scale
            if period:
                scores = jnp.where(same_place(size, period), scores, -1e30)
            largest = jnp.max(scores, 1, keepdims=True)
            weight = jnp.exp(scores - largest)
            total = jnp.sum(weight, 1, keepdims=True)
            probs = (weight * (1.0 / total)).astype(jnp.bfloat16)
            outs.append(dot(probs, value, PLAIN))
            logs = jnp.where(log_lane == head, largest + jnp.log(total), logs)
        heads_ref[0, group * size : (group + 1) * size, :] = jnp.concatenate(outs, 1).astype(
            jnp.bfloat16
        )
        log_ref[0, group * size : (group + 1) * size, :] = logs
    for half in range(2):
        acc[half] += dot(heads_ref[0], weights[half][0, :, columns - padded :], TURNED)

    @pl.when(step == steps - 1)
    def _():
        for half in range(2):
            total = acc[half] + added_ref[half]
            out_ref[half] = total.astype(jnp.bfloat16)
            mid_ref[half] = stream_ref[half] + mod_ref[half, 2:3, :] * total


def attention_forward(stream, modulation, weights, bias, added, size, period):
    steps = weights[0].shape[0]
    _, tokens, half = stream.shape
    columns = weights[0].shape[2]
    used = round_up(3 * columns // 4)
    padded = columns - (3 * columns // 4) // LANES * LANES
    bf16, f32 = (jnp.bfloat16, jnp.float32)
    return pl.pallas_call(
        functools.partial(attention_kernel, size, period, steps),
        grid=(steps,),
        in_specs=[
            whole(stream.shape),
            whole(modulation.shape),
            stepped((1, used)),
            whole(added.shape),
        ]
        + [stepped((half, columns))] * 2,
        out_specs=[
            whole(stream.shape),
            whole((tokens, half)),
            whole((half, tokens)),
            stepped((tokens, used)),
            stepped((tokens, padded)),
            stepped((tokens, LANES)),
            whole(stream.shape),
        ],
        out_shape=[
            of(stream.shape, f32),
            of((tokens, half), bf16),
            of((half, tokens), bf16),
            of((steps, tokens, used), bf16),
            of((steps, tokens, padded), bf16),
            of((steps, tokens, LANES), f32),
            of(stream.shape, bf16),
        ],
        scratch_shapes=[
            pltpu.VMEM(stream.shape, f32),
            pltpu.VMEM((tokens, half), bf16),
        ],
        compiler_params=pltpu.CompilerParams(vmem_limit_bytes=VMEM_BYTES),
        cost_estimate=SMALL_COST,
        name="attention_forward",
    )(stream, modulation, bias, added, *weights)


def mlp_kernel(steps, *refs):
    mid_ref, mod_ref, bias_ref, added_ref = refs[:4]
    hidden, output = (refs[4:6], refs[6:8])
    stream_ref, mine_ref, other_ref, active_ref, slope_ref, out_ref, acc, kept_ref = refs[8:]
    input_refs = (mine_ref, kept_ref)
    step = pl.program_id(0)

    @pl.when(step == 0)
    def _():
        normed = norm_parts(mid_ref)
        for half in range(2):
            input_refs[half][...] = (
                normed[half] * (1.0 + mod_ref[half, 4:5, :]) + mod_ref[half, 3:4, :]
            ).astype(jnp.bfloat16)
        other_ref[...] = kept_ref[...].T
        acc[...] = jnp.zeros_like(acc)

    pre = dot(input_refs[0][...], hidden[0][0], PLAIN)
    pre = pre + dot(input_refs[1][...], hidden[1][0], PLAIN) + bias_ref[0]
    root = (2.0 / jnp.pi) ** 0.5
    square = pre * pre
    bend = jnp.tanh(pre * (root + root * 0.044715 * square))
    active_ref[0] = (0.5 * pre * (1.0 + bend)).astype(jnp.bfloat16)
    slope_ref[0] = (
        0.5 * (1.0 + bend)
        + 0.5 * pre * (1.0 - bend * bend) * (root + 3.0 * root * 0.044715 * square)
    ).astype(jnp.bfloat16)
    for half in range(2):
        acc[half] += dot(active_ref[0], output[half][0], TURNED)

    @pl.when(step == steps - 1)
    def _():
        for half in range(2):
            total = acc[half] + added_ref[half]
            out_ref[half] = total.astype(jnp.bfloat16)
            stream_ref[half] = mid_ref[half] + mod_ref[half, 5:6, :] * total


def mlp_forward(mid, modulation, hidden, output, bias, added):
    steps = hidden[0].shape[0]
    _, tokens, half = mid.shape
    columns = hidden[0].shape[2]
    bf16, f32 = (jnp.bfloat16, jnp.float32)
    return pl.pallas_call(
        functools.partial(mlp_kernel, steps),
        grid=(steps,),
        in_specs=[
            whole(mid.shape),
            whole(modulation.shape),
            stepped((1, columns)),
            whole(added.shape),
        ]
        + [stepped((half, columns))] * 4,
        out_specs=[
            whole(mid.shape),
            whole((tokens, half)),
            whole((half, tokens)),
            stepped((tokens, columns)),
            stepped((tokens, columns)),
            whole(mid.shape),
        ],
        out_shape=[
            of(mid.shape, f32),
            of((tokens, half), bf16),
            of((half, tokens), bf16),
            of((steps, tokens, columns), bf16),
            of((steps, tokens, columns), bf16),
            of(mid.shape, bf16),
        ],
        scratch_shapes=[
            pltpu.VMEM(mid.shape, f32),
            pltpu.VMEM((tokens, half), bf16),
        ],
        compiler_params=pltpu.CompilerParams(vmem_limit_bytes=VMEM_BYTES),
        cost_estimate=SMALL_COST,
        name="mlp_forward",
    )(mid, modulation, bias, added, *hidden, *output)


def mlp_back_kernel(steps, *refs):
    grad_ref, mid_ref, out_ref, slope_ref, mod_ref = refs[:5]
    hidden, output = (refs[5:7], refs[7:9])
    grad_mid_ref, mine_ref, other_ref, grad_pre_ref, small_ref, sum_ref, acc, kept_ref = refs[9:]
    grad_mlp_refs = (mine_ref, kept_ref)
    step = pl.program_id(0)

    @pl.when(step == 0)
    def _():
        for half in range(2):
            grad = grad_ref[half]
            scaled = (grad * mod_ref[half, 5:6, :]).astype(jnp.bfloat16)
            grad_mlp_refs[half][...] = scaled
            small_ref[half, 2:3, :] = jnp.sum(
                grad * out_ref[half].astype(jnp.float32), 0, keepdims=True
            )
            small_ref[half, 3:4, :] = jnp.sum(scaled.astype(jnp.float32), 0, keepdims=True)
        other_ref[...] = kept_ref[...].T
        acc[...] = jnp.zeros_like(acc)

    grad_act = dot(grad_mlp_refs[0][...], output[0][0], PLAIN)
    grad_act = grad_act + dot(grad_mlp_refs[1][...], output[1][0], PLAIN)
    grad_pre = (grad_act * slope_ref[0].astype(jnp.float32)).astype(jnp.bfloat16)
    grad_pre_ref[0] = grad_pre
    sum_ref[0] = jnp.sum(grad_pre.astype(jnp.float32), 0, keepdims=True)
    for half in range(2):
        acc[half] += dot(grad_pre, hidden[half][0], TURNED)

    @pl.when(step == steps - 1)
    def _():
        norm_grads(mid_ref, acc, mod_ref, 4, grad_ref, grad_mid_ref, small_ref)


def mlp_backward(grad, mid, out, slope, modulation, hidden, output):
    steps = hidden[0].shape[0]
    _, tokens, half = mid.shape
    columns = hidden[0].shape[2]
    bf16, f32 = (jnp.bfloat16, jnp.float32)
    return pl.pallas_call(
        functools.partial(mlp_back_kernel, steps),
        grid=(steps,),
        in_specs=[
            whole(mid.shape),
            whole(mid.shape),
            whole(mid.shape),
            stepped((tokens, columns)),
            whole(modulation.shape),
        ]
        + [stepped((half, columns))] * 4,
        out_specs=[
            whole(mid.shape),
            whole((tokens, half)),
            whole((half, tokens)),
            stepped((tokens, columns)),
            whole((2, 8, half)),
            stepped((1, columns)),
        ],
        out_shape=[
            of(mid.shape, f32),
            of((tokens, half), bf16),
            of((half, tokens), bf16),
            of((steps, tokens, columns), bf16),
            of((2, 8, half), f32),
            of((steps, 1, columns), f32),
        ],
        scratch_shapes=[
            pltpu.VMEM(mid.shape, f32),
            pltpu.VMEM((tokens, half), bf16),
        ],
        compiler_params=pltpu.CompilerParams(vmem_limit_bytes=VMEM_BYTES),
        cost_estimate=SMALL_COST,
        name="mlp_backward",
    )(grad, mid, out, slope, modulation, *hidden, *output)


def attention_back_kernel(size, period, steps, *refs):
    grad_ref, stream_ref, out_ref, qkv_ref, log_ref, mod_ref = refs[:6]
    weights = refs[6:8]
    grad_in_ref, mine_ref, other_ref, grad_qkv_ref, small_ref, sum_ref, acc, kept_ref = refs[8:]
    grad_attn_refs = (mine_ref, kept_ref)
    step = pl.program_id(0)
    tokens = stream_ref.shape[1]
    used = qkv_ref.shape[2]
    columns = weights[0].shape[2]
    width = columns // 4
    padded = columns - (3 * width) // LANES * LANES
    count = width // HEAD_DIM
    scale = HEAD_DIM ** (-0.5)

    @pl.when(step == 0)
    def _():
        for half in range(2):
            grad = grad_ref[half]
            scaled = (grad * mod_ref[half, 2:3, :]).astype(jnp.bfloat16)
            grad_attn_refs[half][...] = scaled
            small_ref[half, 2:3, :] = jnp.sum(
                grad * out_ref[half].astype(jnp.float32), 0, keepdims=True
            )
            small_ref[half, 3:4, :] = jnp.sum(scaled.astype(jnp.float32), 0, keepdims=True)
        other_ref[...] = kept_ref[...].T
        acc[...] = jnp.zeros_like(acc)

    grad_heads = dot(grad_attn_refs[0][...], weights[0][0, :, columns - padded :], PLAIN)
    grad_heads = grad_heads + dot(grad_attn_refs[1][...], weights[1][0, :, columns - padded :], PLAIN)
    grad_heads = grad_heads.astype(jnp.bfloat16)
    total = jnp.zeros((1, used), jnp.float32)
    for group in range(tokens // size):
        rows = slice(group * size, (group + 1) * size)
        block = qkv_ref[0, rows, :]
        logs = log_ref[0, rows, :]
        grad_queries, grad_keys, grad_values = ([], [], [])
        for head in range(count):
            start = head * HEAD_DIM
            query = block[:, start : start + HEAD_DIM]
            key = block[:, width + start : width + start + HEAD_DIM]
            value = block[:, 2 * width + start : 2 * width + start + HEAD_DIM]
            start = padded - width + head * HEAD_DIM
            grad_out = grad_heads[rows, start : start + HEAD_DIM]
            scores = dot(query, key, TURNED) * scale - logs[:, head : head + 1]
            if period:
                scores = jnp.where(same_place(size, period), scores, -1e30)
            probs = jnp.exp(scores)
            grad_probs = dot(grad_out, value, TURNED)
            delta = jnp.sum(probs * grad_probs, 1, keepdims=True)
            grad_scores = (probs * (grad_probs - delta)).astype(jnp.bfloat16)
            grad_values.append(dot(probs.astype(jnp.bfloat16), grad_out, SUMMED))
            grad_queries.append(dot(grad_scores, key, PLAIN) * scale)
            grad_keys.append(dot(grad_scores, query, SUMMED) * scale)
        rest = [jnp.zeros((size, used - 3 * width), jnp.float32)]
        joined = jnp.concatenate(grad_queries + grad_keys + grad_values + rest, 1)
        joined = joined.astype(jnp.bfloat16)
        grad_qkv_ref[0, rows, :] = joined
        total = total + jnp.sum(joined.astype(jnp.float32), 0, keepdims=True)
    sum_ref[0] = total
    for half in range(2):
        acc[half] += dot(grad_qkv_ref[0], weights[half][0, :, :used], TURNED)

    @pl.when(step == steps - 1)
    def _():
        norm_grads(stream_ref, acc, mod_ref, 1, grad_ref, grad_in_ref, small_ref)


def attention_backward(grad, stream, out, qkv, logs, modulation, weights, size, period):
    steps = weights[0].shape[0]
    _, tokens, half = stream.shape
    columns = weights[0].shape[2]
    used = qkv.shape[2]
    bf16, f32 = (jnp.bfloat16, jnp.float32)
    return pl.pallas_call(
        functools.partial(attention_back_kernel, size, period, steps),
        grid=(steps,),
        in_specs=[
            whole(stream.shape),
            whole(stream.shape),
            whole(stream.shape),
            stepped((tokens, used)),
            stepped((tokens, LANES)),
            whole(modulation.shape),
        ]
        + [stepped((half, columns))] * 2,
        out_specs=[
            whole(stream.shape),
            whole((tokens, half)),
            whole((half, tokens)),
            stepped((tokens, used)),
            whole((2, 8, half)),
            stepped((1, used)),
        ],
        out_shape=[
            of(stream.shape, f32),
            of((tokens, half), bf16),
            of((half, tokens), bf16),
            of((steps, tokens, used), bf16),
            of((2, 8, half), f32),
            of((steps, 1, used), f32),
        ],
        scratch_shapes=[
            pltpu.VMEM(stream.shape, f32),
            pltpu.VMEM((tokens, half), bf16),
        ],
        compiler_params=pltpu.CompilerParams(vmem_limit_bytes=VMEM_BYTES),
        cost_estimate=SMALL_COST,
        name="attention_backward",
    )(grad, stream, out, qkv, logs, modulation, *weights)


def weight_kernel(pairs, overlap, steps, *refs):
    inputs = refs[: 4 * pairs]
    outs = refs[4 * pairs : 4 * pairs + 5]
    turned = refs[4 * pairs + 5 : 5 * pairs + 5]
    buffer, sems = refs[5 * pairs + 5 :]
    step = pl.program_id(0)
    slot = step % 2
    for pair in range(pairs):
        mine = inputs[4 * pair]

        @pl.when(step == 0)
        def _():
            turned[pair][...] = mine[...].T

    @pl.when(step >= 2)
    def _():
        pltpu.make_async_copy(buffer.at[slot], outs[0], sems.at[slot]).wait()

    sums = []
    for pair in range(pairs):
        _, rows, mine, theirs = inputs[4 * pair : 4 * pair + 4]
        total = dot(turned[pair][...], mine[0], PLAIN)
        sums.append(total + dot(rows[...], theirs[0], PLAIN))
    if pairs == 1:
        buffer[slot] = sums[0].astype(jnp.bfloat16)
    else:
        first = sums[0].shape[1] - overlap
        buffer[slot, :, :first] = sums[0][:, :first].astype(jnp.bfloat16)
        buffer[slot, :, first : first + overlap] = (
            sums[0][:, first:] + sums[1][:, :overlap]
        ).astype(jnp.bfloat16)
        buffer[slot, :, first + overlap :] = sums[1][:, overlap:].astype(jnp.bfloat16)
    for index in range(steps):

        @pl.when(step == index)
        def _():
            source = buffer.at[index % 2]
            sem = sems.at[index % 2]
            if index == 0:
                pltpu.make_async_copy(source, outs[0], sem).start()
            else:
                rows = outs[1].shape[0]
                upper, lower = (
                    (outs[1], outs[2].at[:rows]),
                    (outs[3].at[:rows], outs[4]),
                    (outs[3].at[rows:], outs[2].at[rows:]),
                )[index - 1]
                pltpu.make_async_copy(source.at[:rows], upper, sem).start()
                pltpu.make_async_copy(source.at[rows:], lower, sem).start()

    @pl.when(step == steps - 1)
    def _():
        for index in range(2):
            pltpu.make_async_copy(buffer.at[index], outs[0], sems.at[index]).wait()


def weight_grads(columns, overlap, *pairs, flops=0):
    steps, tokens, _ = pairs[0][2].shape
    half = pairs[0][1].shape[0]
    bf16 = jnp.bfloat16
    specs, values, turned = ([], [], [])
    for mine, theirs, blocks, their_blocks in pairs:
        specs += [
            whole(mine.shape),
            whole(theirs.shape),
            stepped(blocks.shape[1:]),
            stepped(blocks.shape[1:]),
        ]
        values += [mine, theirs, blocks, their_blocks]
        turned.append(pltpu.VMEM((half, tokens), bf16))
    return pl.pallas_call(
        functools.partial(weight_kernel, len(pairs), overlap, steps),
        grid=(steps,),
        in_specs=specs,
        out_specs=[IN_HBM] * 5,
        out_shape=[
            of((rows, columns), bf16) for rows in (half, half // 2, half, half, half // 2)
        ],
        scratch_shapes=turned
        + [pltpu.VMEM((2, half, columns), bf16), pltpu.SemaphoreType.DMA((2,))],
        compiler_params=pltpu.CompilerParams(vmem_limit_bytes=VMEM_BYTES),
        cost_estimate=pl.CostEstimate(flops=flops, bytes_accessed=0, transcendentals=0),
        name="weight_grads",
    )(*values)


def pack_kernel(held, across, above, lower, upper, out, buffer, sems):
    size = held.shape[0]
    half = size // 2
    corner = pl.ds(lower.shape[0] - half, half)
    incoming = [
        pltpu.make_async_copy(source, target, sems.at[index])
        for index, (source, target) in enumerate(
            (
                (held, buffer.at[0]),
                (across.at[:size], buffer.at[1]),
                (above.at[:size], buffer.at[2]),
                (upper.at[corner], buffer.at[3, :half]),
                (lower.at[corner], buffer.at[3, half:]),
            )
        )
    ]
    outgoing = [
        pltpu.make_async_copy(buffer.at[index], out.at[index], sems.at[5 + index])
        for index in range(4)
    ]
    for copy in incoming:
        copy.start()
    for index in range(3):
        incoming[index].wait()
        outgoing[index].start()
    incoming[3].wait()
    incoming[4].wait()
    outgoing[3].start()
    for copy in outgoing:
        copy.wait()


def pack_blocks(blocks):
    shape = (4,) + blocks[0].shape
    return pl.pallas_call(
        pack_kernel,
        in_specs=[IN_HBM] * 5,
        out_specs=IN_HBM,
        out_shape=of(shape, jnp.bfloat16),
        scratch_shapes=[pltpu.VMEM(shape, jnp.bfloat16), pltpu.SemaphoreType.DMA((9,))],
        compiler_params=pltpu.CompilerParams(vmem_limit_bytes=VMEM_BYTES // 4),
        cost_estimate=SMALL_COST,
        name="pack_blocks",
    )(*blocks)


def placing_matrix(core, part, block, half, shape):
    feature = lax.broadcasted_iota(jnp.int32, shape, 0) + block * shape[0]
    target = lax.broadcasted_iota(jnp.int32, shape, 1)
    row = feature // part
    match = (row & 1) == (core ^ half)
    match &= (row // 2) * part + (feature - row * part) == target
    return jnp.where(match, 1.0, 0.0).astype(jnp.bfloat16)


def enter_kernel(part, where_ref, *refs):
    *blocks, out_ref = refs
    shape = (blocks[0].shape[1], out_ref.shape[2])
    for half in range(2):
        total = None
        for step, block in enumerate(blocks):
            matrix = placing_matrix(where_ref[0], part, where_ref[1] ^ step, half, shape)
            term = dot(block[...], matrix, PLAIN)
            total = term if total is None else total + term
        out_ref[half] = total


def leave_kernel(part, where_ref, halves_ref, *outs):
    shape = (outs[0].shape[1], halves_ref.shape[2])
    halves = [halves_ref[half].astype(jnp.bfloat16) for half in range(2)]
    for step, out in enumerate(outs):
        total = None
        for half in range(2):
            matrix = placing_matrix(where_ref[0], part, where_ref[1] ^ step, half, shape)
            term = dot(halves[half], matrix, TURNED)
            total = term if total is None else total + term
        out[...] = total.astype(jnp.bfloat16)


def assemble_kernel(where_ref, *refs):
    *blocks, out_ref = refs
    for step, block in enumerate(blocks):
        out_ref[where_ref[1] ^ step] = block[...].astype(out_ref.dtype)


def reorder(kernel, values, outs, place):
    in_vmem = pl.BlockSpec(memory_space=pltpu.VMEM)
    where = jnp.stack((place.core, place.col)).astype(jnp.int32)
    return pl.pallas_call(
        kernel,
        in_specs=[pl.BlockSpec(memory_space=pltpu.SMEM)] + [in_vmem] * len(values),
        out_specs=[in_vmem] * len(outs),
        out_shape=outs,
        compiler_params=pltpu.CompilerParams(vmem_limit_bytes=VMEM_BYTES // 2),
        cost_estimate=SMALL_COST,
        name="reorder",
    )(where, *values)


def add_kernel(held, across_upper, across_first, above_first, above_lower, out):
    rows = across_upper.shape[0]
    for start, pair in ((0, (across_upper, above_first)), (rows, (across_first, above_lower))):
        total = held[start : start + rows].astype(jnp.float32)
        for value in pair:
            total += value[:rows].astype(jnp.float32)
        out[start : start + rows] = total.astype(jnp.bfloat16)


def add_blocks(blocks):
    in_vmem = pl.BlockSpec(memory_space=pltpu.VMEM)
    return pl.pallas_call(
        add_kernel,
        in_specs=[in_vmem] * 5,
        out_specs=in_vmem,
        out_shape=of(blocks[0].shape, jnp.bfloat16),
        compiler_params=pltpu.CompilerParams(vmem_limit_bytes=VMEM_BYTES // 2),
        cost_estimate=SMALL_COST,
        name="add_blocks",
    )(*blocks)


def token_parallel(
    tokens,
    conditioning,
    ada_weight,
    ada_bias,
    qkv_weight,
    attn_bias,
    mixing_weight,
    mixing_bias,
    hidden_weight,
    hidden_bias,
    output_weight,
    output_bias,
    cotangent,
):
    place = Place()
    col_width = ada_bias.shape[2]
    row_width = conditioning.shape[1]
    hidden_width = hidden_bias.shape[1]
    layer_count = ada_bias.shape[0]
    clip_count = conditioning.shape[0]
    width = col_width * place.col_count

    copies = (place.row_count // 2, 1)

    def attn_shards(*gate):
        first, second = together(qkv_weight, mixing_weight, *gate)[:2]
        return [
            jnp.tile(
                jnp.concatenate(
                    (
                        first[depth].reshape(row_width, 3 * col_width),
                        second[depth].reshape(col_width, row_width).T,
                    ),
                    1,
                ),
                copies,
            )
            for depth in range(layer_count)
        ]

    def hidden_shards(*gate):
        value = after(hidden_weight, *gate)
        return [
            jnp.tile(value[depth].reshape(row_width, hidden_width), copies)
            for depth in range(layer_count)
        ]

    def output_shards(*gate):
        value = after(output_weight, *gate)
        return [
            jnp.tile(value[depth].reshape(hidden_width, row_width).T, copies)
            for depth in range(layer_count)
        ]

    def arriving(held):
        return trade(relative(held.reshape(clip_count, -1, col_width), place))

    def entered(blocks):
        outs = [of((2, blocks[0].shape[0], width // 2), jnp.float32)]
        return reorder(functools.partial(enter_kernel, row_width), blocks, outs, place)[0]

    gathering = Gathering(place)
    attn_ready = attn_shards()
    tokens = after(open_tokens(tokens, col_width), attn_ready[0])
    cotangent = open_tokens(cotangent, col_width)
    frame_part, places = tokens.shape[1:3]
    frames, place_part = cotangent.shape[1:3]
    period = 16 if place_part % 16 == 0 else place_part
    groups = place_part // period
    first_size = places
    second_size = frames * period
    gathering.step(attn_ready[0])
    token_blocks = arriving(tokens)
    hidden_ready = hidden_shards(attn_ready[0])
    hidden_ready, attn_ready, token_blocks = together(hidden_ready, attn_ready, token_blocks)
    gathering.step(hidden_ready[0], *token_blocks)
    conditioning, ada_weight, attn_bias, token_blocks, output_gate = after(
        (conditioning, ada_weight, attn_bias, token_blocks, output_weight), *gathering.sent
    )
    output_weight = output_gate
    output_ready = output_shards()
    stream_first = entered(token_blocks)
    ada_weight = ada_weight.reshape(layer_count, row_width, 6, col_width)

    half = width // 2

    def leaving(halves):
        outs = [of((halves.shape[1], col_width), jnp.bfloat16)] * place.col_count
        return reorder(functools.partial(leave_kernel, row_width), [halves], outs, place)

    def assembled(blocks, dtype):
        outs = [of((len(blocks),) + blocks[0].shape, dtype)]
        return reorder(assemble_kernel, blocks, outs, place)[0]

    cond_act = jax.nn.silu(conditioning).astype(jnp.bfloat16)
    modulation = matmul("cr,lrsk->clsk", cond_act, ada_weight)
    modulation = modulation.reshape(clip_count, -1)
    cut = modulation.shape[1]
    own = [modulation] + [
        value.reshape(clip_count, -1)
        for value in (attn_bias, hidden_bias, mixing_bias, output_bias, ada_bias)
    ]
    met = lax.all_gather(jnp.concatenate(own, 1), ("row", "col"), axis=0)
    met = met.reshape(place.row_count, place.col_count, clip_count, -1)
    modulation = lax.dynamic_index_in_dim(met, place.col, 2, keepdims=False)[:, :, :cut]
    modulation = jnp.sum(modulation, 0).reshape(-1, layer_count, 6, col_width)
    rest = met[0, :, :, cut:]
    vectors = []
    for value in (attn_bias, hidden_bias, mixing_bias, output_bias, ada_bias):
        size = value.size // clip_count
        vectors.append(rest[:, :, :size].reshape((place.col_count,) + value.shape))
        rest = rest[:, :, size:]
    modulation = modulation + vectors.pop()
    modulation = jnp.moveaxis(modulation, 0, 2).reshape(layer_count, 6, width)
    modulation = jnp.swapaxes(to_halves(modulation, place), 1, 2)
    attn_add, hidden_add, mixing_add, output_add = vectors
    attn_add, hidden_add = (relative(value, place) for value in (attn_add, hidden_add))

    def whole_vector(blocks):
        joined = jnp.moveaxis(blocks, 0, 1).reshape(layer_count, width)
        return to_halves(joined, place)

    mixing_add = whole_vector(mixing_add)
    output_add = whole_vector(output_add)

    blank = jnp.zeros((round_up(3 * col_width) - 3 * col_width,), jnp.float32)

    def biases_of(depth):
        attn_rows = [
            jnp.concatenate((block[depth, 0], jnp.zeros_like(block[depth, 0]), block[depth, 1], blank))
            for block in attn_add
        ]
        return (
            jnp.stack(attn_rows)[:, None, :],
            mixing_add[depth][:, None, :],
            jnp.stack([block[depth] for block in hidden_add])[:, None, :],
            output_add[depth][:, None, :],
        )

    attn_biases, mixing_biases, hidden_biases, output_biases = zip(biases_of(0), biases_of(1))
    sizes = (first_size, second_size)
    periods = (0, period)

    def attn_part(depth, stream):
        return attention_forward(
            stream,
            modulation[depth],
            gathering.done[3 * depth],
            attn_biases[depth],
            mixing_biases[depth],
            sizes[depth],
            periods[depth],
        )

    def mlp_part(depth, mid):
        return mlp_forward(
            mid,
            modulation[depth],
            gathering.done[3 * depth + 1],
            gathering.done[3 * depth + 2],
            hidden_biases[depth],
            output_biases[depth],
        )

    def mlp_grads(depth, grad, saved):
        _, mid, _, (_, _, _, slope, mlp_out) = saved
        return mlp_backward(
            grad, mid, mlp_out, slope, modulation[depth], *gathering.done[3 * depth + 1 : 3 * depth + 3]
        )

    def attn_grads(depth, grad_mid, saved):
        stream, _, (_, _, qkv, _, logs, attn_out), _ = saved
        return attention_backward(
            grad_mid,
            stream,
            attn_out,
            qkv,
            logs,
            modulation[depth],
            gathering.done[3 * depth],
            sizes[depth],
            periods[depth],
        )

    def attn_terms(saved, swapped, grad_attn, grad_qkv, received, flops=0):
        input_attn, _, _, heads, _, _ = saved[2]
        columns = 4 * col_width
        return weight_grads(
            columns,
            grad_qkv.shape[2] + heads.shape[2] - columns,
            (input_attn, swapped[0], grad_qkv, received[0]),
            (grad_attn, received[1], heads, swapped[1]),
            flops=flops,
        )

    def output_terms(saved, swapped, grad_mlp, received):
        active = saved[3][2]
        return weight_grads(active.shape[2], 0, (grad_mlp, received, active, swapped[3]))

    def hidden_terms(saved, swapped, grad_pre, received):
        return weight_grads(
            grad_pre.shape[2], 0, (saved[3][0], swapped[2], grad_pre, received)
        )

    gathering.step(output_ready[0], stream_first, *output_ready)
    gathering.step(attn_ready[1], modulation)
    mid_first, *attn_first = attn_part(0, after(stream_first, *gathering.sent))
    gathering.step(hidden_ready[1], mid_first)
    cotangent = after(cotangent, *gathering.sent)
    cotangent = cotangent.reshape(clip_count, frames, groups, period, col_width)
    gradient_blocks = relative(
        jnp.swapaxes(cotangent, 1, 2).reshape(clip_count, -1, col_width), place
    )
    gathering.step(output_ready[1], *gradient_blocks)
    input_attn, heads = after((attn_first[1], attn_first[3]), *gathering.sent)
    swapped_first = [swap(input_attn), swap(heads)]
    output_first, *mlp_first = mlp_part(0, after(mid_first, *gathering.sent))
    saved_first = (stream_first, mid_first, attn_first, mlp_first)
    gathering.step(None, output_first, *swapped_first)
    input_mlp, active, moving = after(
        (mlp_first[1], mlp_first[2], output_first), *gathering.sent
    )
    swapped_first += [swap(input_mlp), swap(active)]
    moving = mine_first(moving.astype(jnp.bfloat16), place, 0)
    moving = moving.reshape(2, frame_part, place.row_count, groups, period, half)
    moving = moving.transpose(0, 2, 3, 1, 4, 5)
    moved = lax.all_to_all(moving, "row", split_axis=1, concat_axis=3, tiled=True)
    gathering.step(None, moved, *swapped_first[2:])
    moved = after(moved, *gathering.sent)
    moved = moved.reshape(2, -1, half)
    stream_second = mine_first(moved, place, 0).astype(jnp.float32)
    gathering.step(None)
    stream_second = after(stream_second, gathering.done[5][0])
    mid_second, *attn_second = attn_part(1, stream_second)
    mid_second, input_attn, heads = together(mid_second, attn_second[1], attn_second[3])
    swapped_second = [swap(input_attn), swap(heads)]
    gradient_blocks = trade(after(gradient_blocks, mid_second))
    output_second, *mlp_second = mlp_part(1, mid_second)
    saved_second = (stream_second, mid_second, attn_second, mlp_second)
    gradient_blocks, swapped_second, input_mlp, active, output_second = together(
        gradient_blocks, swapped_second, mlp_second[1], mlp_second[2], output_second
    )
    grad = entered(gradient_blocks)
    swapped_second += [swap(input_mlp), swap(active)]

    grad_mid, grad_mlp, grad_sent, grad_pre, small_mlp_second, hidden_sum_second = mlp_grads(
        1, grad, saved_second
    )
    grad_mid, grad_mlp, grad_sent, grad_pre, swapped_second, output_second = together(
        grad_mid, grad_mlp, grad_sent, grad_pre, swapped_second, output_second
    )
    received = swap(grad_sent)
    received, grad_pre = together(received, grad_pre)
    received_pre = swap(grad_pre)
    output_part = output_terms(saved_second, swapped_second, grad_mlp, received)
    output_part, received_pre, grad_mid = together(output_part, received_pre, grad_mid)
    output_part = scatter_corner(output_part)
    hidden_part = hidden_terms(saved_second, swapped_second, grad_pre, received_pre)
    hidden_part, grad_mid = together(hidden_part, grad_mid)
    hidden_part = scatter_corner(hidden_part)
    grad_second, grad_attn, grad_sent, grad_qkv, small_attn_second, qkv_sum_second = attn_grads(
        1, grad_mid, saved_second
    )
    grad_second, grad_attn, grad_sent, grad_qkv, output_part, output_second = together(
        grad_second, grad_attn, grad_sent, grad_qkv, output_part, output_second
    )
    received = [swap(grad_qkv), swap(grad_sent)]
    sides = scatter_sides(output_part)
    result_blocks = leaving(output_second)
    moving = mine_first(grad_second.astype(jnp.bfloat16), place, 0)
    moving = moving.reshape(2, 1, groups, frames, period, half)
    moved = lax.all_to_all(moving, "row", split_axis=3, concat_axis=1, tiled=True)
    received, grad_attn, grad_qkv, sides, result_blocks = together(
        received, grad_attn, grad_qkv, sides, result_blocks
    )
    output_part = scatter_plane(output_part, sides)
    attn_blocks = attn_terms(
        saved_second, swapped_second, grad_attn, grad_qkv, received, 15 * 10**9
    )
    attn_blocks, hidden_part, output_part = together(attn_blocks, hidden_part, output_part)
    attn_part_second = scatter_corner(attn_blocks)
    sides = scatter_sides(hidden_part)
    output_total = add_blocks(output_part)
    moved, output_total, sides = together(moved, output_total, sides)
    hidden_part = scatter_plane(hidden_part, sides)
    moved = moved.transpose(0, 3, 1, 2, 4, 5).reshape(2, -1, half)
    returned = mine_first(moved, place, 0).astype(jnp.float32)
    output_pieces = over_depth(output_total, place)
    result_blocks = trade(after(result_blocks, output_total))
    grad_mid, grad_mlp, grad_sent, grad_pre, small_mlp_first, hidden_sum_first = mlp_grads(
        0, returned, saved_first
    )
    grad_mid, grad_mlp, grad_sent, grad_pre, output_pieces, hidden_part, result_blocks = together(
        grad_mid, grad_mlp, grad_sent, grad_pre, output_pieces, hidden_part, result_blocks
    )
    received = swap(grad_sent)
    hidden_total = add_blocks(hidden_part)
    received, hidden_total, grad_pre = together(received, hidden_total, grad_pre)
    hidden_pieces = over_depth(hidden_total, place)
    received_pre = swap(grad_pre)
    output_blocks = output_terms(saved_first, swapped_first, grad_mlp, received)
    output_blocks, received_pre = together(output_blocks, received_pre)
    output_part = scatter_corner(output_blocks)
    hidden_blocks = hidden_terms(saved_first, swapped_first, grad_pre, received_pre)
    hidden_blocks, grad_mid, attn_part_second = together(
        hidden_blocks, grad_mid, attn_part_second
    )
    sides = scatter_sides(attn_part_second)
    grad_mid, sides = together(grad_mid, sides)
    attn_part_second = scatter_plane(attn_part_second, sides)
    hidden_part = scatter_corner(hidden_blocks)
    grad_first, grad_attn, grad_sent, grad_qkv, small_attn_first, qkv_sum_first = attn_grads(
        0, grad_mid, saved_first
    )
    (
        grad_first,
        grad_attn,
        grad_sent,
        grad_qkv,
        output_part,
        attn_part_second,
        hidden_pieces,
    ) = together(
        grad_first, grad_attn, grad_sent, grad_qkv, output_part, attn_part_second, hidden_pieces
    )
    received = [swap(grad_qkv), swap(grad_sent)]
    sides = scatter_sides(output_part)
    attn_total = add_blocks(attn_part_second)
    received, sides, attn_total, grad_attn, grad_qkv = together(
        received, sides, attn_total, grad_attn, grad_qkv
    )
    output_part = scatter_plane(output_part, sides)
    attn_pieces = over_depth(attn_total, place)
    attn_blocks = attn_terms(saved_first, swapped_first, grad_attn, grad_qkv, received)
    def small_grads(small_attn, small_mlp, qkv_sum, hidden_sum):
        return (
            jnp.concatenate((small_attn[:, :3], small_mlp[:, :3]), 1),
            (qkv_sum[:, 0], small_attn[:, 3], hidden_sum[:, 0], small_mlp[:, 3]),
        )

    modgrad_first, biasgrad_first = small_grads(
        small_attn_first, small_mlp_first, qkv_sum_first, hidden_sum_first
    )
    modgrad_second, biasgrad_second = small_grads(
        small_attn_second, small_mlp_second, qkv_sum_second, hidden_sum_second
    )
    def by_block(halves):
        features = from_halves(halves, place)
        features = features.reshape(features.shape[:-1] + (place.col_count, col_width))
        return relative(jnp.moveaxis(features, -2, 0), place)

    modgrad = by_block(jnp.swapaxes(jnp.stack((modgrad_first, modgrad_second)), 1, 2))
    mixgrad = by_block(jnp.stack((biasgrad_first[1], biasgrad_second[1])))
    outgrad = by_block(jnp.stack((biasgrad_first[3], biasgrad_second[3])))
    sending = []
    for step in range(place.col_count):
        pieces = [modgrad[step].reshape(-1)]
        for grads in (biasgrad_first, biasgrad_second):
            pieces.append(grads[0][step][:col_width])
            pieces.append(grads[0][step][2 * col_width : 3 * col_width])
        for grads in (biasgrad_first, biasgrad_second):
            pieces.append(grads[2][step])
        pieces.append(mixgrad[step].reshape(-1))
        pieces.append(outgrad[step].reshape(-1))
        sending.append(jnp.concatenate(pieces))
    sending = [value.reshape(-1, LANES) for value in sending]
    attn_blocks, output_part, hidden_part, grad_first, result_blocks = together(
        attn_blocks, output_part, hidden_part, grad_first, result_blocks
    )
    attn_part_first = scatter_corner(attn_blocks)
    sides = scatter_sides(hidden_part)
    output_total = add_blocks(output_part)
    output_total, sides, grad_first, attn_pieces = together(
        output_total, sides, grad_first, attn_pieces
    )
    hidden_part = scatter_plane(hidden_part, sides)
    output_first_pieces = over_depth(output_total, place)
    gradient_blocks = leaving(grad_first)

    result = assembled(result_blocks, jnp.bfloat16)
    result = result.reshape(clip_count, groups, frames, period, col_width)
    result = jnp.swapaxes(result, 1, 2).reshape(clip_count, frames, place_part, col_width)
    result = close_tokens(result)
    attn_part_first, hidden_part, gradient_blocks, sending, result = together(
        attn_part_first, hidden_part, gradient_blocks, sending, result
    )
    sides = scatter_sides(attn_part_first)
    hidden_total = add_blocks(hidden_part)
    sides, hidden_total, sending, output_first_pieces = together(
        sides, hidden_total, sending, output_first_pieces
    )
    attn_part_first = scatter_plane(attn_part_first, sides)
    met = trade(sending)
    hidden_first_pieces = over_depth(hidden_total, place)
    met = [value.reshape(-1) for value in met]
    modgrad = jnp.concatenate([block[:cut] for block in met])
    biasgrad = sum(block[cut:] for block in met)
    small = jnp.concatenate((modgrad, biasgrad))
    small = small + swap(small)
    small, attn_part_first = together(small, attn_part_first)
    attn_total = add_blocks(attn_part_first)
    small, attn_total = together(small, attn_total)
    gradient_blocks = trade(gradient_blocks)
    for mask in place.depth_masks:
        small = small + exchange(small, "row", mask)
    sums = [add_all(pieces, place) for pieces in (attn_pieces, hidden_pieces, output_pieces)]
    gradient_blocks, hidden_first_pieces, attn_total, small, sums = together(
        gradient_blocks, hidden_first_pieces, attn_total, small, sums
    )
    attn_first_pieces = over_depth(attn_total, place)
    tokens_gradient = assembled(gradient_blocks, jnp.float32)
    tokens_gradient = tokens_gradient.reshape(clip_count, frame_part, places, col_width)
    first_sums = [
        add_all(pieces, place)
        for pieces in (attn_first_pieces, hidden_first_pieces, output_first_pieces)
    ]
    modgrad = small[: cut * clip_count].reshape(clip_count, layer_count, 6, col_width)
    modgrad = jnp.moveaxis(jnp.stack(relative(modgrad, place)), 1, 0)
    rest = small[cut * clip_count :]
    bias_grads = []
    for value in (attn_bias, hidden_bias, mixing_bias, output_bias):
        bias_grads.append(rest[: value.size].reshape(value.shape))
        rest = rest[value.size :]
    ada_bias_grad = jnp.sum(modgrad, 1)
    ada_weight_grad = jnp.einsum(
        "cr,lcsk->lrsk", cond_act.astype(jnp.float32), modgrad, precision=highest
    )
    cond_part = jnp.einsum(
        "lcsk,lrsk->cr", modgrad, ada_weight.astype(jnp.float32), precision=highest
    )
    for mask in (1, 2):
        cond_part = cond_part + exchange(cond_part, "col", mask)
    conditioning_gradient = jax.vjp(jax.nn.silu, conditioning)[1](cond_part)[0]

    attn_sums, hidden_sums, output_sums = (
        jnp.stack((first_sums[index], sums[index])) for index in range(3)
    )
    return (
        result,
        close_tokens(tokens_gradient),
        conditioning_gradient,
        close_weight(ada_weight_grad),
        ada_bias_grad,
        close_weight(attn_sums[:, :, : 3 * col_width]),
        bias_grads[0],
        close_weight(jnp.swapaxes(attn_sums[:, :, 3 * col_width :], 1, 2)),
        bias_grads[2],
        close_weight(hidden_sums),
        bias_grads[1],
        close_weight(jnp.swapaxes(output_sums, 1, 2)),
        bias_grads[3],
    )


def suits_tokens(mesh):
    rows, cols = (mesh.shape["row"], mesh.shape["col"])
    return cols == 4 and rows >= 2 and rows & (rows - 1) == 0


def solution(mesh):
    placed = (
        P(None, "row", "col", None),
        P(None, "row"),
        P(None, "row", "col", None),
        P(None, None, "col"),
        P(None, "row", "col", None),
        P(None, None, "col"),
        P(None, "col", "row", None),
        P(None, "col"),
        P(None, "row", "col", None),
        P(None, "col"),
        P(None, "col", "row", None),
        P(None, "col"),
        P(None, None, "col", "row"),
    )
    return jax.shard_map(
        token_parallel if suits_tokens(mesh) else tensor_parallel,
        mesh=mesh,
        in_specs=placed,
        out_specs=(
            P(None, None, "col", "row"),
            P(None, "row", "col", None),
            P(None, "row"),
            P(None, "row", "col", None),
            P(None, None, "col"),
            P(None, "row", "col", None),
            P(None, None, "col"),
            P(None, "col", "row", None),
            P(None, "col"),
            P(None, "row", "col", None),
            P(None, "col"),
            P(None, "col", "row", None),
            P(None, "col"),
        ),
        check_vma=False,
    )
```

```python
import functools

import jax
import jax.numpy as jnp
from jax import lax
from jax.experimental import pallas as pl
from jax.experimental.pallas import tpu as pltpu
from jax.sharding import PartitionSpec as P

HEAD_DIM = 72


epsilon = 1e-06
highest = lax.Precision.HIGHEST
spatial_forms = ("caqhe,cakhe->cahqk", "cahqk,cakhe->caqhe", "cahqk,caqhe->cakhe")
temporal_forms = ("cqbhe,ckbhe->cbhqk", "cbhqk,ckbhe->cqbhe", "cbhqk,cqbhe->ckbhe")


def matmul(pattern, left, right):
    return jnp.einsum(pattern, left, right, preferred_element_type=jnp.float32)


def split_heads(values):
    return values.reshape(values.shape[:-1] + (values.shape[-1] // HEAD_DIM, HEAD_DIM))


def merge_heads(values):
    return values.reshape(values.shape[:-2] + (values.shape[-2] * values.shape[-1],))


def gelu_tanh(values):
    return jax.nn.gelu(values, approximate=True)


def open_tokens(blocked, width):
    return blocked.reshape(blocked.shape[0], blocked.shape[1], blocked.shape[3] // width, width)


def close_tokens(plain_layout):
    return plain_layout.reshape(
        plain_layout.shape[0],
        plain_layout.shape[1],
        1,
        plain_layout.shape[2] * plain_layout.shape[3],
    )


def close_weight(plain_layout):
    return plain_layout.reshape(plain_layout.shape[0], 1, 1, -1)


def normalize(stream):
    feature_count = stream.shape[-1] * lax.axis_size("col")
    row_total, squares = lax.psum((jnp.sum(stream, -1), jnp.sum(stream * stream, -1)), "col")
    average = row_total / feature_count
    variance = squares / feature_count - average * average
    inverse = lax.rsqrt(variance + epsilon)
    return ((stream - average[..., None]) * inverse[..., None], inverse)


def normalize_back(grad_normed, normed, inverse):
    feature_count = grad_normed.shape[-1] * lax.axis_size("col")
    first, second = lax.psum((jnp.sum(grad_normed, -1), jnp.sum(grad_normed * normed, -1)), "col")
    return inverse[..., None] * (
        grad_normed - first[..., None] / feature_count - normed * second[..., None] / feature_count
    )


def spread(values):
    return lax.all_gather(values, "col", axis=3, tiled=True)


def collect(terms):
    return lax.psum_scatter(
        terms.astype(jnp.bfloat16), "col", scatter_dimension=3, tiled=True
    ).astype(jnp.float32)


def spread_grad(values):
    return lax.all_gather(values, "col", axis=3, tiled=True)


def collect_grad(terms):
    return lax.psum_scatter(
        terms.astype(jnp.bfloat16), "col", scatter_dimension=3, tiled=True
    ).astype(jnp.float32)


def fetch_weights(qkv_weight, mixing_weight, hidden_weight, output_weight, depth):
    return (
        lax.all_gather(qkv_weight[depth], "row", axis=0, tiled=True),
        lax.all_gather(mixing_weight[depth], "row", axis=1, tiled=True),
        lax.all_gather(hidden_weight[depth], "row", axis=0, tiled=True),
        lax.all_gather(output_weight[depth], "row", axis=1, tiled=True),
    )


def attend(queries, key_rows, value_rows, forms):
    softmax_scale = HEAD_DIM ** (-0.5)
    scores = matmul(forms[0], split_heads(queries), split_heads(key_rows)) * softmax_scale
    largest = jnp.max(scores, -1, keepdims=True)
    weights = jnp.exp(scores - largest)
    totals = jnp.sum(weights, -1, keepdims=True)
    probs = (weights / totals).astype(jnp.bfloat16)
    mixed = matmul(forms[1], probs, split_heads(value_rows))
    return (merge_heads(mixed).astype(jnp.bfloat16), largest + jnp.log(totals))


def attend_back(queries, key_rows, value_rows, grad_heads, log_totals, forms):
    softmax_scale = HEAD_DIM ** (-0.5)
    query_split = split_heads(queries)
    key_split = split_heads(key_rows)
    value_split = split_heads(value_rows)
    grad_split = split_heads(grad_heads)
    scores = matmul(forms[0], query_split, key_split) * softmax_scale
    probs = jnp.exp(scores - log_totals)
    grad_values = matmul(forms[2], probs.astype(jnp.bfloat16), grad_split)
    grad_probs = matmul(forms[0], grad_split, value_split)
    row_delta = jnp.sum(probs * grad_probs, -1, keepdims=True)
    grad_scores = (probs * (grad_probs - row_delta)).astype(jnp.bfloat16)
    grad_queries = matmul(forms[1], grad_scores, key_split) * softmax_scale
    grad_keys = matmul(forms[2], grad_scores, query_split) * softmax_scale
    return tuple(
        (
            merge_heads(part_grad).astype(jnp.bfloat16)
            for part_grad in (grad_queries, grad_keys, grad_values)
        )
    )


def residual_forward(stream, modulation, weights, biases, forms):
    qkv_full, mixing_full, hidden_full, output_full = weights
    attn_add, mixing_add, hidden_add, output_add = biases

    def piece_of(column):
        return modulation[:, column][:, None, None, :]

    normed_attn, inv_attn = normalize(stream)
    input_attn = spread((normed_attn * (1.0 + piece_of(1)) + piece_of(0)).astype(jnp.bfloat16))
    qkv_rows = matmul("cabd,dsk->cabsk", input_attn, qkv_full)
    queries = (qkv_rows[..., 0, :] + attn_add[0]).astype(jnp.bfloat16)
    key_rows = qkv_rows[..., 1, :].astype(jnp.bfloat16)
    value_rows = (qkv_rows[..., 2, :] + attn_add[1]).astype(jnp.bfloat16)
    heads_out, log_totals = attend(queries, key_rows, value_rows, forms)
    attn_out = collect(matmul("cabk,kd->cabd", heads_out, mixing_full)) + mixing_add
    stream_mid = stream + piece_of(2) * attn_out
    normed_mlp, inv_mlp = normalize(stream_mid)
    input_mlp = spread((normed_mlp * (1.0 + piece_of(4)) + piece_of(3)).astype(jnp.bfloat16))
    pre_gelu = matmul("cabd,df->cabf", input_mlp, hidden_full) + hidden_add
    activated = gelu_tanh(pre_gelu).astype(jnp.bfloat16)
    mlp_out = collect(matmul("cabf,fd->cabd", activated, output_full)) + output_add
    stream_out = stream_mid + piece_of(5) * mlp_out
    saved = (
        normed_attn,
        inv_attn,
        input_attn,
        queries,
        key_rows,
        value_rows,
        heads_out,
        log_totals,
        attn_out,
        normed_mlp,
        inv_mlp,
        input_mlp,
        pre_gelu,
        activated,
        mlp_out,
    )
    return (stream_out, saved)


def residual_backward(grad_stream, saved, modulation, weights, forms):
    (
        normed_attn,
        inv_attn,
        input_attn,
        queries,
        key_rows,
        value_rows,
        heads_out,
        log_totals,
        attn_out,
        normed_mlp,
        inv_mlp,
        input_mlp,
        pre_gelu,
        activated,
        mlp_out,
    ) = saved
    qkv_full, mixing_full, hidden_full, output_full = weights

    def piece_of(column):
        return modulation[:, column][:, None, None, :]

    grad_mlp = (grad_stream * piece_of(5)).astype(jnp.bfloat16)
    gate_mlp_grad = jnp.sum(grad_stream * mlp_out, (1, 2))
    grad_mlp_all = spread_grad(grad_mlp)
    output_weight_term = matmul("cabf,cabd->fd", activated, grad_mlp_all)
    grad_act = matmul("cabd,fd->cabf", grad_mlp_all, output_full)
    grad_pre = jax.vjp(gelu_tanh, pre_gelu)[1](grad_act)[0].astype(jnp.bfloat16)
    hidden_weight_term = matmul("cabd,cabf->df", input_mlp, grad_pre)
    grad_input_mlp = collect_grad(matmul("cabf,df->cabd", grad_pre, hidden_full))
    shift_mlp_grad = jnp.sum(grad_input_mlp, (1, 2))
    scale_mlp_grad = jnp.sum(grad_input_mlp * normed_mlp, (1, 2))
    grad_mid = grad_stream + normalize_back(
        grad_input_mlp * (1.0 + piece_of(4)), normed_mlp, inv_mlp
    )
    grad_attn = (grad_mid * piece_of(2)).astype(jnp.bfloat16)
    gate_attn_grad = jnp.sum(grad_mid * attn_out, (1, 2))
    grad_attn_all = spread_grad(grad_attn)
    mixing_weight_term = matmul("cabk,cabd->kd", heads_out, grad_attn_all)
    grad_heads = matmul("cabd,kd->cabk", grad_attn_all, mixing_full).astype(jnp.bfloat16)
    grad_queries, grad_keys, grad_values = attend_back(
        queries, key_rows, value_rows, grad_heads, log_totals, forms
    )
    grad_qkv = jnp.stack((grad_queries, grad_keys, grad_values), 3)
    qkv_weight_term = matmul("cabd,cabsk->dsk", input_attn, grad_qkv)
    grad_input_attn = collect_grad(matmul("cabsk,dsk->cabd", grad_qkv, qkv_full))
    shift_attn_grad = jnp.sum(grad_input_attn, (1, 2))
    scale_attn_grad = jnp.sum(grad_input_attn * normed_attn, (1, 2))
    grad_input = grad_mid + normalize_back(
        grad_input_attn * (1.0 + piece_of(1)), normed_attn, inv_attn
    )
    weight_terms = (
        lax.psum_scatter(
            qkv_weight_term.astype(jnp.bfloat16), "row", scatter_dimension=0, tiled=True
        ).astype(jnp.float32),
        lax.psum_scatter(
            mixing_weight_term.astype(jnp.bfloat16), "row", scatter_dimension=1, tiled=True
        ).astype(jnp.float32),
        lax.psum_scatter(
            hidden_weight_term.astype(jnp.bfloat16), "row", scatter_dimension=0, tiled=True
        ).astype(jnp.float32),
        lax.psum_scatter(
            output_weight_term.astype(jnp.bfloat16), "row", scatter_dimension=1, tiled=True
        ).astype(jnp.float32),
    )
    modulation_grad = jnp.stack(
        (
            shift_attn_grad,
            scale_attn_grad,
            gate_attn_grad,
            shift_mlp_grad,
            scale_mlp_grad,
            gate_mlp_grad,
        ),
        1,
    )
    attn_bias_term = jnp.stack(
        (
            jnp.sum(grad_queries.astype(jnp.float32), (0, 1, 2)),
            jnp.sum(grad_values.astype(jnp.float32), (0, 1, 2)),
        )
    )
    bias_terms = (
        attn_bias_term,
        jnp.sum(grad_attn.astype(jnp.float32), (0, 1, 2)),
        jnp.sum(grad_pre.astype(jnp.float32), (0, 1, 2)),
        jnp.sum(grad_mlp.astype(jnp.float32), (0, 1, 2)),
    )
    return (grad_input, weight_terms, modulation_grad, bias_terms)


def tensor_parallel(
    tokens,
    conditioning,
    ada_weight,
    ada_bias,
    qkv_weight,
    attn_bias,
    mixing_weight,
    mixing_bias,
    hidden_weight,
    hidden_bias,
    output_weight,
    output_bias,
    cotangent,
):
    col_width = ada_bias.shape[2]
    row_width = conditioning.shape[1]
    hidden_width = hidden_bias.shape[1]
    layer_count = ada_bias.shape[0]
    ada_weight = ada_weight.reshape(layer_count, row_width, 6, col_width)
    qkv_weight = qkv_weight.reshape(layer_count, row_width, 3, col_width)
    mixing_weight = mixing_weight.reshape(layer_count, col_width, row_width)
    hidden_weight = hidden_weight.reshape(layer_count, row_width, hidden_width)
    output_weight = output_weight.reshape(layer_count, hidden_width, row_width)
    tokens = open_tokens(tokens, col_width)
    cotangent = open_tokens(cotangent, col_width)
    cond_act = jax.nn.silu(conditioning).astype(jnp.bfloat16)
    modulation = lax.psum(
        (
            matmul("cr,rsk->csk", cond_act, ada_weight[0]),
            matmul("cr,rsk->csk", cond_act, ada_weight[1]),
        ),
        "row",
    )
    modulation = (modulation[0] + ada_bias[0][None], modulation[1] + ada_bias[1][None])

    def biases_of(depth):
        return (attn_bias[depth], mixing_bias[depth], hidden_bias[depth], output_bias[depth])

    stream_first = tokens.astype(jnp.float32)
    weights_first = fetch_weights(qkv_weight, mixing_weight, hidden_weight, output_weight, 0)
    output_first, saved_first = residual_forward(
        stream_first, modulation[0], weights_first, biases_of(0), spatial_forms
    )
    moved = lax.all_to_all(
        output_first.astype(jnp.bfloat16), "row", split_axis=2, concat_axis=1, tiled=True
    )
    stream_second = moved.astype(jnp.float32)
    weights_second = fetch_weights(qkv_weight, mixing_weight, hidden_weight, output_weight, 1)
    output_second, saved_second = residual_forward(
        stream_second, modulation[1], weights_second, biases_of(1), temporal_forms
    )
    result = output_second.astype(jnp.bfloat16)
    weights_second = fetch_weights(qkv_weight, mixing_weight, hidden_weight, output_weight, 1)
    saved_second = residual_forward(
        stream_second, modulation[1], weights_second, biases_of(1), temporal_forms
    )[1]
    grad_second, terms_second, modgrad_second, biasgrad_second = residual_backward(
        cotangent.astype(jnp.float32), saved_second, modulation[1], weights_second, temporal_forms
    )
    returned = lax.all_to_all(
        grad_second.astype(jnp.bfloat16), "row", split_axis=1, concat_axis=2, tiled=True
    )
    weights_first = fetch_weights(qkv_weight, mixing_weight, hidden_weight, output_weight, 0)
    saved_first = residual_forward(
        stream_first, modulation[0], weights_first, biases_of(0), spatial_forms
    )[1]
    grad_first, terms_first, modgrad_first, biasgrad_first = residual_backward(
        returned.astype(jnp.float32), saved_first, modulation[0], weights_first, spatial_forms
    )
    summed = (
        lax.psum(jnp.stack((modgrad_first, modgrad_second)).astype(jnp.bfloat16), "row").astype(
            jnp.float32
        ),
        lax.psum(
            jnp.stack((biasgrad_first[0], biasgrad_second[0])).astype(jnp.bfloat16), "row"
        ).astype(jnp.float32),
        lax.psum(
            jnp.stack((biasgrad_first[1], biasgrad_second[1])).astype(jnp.bfloat16), "row"
        ).astype(jnp.float32),
        lax.psum(
            jnp.stack((biasgrad_first[2], biasgrad_second[2])).astype(jnp.bfloat16), "row"
        ).astype(jnp.float32),
        lax.psum(
            jnp.stack((biasgrad_first[3], biasgrad_second[3])).astype(jnp.bfloat16), "row"
        ).astype(jnp.float32),
    )
    modulation_grad = summed[0]
    ada_bias_grad = jnp.sum(modulation_grad, 1)
    ada_weight_grad = jnp.einsum(
        "cr,lcsk->lrsk", cond_act.astype(jnp.float32), modulation_grad, precision=highest
    )
    cond_part = jnp.einsum(
        "lcsk,lrsk->cr", modulation_grad, ada_weight.astype(jnp.float32), precision=highest
    )
    cond_part = lax.psum(cond_part, "col")
    conditioning_gradient = jax.vjp(jax.nn.silu, conditioning)[1](cond_part)[0]
    qkv_weight_grad = jnp.stack((terms_first[0], terms_second[0]))
    mixing_weight_grad = jnp.stack((terms_first[1], terms_second[1]))
    hidden_weight_grad = jnp.stack((terms_first[2], terms_second[2]))
    output_weight_grad = jnp.stack((terms_first[3], terms_second[3]))
    return (
        close_tokens(result),
        close_tokens(grad_first),
        conditioning_gradient,
        close_weight(ada_weight_grad),
        ada_bias_grad,
        close_weight(qkv_weight_grad),
        summed[1],
        close_weight(mixing_weight_grad),
        summed[2],
        close_weight(hidden_weight_grad),
        summed[3],
        close_weight(output_weight_grad),
        summed[4],
    )


def exchange(values, axis, mask):
    count = lax.axis_size(axis)
    return lax.ppermute(values, axis, [(index, index ^ mask) for index in range(count)])


def add_low(first, second):
    return (first.astype(jnp.float32) + second.astype(jnp.float32)).astype(jnp.bfloat16)


def after(values, *others):
    return lax.optimization_barrier((values,) + others)[0]


def together(*values):
    return lax.optimization_barrier(values)


def over_depth(values, place):
    groups = [list(range(core, place.row_count, 2)) for core in range(2)]
    return lax.all_to_all(
        values, "row", split_axis=0, concat_axis=0, tiled=True, axis_index_groups=groups
    )


def swap(values):
    return exchange(values, "row", 1)


class Gathering:
    def __init__(self, place):
        self.place = place
        self.held = ()
        self.plane = ()
        self.corner = ()
        self.sent = ()
        self.done = []

    def step(self, shard, *gates):
        groups = (self.held, self.plane, self.corner)
        values = list(together(*[value for group in groups for value in group], *gates))
        held, plane, corner = [[values.pop(0) for _ in group] for group in groups]
        across, above = ([], [])
        if held:
            across.append(held[0])
            above.append(held[0])
        if plane:
            size = plane[0].shape[0]
            across.append(plane[2][size // 2 : size])
            above.append(plane[1][: size // 2])
        across = [jnp.concatenate(across, 0)] if across else []
        above = [jnp.concatenate(above, 0)] if above else []
        self.sent = tuple(across + above)
        self.held = ()
        if shard is not None:
            self.held = (over_depth(after(shard, *self.sent), self.place),)
        if corner:
            own = pack_blocks(after(corner, *self.sent))
            self.done.append((own, swap(own)))
        met = tuple(
            exchange(value[0], "col", mask) for mask, value in ((1, across), (2, above)) if value
        )
        self.corner = tuple(plane) + met if plane else ()
        self.plane = tuple(held) + met if held else ()


def scatter_corner(blocks):
    held, across_upper, across_first, above_first, above_lower = blocks
    return (
        held,
        across_upper,
        exchange(across_first, "col", 1),
        exchange(above_first, "col", 2),
        above_lower,
    )


def scatter_sides(blocks):
    held, across_upper, across_first, above_first, above_lower = blocks
    half = across_upper.shape[0]
    return (
        add_low(across_upper, above_first[half:]),
        add_low(above_lower, across_first[half:]),
    )


def scatter_plane(blocks, sides):
    held, _, across_first, above_first, _ = blocks
    across, above = sides
    return (held, exchange(across, "col", 1), across_first, above_first, exchange(above, "col", 2))


def add_all(pieces, place):
    count = place.row_count // 2
    pieces = pieces.reshape((count, -1) + pieces.shape[1:])
    return jnp.sum(pieces.astype(jnp.float32), 0)


class Place:
    def __init__(self):
        self.row = lax.axis_index("row")
        self.col = lax.axis_index("col")
        self.row_count = lax.axis_size("row")
        self.col_count = lax.axis_size("col")
        self.core = self.row & 1
        self.depth_masks = []
        mask = 2
        while mask < self.row_count:
            self.depth_masks.append(mask)
            mask *= 2


def mine_first(halves, place, axis):
    return jnp.where(place.core == 1, jnp.flip(halves, axis), halves)


def to_halves(features, place):
    width = features.shape[-1]
    lead = features.shape[:-1]
    split_up = features.reshape(lead + (place.row_count // 2, 2, width // place.row_count))
    halves = jnp.swapaxes(split_up, -3, -2).reshape(lead + (2, width // 2))
    return mine_first(halves, place, len(lead))


def from_halves(halves, place):
    lead = halves.shape[:-2]
    half = halves.shape[-1]
    halves = mine_first(halves, place, len(lead))
    split_up = halves.reshape(lead + (2, place.row_count // 2, half // (place.row_count // 2)))
    return jnp.swapaxes(split_up, -3, -2).reshape(lead + (2 * half,))


def relative(stacked, place):
    return [
        lax.dynamic_index_in_dim(stacked, place.col ^ step, 0, keepdims=False)
        for step in range(place.col_count)
    ]


def absolute(blocks, place):
    return jnp.stack(relative(jnp.stack(blocks), place))


def trade(blocks):
    return [
        block if step == 0 else exchange(block, "col", step) for step, block in enumerate(blocks)
    ]


PLAIN = ((1,), (0,))
TURNED = ((1,), (1,))
SUMMED = ((0,), (0,))
VMEM_BYTES = 58 * 1024 * 1024
LANES = 128
IN_HBM = pl.BlockSpec(memory_space=pl.ANY)
SMALL_COST = pl.CostEstimate(flops=0, bytes_accessed=0, transcendentals=0)


def dot(left, right, dims):
    return lax.dot_general(left, right, (dims, ((), ())), preferred_element_type=jnp.float32)


def round_up(value):
    return -(-value // LANES) * LANES


def whole(shape):
    return pl.BlockSpec(shape, lambda step: (0,) * len(shape))


def stepped(shape):
    return pl.BlockSpec((1,) + shape, lambda step: (step,) + (0,) * len(shape))


def of(shape, dtype):
    return jax.ShapeDtypeStruct(shape, dtype)


def norm_parts(stream_ref):
    first, second = (stream_ref[0], stream_ref[1])
    count = 2 * first.shape[1]
    average = (jnp.sum(first, 1, keepdims=True) + jnp.sum(second, 1, keepdims=True)) / count
    first, second = (first - average, second - average)
    variance = (
        jnp.sum(first * first, 1, keepdims=True) + jnp.sum(second * second, 1, keepdims=True)
    ) / count
    inverse = lax.rsqrt(variance + epsilon)
    return (first * inverse, second * inverse, inverse)


def norm_grads(stream_ref, acc, mod_ref, scale_row, grad_ref, out_ref, small_ref):
    normed = norm_parts(stream_ref)
    inverse = normed[2]
    count = 2 * normed[0].shape[1]
    weighted = []
    for half in range(2):
        grad_input = acc[half]
        small_ref[half, 0:1, :] = jnp.sum(grad_input, 0, keepdims=True)
        small_ref[half, 1:2, :] = jnp.sum(grad_input * normed[half], 0, keepdims=True)
        weighted.append(grad_input * (1.0 + mod_ref[half, scale_row : scale_row + 1, :]))
    first = sum(jnp.sum(value, 1, keepdims=True) for value in weighted) / count
    second = (
        sum(jnp.sum(value * normed[half], 1, keepdims=True) for half, value in enumerate(weighted))
        / count
    )
    for half in range(2):
        out_ref[half] = grad_ref[half] + inverse * (
            weighted[half] - first - normed[half] * second
        )


def same_place(size, period):
    row = lax.broadcasted_iota(jnp.int32, (size, size), 0)
    column = lax.broadcasted_iota(jnp.int32, (size, size), 1)
    return (row % period) == (column % period)


def attention_kernel(size, period, steps, *refs):
    stream_ref, mod_ref, bias_ref, added_ref = refs[:4]
    weights = refs[4:6]
    mid_ref, mine_ref, other_ref, qkv_ref, heads_ref, log_ref, out_ref, acc, kept_ref = refs[6:]
    input_refs = (mine_ref, kept_ref)
    step = pl.program_id(0)
    tokens = stream_ref.shape[1]
    used = qkv_ref.shape[2]
    padded = heads_ref.shape[2]
    columns = weights[0].shape[2]
    width = columns // 4
    count = width // HEAD_DIM
    scale = HEAD_DIM ** (-0.5)

    @pl.when(step == 0)
    def _():
        normed = norm_parts(stream_ref)
        for half in range(2):
            input_refs[half][...] = (
                normed[half] * (1.0 + mod_ref[half, 1:2, :]) + mod_ref[half, 0:1, :]
            ).astype(jnp.bfloat16)
        other_ref[...] = kept_ref[...].T
        acc[...] = jnp.zeros_like(acc)

    rows = dot(input_refs[0][...], weights[0][0, :, :used], PLAIN)
    rows = rows + dot(input_refs[1][...], weights[1][0, :, :used], PLAIN) + bias_ref[0]
    lane = lax.broadcasted_iota(jnp.int32, rows.shape, 1)
    qkv_ref[0] = jnp.where(lane < 3 * width, rows, 0.0).astype(jnp.bfloat16)
    log_lane = lax.broadcasted_iota(jnp.int32, (size, LANES), 1)
    for group in range(tokens // size):
        block = qkv_ref[0, group * size : (group + 1) * size, :]
        outs = [jnp.zeros((size, padded - width), jnp.float32)]
        logs = jnp.zeros((size, LANES), jnp.float32)
        for head in range(count):
            start = head * HEAD_DIM
            query = block[:, start : start + HEAD_DIM]
            key = block[:, width + start : width + start + HEAD_DIM]
            value = block[:, 2 * width + start : 2 * width + start + HEAD_DIM]
            scores = dot(query, key, TURNED) * scale
            if period:
                scores = jnp.where(same_place(size, period), scores, -1e30)
            largest = jnp.max(scores, 1, keepdims=True)
            weight = jnp.exp(scores - largest)
            total = jnp.sum(weight, 1, keepdims=True)
            probs = (weight * (1.0 / total)).astype(jnp.bfloat16)
            outs.append(dot(probs, value, PLAIN))
            logs = jnp.where(log_lane == head, largest + jnp.log(total), logs)
        heads_ref[0, group * size : (group + 1) * size, :] = jnp.concatenate(outs, 1).astype(
            jnp.bfloat16
        )
        log_ref[0, group * size : (group + 1) * size, :] = logs
    for half in range(2):
        acc[half] += dot(heads_ref[0], weights[half][0, :, columns - padded :], TURNED)

    @pl.when(step == steps - 1)
    def _():
        for half in range(2):
            total = acc[half] + added_ref[half]
            out_ref[half] = total.astype(jnp.bfloat16)
            mid_ref[half] = stream_ref[half] + mod_ref[half, 2:3, :] * total


def attention_forward(stream, modulation, weights, bias, added, size, period):
    steps = weights[0].shape[0]
    _, tokens, half = stream.shape
    columns = weights[0].shape[2]
    used = round_up(3 * columns // 4)
    padded = columns - (3 * columns // 4) // LANES * LANES
    bf16, f32 = (jnp.bfloat16, jnp.float32)
    return pl.pallas_call(
        functools.partial(attention_kernel, size, period, steps),
        grid=(steps,),
        in_specs=[
            whole(stream.shape),
            whole(modulation.shape),
            stepped((1, used)),
            whole(added.shape),
        ]
        + [stepped((half, columns))] * 2,
        out_specs=[
            whole(stream.shape),
            whole((tokens, half)),
            whole((half, tokens)),
            stepped((tokens, used)),
            stepped((tokens, padded)),
            stepped((tokens, LANES)),
            whole(stream.shape),
        ],
        out_shape=[
            of(stream.shape, f32),
            of((tokens, half), bf16),
            of((half, tokens), bf16),
            of((steps, tokens, used), bf16),
            of((steps, tokens, padded), bf16),
            of((steps, tokens, LANES), f32),
            of(stream.shape, bf16),
        ],
        scratch_shapes=[
            pltpu.VMEM(stream.shape, f32),
            pltpu.VMEM((tokens, half), bf16),
        ],
        compiler_params=pltpu.CompilerParams(vmem_limit_bytes=VMEM_BYTES),
        cost_estimate=SMALL_COST,
        name="attention_forward",
    )(stream, modulation, bias, added, *weights)


def mlp_kernel(steps, *refs):
    mid_ref, mod_ref, bias_ref, added_ref = refs[:4]
    hidden, output = (refs[4:6], refs[6:8])
    stream_ref, mine_ref, other_ref, active_ref, slope_ref, out_ref, acc, kept_ref = refs[8:]
    input_refs = (mine_ref, kept_ref)
    step = pl.program_id(0)

    @pl.when(step == 0)
    def _():
        normed = norm_parts(mid_ref)
        for half in range(2):
            input_refs[half][...] = (
                normed[half] * (1.0 + mod_ref[half, 4:5, :]) + mod_ref[half, 3:4, :]
            ).astype(jnp.bfloat16)
        other_ref[...] = kept_ref[...].T
        acc[...] = jnp.zeros_like(acc)

    pre = dot(input_refs[0][...], hidden[0][0], PLAIN)
    pre = pre + dot(input_refs[1][...], hidden[1][0], PLAIN) + bias_ref[0]
    root = (2.0 / jnp.pi) ** 0.5
    square = pre * pre
    bend = jnp.tanh(pre * (root + root * 0.044715 * square))
    active_ref[0] = (0.5 * pre * (1.0 + bend)).astype(jnp.bfloat16)
    slope_ref[0] = (
        0.5 * (1.0 + bend)
        + 0.5 * pre * (1.0 - bend * bend) * (root + 3.0 * root * 0.044715 * square)
    ).astype(jnp.bfloat16)
    for half in range(2):
        acc[half] += dot(active_ref[0], output[half][0], TURNED)

    @pl.when(step == steps - 1)
    def _():
        for half in range(2):
            total = acc[half] + added_ref[half]
            out_ref[half] = total.astype(jnp.bfloat16)
            stream_ref[half] = mid_ref[half] + mod_ref[half, 5:6, :] * total


def mlp_forward(mid, modulation, hidden, output, bias, added):
    steps = hidden[0].shape[0]
    _, tokens, half = mid.shape
    columns = hidden[0].shape[2]
    bf16, f32 = (jnp.bfloat16, jnp.float32)
    return pl.pallas_call(
        functools.partial(mlp_kernel, steps),
        grid=(steps,),
        in_specs=[
            whole(mid.shape),
            whole(modulation.shape),
            stepped((1, columns)),
            whole(added.shape),
        ]
        + [stepped((half, columns))] * 4,
        out_specs=[
            whole(mid.shape),
            whole((tokens, half)),
            whole((half, tokens)),
            stepped((tokens, columns)),
            stepped((tokens, columns)),
            whole(mid.shape),
        ],
        out_shape=[
            of(mid.shape, f32),
            of((tokens, half), bf16),
            of((half, tokens), bf16),
            of((steps, tokens, columns), bf16),
            of((steps, tokens, columns), bf16),
            of(mid.shape, bf16),
        ],
        scratch_shapes=[
            pltpu.VMEM(mid.shape, f32),
            pltpu.VMEM((tokens, half), bf16),
        ],
        compiler_params=pltpu.CompilerParams(vmem_limit_bytes=VMEM_BYTES),
        cost_estimate=SMALL_COST,
        name="mlp_forward",
    )(mid, modulation, bias, added, *hidden, *output)


def mlp_back_kernel(steps, *refs):
    grad_ref, mid_ref, out_ref, slope_ref, mod_ref = refs[:5]
    hidden, output = (refs[5:7], refs[7:9])
    grad_mid_ref, mine_ref, other_ref, grad_pre_ref, small_ref, sum_ref, acc, kept_ref = refs[9:]
    grad_mlp_refs = (mine_ref, kept_ref)
    step = pl.program_id(0)

    @pl.when(step == 0)
    def _():
        for half in range(2):
            grad = grad_ref[half]
            scaled = (grad * mod_ref[half, 5:6, :]).astype(jnp.bfloat16)
            grad_mlp_refs[half][...] = scaled
            small_ref[half, 2:3, :] = jnp.sum(
                grad * out_ref[half].astype(jnp.float32), 0, keepdims=True
            )
            small_ref[half, 3:4, :] = jnp.sum(scaled.astype(jnp.float32), 0, keepdims=True)
        other_ref[...] = kept_ref[...].T
        acc[...] = jnp.zeros_like(acc)

    grad_act = dot(grad_mlp_refs[0][...], output[0][0], PLAIN)
    grad_act = grad_act + dot(grad_mlp_refs[1][...], output[1][0], PLAIN)
    grad_pre = (grad_act * slope_ref[0].astype(jnp.float32)).astype(jnp.bfloat16)
    grad_pre_ref[0] = grad_pre
    sum_ref[0] = jnp.sum(grad_pre.astype(jnp.float32), 0, keepdims=True)
    for half in range(2):
        acc[half] += dot(grad_pre, hidden[half][0], TURNED)

    @pl.when(step == steps - 1)
    def _():
        norm_grads(mid_ref, acc, mod_ref, 4, grad_ref, grad_mid_ref, small_ref)


def mlp_backward(grad, mid, out, slope, modulation, hidden, output):
    steps = hidden[0].shape[0]
    _, tokens, half = mid.shape
    columns = hidden[0].shape[2]
    bf16, f32 = (jnp.bfloat16, jnp.float32)
    return pl.pallas_call(
        functools.partial(mlp_back_kernel, steps),
        grid=(steps,),
        in_specs=[
            whole(mid.shape),
            whole(mid.shape),
            whole(mid.shape),
            stepped((tokens, columns)),
            whole(modulation.shape),
        ]
        + [stepped((half, columns))] * 4,
        out_specs=[
            whole(mid.shape),
            whole((tokens, half)),
            whole((half, tokens)),
            stepped((tokens, columns)),
            whole((2, 8, half)),
            stepped((1, columns)),
        ],
        out_shape=[
            of(mid.shape, f32),
            of((tokens, half), bf16),
            of((half, tokens), bf16),
            of((steps, tokens, columns), bf16),
            of((2, 8, half), f32),
            of((steps, 1, columns), f32),
        ],
        scratch_shapes=[
            pltpu.VMEM(mid.shape, f32),
            pltpu.VMEM((tokens, half), bf16),
        ],
        compiler_params=pltpu.CompilerParams(vmem_limit_bytes=VMEM_BYTES),
        cost_estimate=SMALL_COST,
        name="mlp_backward",
    )(grad, mid, out, slope, modulation, *hidden, *output)


def attention_back_kernel(size, period, steps, *refs):
    grad_ref, stream_ref, out_ref, qkv_ref, log_ref, mod_ref = refs[:6]
    weights = refs[6:8]
    grad_in_ref, mine_ref, other_ref, grad_qkv_ref, small_ref, sum_ref, acc, kept_ref = refs[8:]
    grad_attn_refs = (mine_ref, kept_ref)
    step = pl.program_id(0)
    tokens = stream_ref.shape[1]
    used = qkv_ref.shape[2]
    columns = weights[0].shape[2]
    width = columns // 4
    padded = columns - (3 * width) // LANES * LANES
    count = width // HEAD_DIM
    scale = HEAD_DIM ** (-0.5)

    @pl.when(step == 0)
    def _():
        for half in range(2):
            grad = grad_ref[half]
            scaled = (grad * mod_ref[half, 2:3, :]).astype(jnp.bfloat16)
            grad_attn_refs[half][...] = scaled
            small_ref[half, 2:3, :] = jnp.sum(
                grad * out_ref[half].astype(jnp.float32), 0, keepdims=True
            )
            small_ref[half, 3:4, :] = jnp.sum(scaled.astype(jnp.float32), 0, keepdims=True)
        other_ref[...] = kept_ref[...].T
        acc[...] = jnp.zeros_like(acc)

    grad_heads = dot(grad_attn_refs[0][...], weights[0][0, :, columns - padded :], PLAIN)
    grad_heads = grad_heads + dot(grad_attn_refs[1][...], weights[1][0, :, columns - padded :], PLAIN)
    grad_heads = grad_heads.astype(jnp.bfloat16)
    total = jnp.zeros((1, used), jnp.float32)
    for group in range(tokens // size):
        rows = slice(group * size, (group + 1) * size)
        block = qkv_ref[0, rows, :]
        logs = log_ref[0, rows, :]
        grad_queries, grad_keys, grad_values = ([], [], [])
        for head in range(count):
            start = head * HEAD_DIM
            query = block[:, start : start + HEAD_DIM]
            key = block[:, width + start : width + start + HEAD_DIM]
            value = block[:, 2 * width + start : 2 * width + start + HEAD_DIM]
            start = padded - width + head * HEAD_DIM
            grad_out = grad_heads[rows, start : start + HEAD_DIM]
            scores = dot(query, key, TURNED) * scale - logs[:, head : head + 1]
            if period:
                scores = jnp.where(same_place(size, period), scores, -1e30)
            probs = jnp.exp(scores)
            grad_probs = dot(grad_out, value, TURNED)
            delta = jnp.sum(probs * grad_probs, 1, keepdims=True)
            grad_scores = (probs * (grad_probs - delta)).astype(jnp.bfloat16)
            grad_values.append(dot(probs.astype(jnp.bfloat16), grad_out, SUMMED))
            grad_queries.append(dot(grad_scores, key, PLAIN) * scale)
            grad_keys.append(dot(grad_scores, query, SUMMED) * scale)
        rest = [jnp.zeros((size, used - 3 * width), jnp.float32)]
        joined = jnp.concatenate(grad_queries + grad_keys + grad_values + rest, 1)
        joined = joined.astype(jnp.bfloat16)
        grad_qkv_ref[0, rows, :] = joined
        total = total + jnp.sum(joined.astype(jnp.float32), 0, keepdims=True)
    sum_ref[0] = total
    for half in range(2):
        acc[half] += dot(grad_qkv_ref[0], weights[half][0, :, :used], TURNED)

    @pl.when(step == steps - 1)
    def _():
        norm_grads(stream_ref, acc, mod_ref, 1, grad_ref, grad_in_ref, small_ref)


def attention_backward(grad, stream, out, qkv, logs, modulation, weights, size, period):
    steps = weights[0].shape[0]
    _, tokens, half = stream.shape
    columns = weights[0].shape[2]
    used = qkv.shape[2]
    bf16, f32 = (jnp.bfloat16, jnp.float32)
    return pl.pallas_call(
        functools.partial(attention_back_kernel, size, period, steps),
        grid=(steps,),
        in_specs=[
            whole(stream.shape),
            whole(stream.shape),
            whole(stream.shape),
            stepped((tokens, used)),
            stepped((tokens, LANES)),
            whole(modulation.shape),
        ]
        + [stepped((half, columns))] * 2,
        out_specs=[
            whole(stream.shape),
            whole((tokens, half)),
            whole((half, tokens)),
            stepped((tokens, used)),
            whole((2, 8, half)),
            stepped((1, used)),
        ],
        out_shape=[
            of(stream.shape, f32),
            of((tokens, half), bf16),
            of((half, tokens), bf16),
            of((steps, tokens, used), bf16),
            of((2, 8, half), f32),
            of((steps, 1, used), f32),
        ],
        scratch_shapes=[
            pltpu.VMEM(stream.shape, f32),
            pltpu.VMEM((tokens, half), bf16),
        ],
        compiler_params=pltpu.CompilerParams(vmem_limit_bytes=VMEM_BYTES),
        cost_estimate=SMALL_COST,
        name="attention_backward",
    )(grad, stream, out, qkv, logs, modulation, *weights)


def weight_kernel(pairs, overlap, steps, *refs):
    inputs = refs[: 4 * pairs]
    outs = refs[4 * pairs : 4 * pairs + 5]
    turned = refs[4 * pairs + 5 : 5 * pairs + 5]
    buffer, sems = refs[5 * pairs + 5 :]
    step = pl.program_id(0)
    slot = step % 2
    for pair in range(pairs):
        mine = inputs[4 * pair]

        @pl.when(step == 0)
        def _():
            turned[pair][...] = mine[...].T

    @pl.when(step >= 2)
    def _():
        pltpu.make_async_copy(buffer.at[slot], outs[0], sems.at[slot]).wait()

    sums = []
    for pair in range(pairs):
        _, rows, mine, theirs = inputs[4 * pair : 4 * pair + 4]
        total = dot(turned[pair][...], mine[0], PLAIN)
        sums.append(total + dot(rows[...], theirs[0], PLAIN))
    if pairs == 1:
        buffer[slot] = sums[0].astype(jnp.bfloat16)
    else:
        first = sums[0].shape[1] - overlap
        buffer[slot, :, :first] = sums[0][:, :first].astype(jnp.bfloat16)
        buffer[slot, :, first : first + overlap] = (
            sums[0][:, first:] + sums[1][:, :overlap]
        ).astype(jnp.bfloat16)
        buffer[slot, :, first + overlap :] = sums[1][:, overlap:].astype(jnp.bfloat16)
    for index in range(steps):

        @pl.when(step == index)
        def _():
            source = buffer.at[index % 2]
            sem = sems.at[index % 2]
            if index == 0:
                pltpu.make_async_copy(source, outs[0], sem).start()
            else:
                rows = outs[1].shape[0]
                upper, lower = (
                    (outs[1], outs[2].at[:rows]),
                    (outs[3].at[:rows], outs[4]),
                    (outs[3].at[rows:], outs[2].at[rows:]),
                )[index - 1]
                pltpu.make_async_copy(source.at[:rows], upper, sem).start()
                pltpu.make_async_copy(source.at[rows:], lower, sem).start()

    @pl.when(step == steps - 1)
    def _():
        for index in range(2):
            pltpu.make_async_copy(buffer.at[index], outs[0], sems.at[index]).wait()


def weight_grads(columns, overlap, *pairs, flops=0):
    steps, tokens, _ = pairs[0][2].shape
    half = pairs[0][1].shape[0]
    bf16 = jnp.bfloat16
    specs, values, turned = ([], [], [])
    for mine, theirs, blocks, their_blocks in pairs:
        specs += [
            whole(mine.shape),
            whole(theirs.shape),
            stepped(blocks.shape[1:]),
            stepped(blocks.shape[1:]),
        ]
        values += [mine, theirs, blocks, their_blocks]
        turned.append(pltpu.VMEM((half, tokens), bf16))
    return pl.pallas_call(
        functools.partial(weight_kernel, len(pairs), overlap, steps),
        grid=(steps,),
        in_specs=specs,
        out_specs=[IN_HBM] * 5,
        out_shape=[
            of((rows, columns), bf16) for rows in (half, half // 2, half, half, half // 2)
        ],
        scratch_shapes=turned
        + [pltpu.VMEM((2, half, columns), bf16), pltpu.SemaphoreType.DMA((2,))],
        compiler_params=pltpu.CompilerParams(vmem_limit_bytes=VMEM_BYTES),
        cost_estimate=pl.CostEstimate(flops=flops, bytes_accessed=0, transcendentals=0),
        name="weight_grads",
    )(*values)


def pack_kernel(held, across, above, lower, upper, out, buffer, sems):
    size = held.shape[0]
    half = size // 2
    corner = pl.ds(lower.shape[0] - half, half)
    incoming = [
        pltpu.make_async_copy(source, target, sems.at[index])
        for index, (source, target) in enumerate(
            (
                (held, buffer.at[0]),
                (across.at[:size], buffer.at[1]),
                (above.at[:size], buffer.at[2]),
                (upper.at[corner], buffer.at[3, :half]),
                (lower.at[corner], buffer.at[3, half:]),
            )
        )
    ]
    outgoing = [
        pltpu.make_async_copy(buffer.at[index], out.at[index], sems.at[5 + index])
        for index in range(4)
    ]
    for copy in incoming:
        copy.start()
    for index in range(3):
        incoming[index].wait()
        outgoing[index].start()
    incoming[3].wait()
    incoming[4].wait()
    outgoing[3].start()
    for copy in outgoing:
        copy.wait()


def pack_blocks(blocks):
    shape = (4,) + blocks[0].shape
    return pl.pallas_call(
        pack_kernel,
        in_specs=[IN_HBM] * 5,
        out_specs=IN_HBM,
        out_shape=of(shape, jnp.bfloat16),
        scratch_shapes=[pltpu.VMEM(shape, jnp.bfloat16), pltpu.SemaphoreType.DMA((9,))],
        compiler_params=pltpu.CompilerParams(vmem_limit_bytes=VMEM_BYTES // 4),
        cost_estimate=SMALL_COST,
        name="pack_blocks",
    )(*blocks)


def placing_matrix(core, part, block, half, shape):
    feature = lax.broadcasted_iota(jnp.int32, shape, 0) + block * shape[0]
    target = lax.broadcasted_iota(jnp.int32, shape, 1)
    row = feature // part
    match = (row & 1) == (core ^ half)
    match &= (row // 2) * part + (feature - row * part) == target
    return jnp.where(match, 1.0, 0.0).astype(jnp.bfloat16)


def enter_kernel(part, where_ref, *refs):
    *blocks, out_ref = refs
    shape = (blocks[0].shape[1], out_ref.shape[2])
    for half in range(2):
        total = None
        for step, block in enumerate(blocks):
            matrix = placing_matrix(where_ref[0], part, where_ref[1] ^ step, half, shape)
            term = dot(block[...], matrix, PLAIN)
            total = term if total is None else total + term
        out_ref[half] = total


def leave_kernel(part, where_ref, halves_ref, *outs):
    shape = (outs[0].shape[1], halves_ref.shape[2])
    halves = [halves_ref[half].astype(jnp.bfloat16) for half in range(2)]
    for step, out in enumerate(outs):
        total = None
        for half in range(2):
            matrix = placing_matrix(where_ref[0], part, where_ref[1] ^ step, half, shape)
            term = dot(halves[half], matrix, TURNED)
            total = term if total is None else total + term
        out[...] = total.astype(jnp.bfloat16)


def assemble_kernel(where_ref, *refs):
    *blocks, out_ref = refs
    for step, block in enumerate(blocks):
        out_ref[where_ref[1] ^ step] = block[...].astype(out_ref.dtype)


def reorder(kernel, values, outs, place):
    in_vmem = pl.BlockSpec(memory_space=pltpu.VMEM)
    where = jnp.stack((place.core, place.col)).astype(jnp.int32)
    return pl.pallas_call(
        kernel,
        in_specs=[pl.BlockSpec(memory_space=pltpu.SMEM)] + [in_vmem] * len(values),
        out_specs=[in_vmem] * len(outs),
        out_shape=outs,
        compiler_params=pltpu.CompilerParams(vmem_limit_bytes=VMEM_BYTES // 2),
        cost_estimate=SMALL_COST,
        name="reorder",
    )(where, *values)


def add_kernel(held, across_upper, across_first, above_first, above_lower, out):
    rows = across_upper.shape[0]
    for start, pair in ((0, (across_upper, above_first)), (rows, (across_first, above_lower))):
        total = held[start : start + rows].astype(jnp.float32)
        for value in pair:
            total += value[:rows].astype(jnp.float32)
        out[start : start + rows] = total.astype(jnp.bfloat16)


def add_blocks(blocks):
    in_vmem = pl.BlockSpec(memory_space=pltpu.VMEM)
    return pl.pallas_call(
        add_kernel,
        in_specs=[in_vmem] * 5,
        out_specs=in_vmem,
        out_shape=of(blocks[0].shape, jnp.bfloat16),
        compiler_params=pltpu.CompilerParams(vmem_limit_bytes=VMEM_BYTES // 2),
        cost_estimate=SMALL_COST,
        name="add_blocks",
    )(*blocks)


def token_parallel(
    tokens,
    conditioning,
    ada_weight,
    ada_bias,
    qkv_weight,
    attn_bias,
    mixing_weight,
    mixing_bias,
    hidden_weight,
    hidden_bias,
    output_weight,
    output_bias,
    cotangent,
):
    place = Place()
    col_width = ada_bias.shape[2]
    row_width = conditioning.shape[1]
    hidden_width = hidden_bias.shape[1]
    layer_count = ada_bias.shape[0]
    clip_count = conditioning.shape[0]
    width = col_width * place.col_count

    copies = (place.row_count // 2, 1)

    def attn_shards(*gate):
        first, second = together(qkv_weight, mixing_weight, *gate)[:2]
        return [
            jnp.tile(
                jnp.concatenate(
                    (
                        first[depth].reshape(row_width, 3 * col_width),
                        second[depth].reshape(col_width, row_width).T,
                    ),
                    1,
                ),
                copies,
            )
            for depth in range(layer_count)
        ]

    def hidden_shards(*gate):
        value = after(hidden_weight, *gate)
        return [
            jnp.tile(value[depth].reshape(row_width, hidden_width), copies)
            for depth in range(layer_count)
        ]

    def output_shards(*gate):
        value = after(output_weight, *gate)
        return [
            jnp.tile(value[depth].reshape(hidden_width, row_width).T, copies)
            for depth in range(layer_count)
        ]

    def arriving(held):
        return trade(relative(held.reshape(clip_count, -1, col_width), place))

    def entered(blocks):
        outs = [of((2, blocks[0].shape[0], width // 2), jnp.float32)]
        return reorder(functools.partial(enter_kernel, row_width), blocks, outs, place)[0]

    gathering = Gathering(place)
    attn_ready = attn_shards()
    tokens = after(open_tokens(tokens, col_width), attn_ready[0])
    cotangent = open_tokens(cotangent, col_width)
    frame_part, places = tokens.shape[1:3]
    frames, place_part = cotangent.shape[1:3]
    period = 16 if place_part % 16 == 0 else place_part
    groups = place_part // period
    first_size = places
    second_size = frames * period
    gathering.step(attn_ready[0])
    token_blocks = arriving(tokens)
    hidden_ready = hidden_shards(attn_ready[0])
    hidden_ready, attn_ready, token_blocks = together(hidden_ready, attn_ready, token_blocks)
    gathering.step(hidden_ready[0], *token_blocks)
    conditioning, ada_weight, attn_bias, token_blocks, output_gate = after(
        (conditioning, ada_weight, attn_bias, token_blocks, output_weight), *gathering.sent
    )
    output_weight = output_gate
    output_ready = output_shards()
    stream_first = entered(token_blocks)
    ada_weight = ada_weight.reshape(layer_count, row_width, 6, col_width)

    half = width // 2

    def leaving(halves):
        outs = [of((halves.shape[1], col_width), jnp.bfloat16)] * place.col_count
        return reorder(functools.partial(leave_kernel, row_width), [halves], outs, place)

    def assembled(blocks, dtype):
        outs = [of((len(blocks),) + blocks[0].shape, dtype)]
        return reorder(assemble_kernel, blocks, outs, place)[0]

    cond_act = jax.nn.silu(conditioning).astype(jnp.bfloat16)
    modulation = matmul("cr,lrsk->clsk", cond_act, ada_weight)
    modulation = modulation.reshape(clip_count, -1)
    cut = modulation.shape[1]
    own = [modulation] + [
        value.reshape(clip_count, -1)
        for value in (attn_bias, hidden_bias, mixing_bias, output_bias, ada_bias)
    ]
    met = lax.all_gather(jnp.concatenate(own, 1), ("row", "col"), axis=0)
    met = met.reshape(place.row_count, place.col_count, clip_count, -1)
    modulation = lax.dynamic_index_in_dim(met, place.col, 2, keepdims=False)[:, :, :cut]
    modulation = jnp.sum(modulation, 0).reshape(-1, layer_count, 6, col_width)
    rest = met[0, :, :, cut:]
    vectors = []
    for value in (attn_bias, hidden_bias, mixing_bias, output_bias, ada_bias):
        size = value.size // clip_count
        vectors.append(rest[:, :, :size].reshape((place.col_count,) + value.shape))
        rest = rest[:, :, size:]
    modulation = modulation + vectors.pop()
    modulation = jnp.moveaxis(modulation, 0, 2).reshape(layer_count, 6, width)
    modulation = jnp.swapaxes(to_halves(modulation, place), 1, 2)
    attn_add, hidden_add, mixing_add, output_add = vectors
    attn_add, hidden_add = (relative(value, place) for value in (attn_add, hidden_add))

    def whole_vector(blocks):
        joined = jnp.moveaxis(blocks, 0, 1).reshape(layer_count, width)
        return to_halves(joined, place)

    mixing_add = whole_vector(mixing_add)
    output_add = whole_vector(output_add)

    blank = jnp.zeros((round_up(3 * col_width) - 3 * col_width,), jnp.float32)

    def biases_of(depth):
        attn_rows = [
            jnp.concatenate((block[depth, 0], jnp.zeros_like(block[depth, 0]), block[depth, 1], blank))
            for block in attn_add
        ]
        return (
            jnp.stack(attn_rows)[:, None, :],
            mixing_add[depth][:, None, :],
            jnp.stack([block[depth] for block in hidden_add])[:, None, :],
            output_add[depth][:, None, :],
        )

    attn_biases, mixing_biases, hidden_biases, output_biases = zip(biases_of(0), biases_of(1))
    sizes = (first_size, second_size)
    periods = (0, period)

    def attn_part(depth, stream):
        return attention_forward(
            stream,
            modulation[depth],
            gathering.done[3 * depth],
            attn_biases[depth],
            mixing_biases[depth],
            sizes[depth],
            periods[depth],
        )

    def mlp_part(depth, mid):
        return mlp_forward(
            mid,
            modulation[depth],
            gathering.done[3 * depth + 1],
            gathering.done[3 * depth + 2],
            hidden_biases[depth],
            output_biases[depth],
        )

    def mlp_grads(depth, grad, saved):
        _, mid, _, (_, _, _, slope, mlp_out) = saved
        return mlp_backward(
            grad, mid, mlp_out, slope, modulation[depth], *gathering.done[3 * depth + 1 : 3 * depth + 3]
        )

    def attn_grads(depth, grad_mid, saved):
        stream, _, (_, _, qkv, _, logs, attn_out), _ = saved
        return attention_backward(
            grad_mid,
            stream,
            attn_out,
            qkv,
            logs,
            modulation[depth],
            gathering.done[3 * depth],
            sizes[depth],
            periods[depth],
        )

    def attn_terms(saved, swapped, grad_attn, grad_qkv, received, flops=0):
        input_attn, _, _, heads, _, _ = saved[2]
        columns = 4 * col_width
        return weight_grads(
            columns,
            grad_qkv.shape[2] + heads.shape[2] - columns,
            (input_attn, swapped[0], grad_qkv, received[0]),
            (grad_attn, received[1], heads, swapped[1]),
            flops=flops,
        )

    def output_terms(saved, swapped, grad_mlp, received):
        active = saved[3][2]
        return weight_grads(active.shape[2], 0, (grad_mlp, received, active, swapped[3]))

    def hidden_terms(saved, swapped, grad_pre, received):
        return weight_grads(
            grad_pre.shape[2], 0, (saved[3][0], swapped[2], grad_pre, received)
        )

    gathering.step(output_ready[0], stream_first, *output_ready)
    gathering.step(attn_ready[1], modulation)
    mid_first, *attn_first = attn_part(0, after(stream_first, *gathering.sent))
    gathering.step(hidden_ready[1], mid_first)
    cotangent = after(cotangent, *gathering.sent)
    cotangent = cotangent.reshape(clip_count, frames, groups, period, col_width)
    gradient_blocks = relative(
        jnp.swapaxes(cotangent, 1, 2).reshape(clip_count, -1, col_width), place
    )
    gathering.step(output_ready[1], *gradient_blocks)
    input_attn, heads = after((attn_first[1], attn_first[3]), *gathering.sent)
    swapped_first = [swap(input_attn), swap(heads)]
    output_first, *mlp_first = mlp_part(0, after(mid_first, *gathering.sent))
    saved_first = (stream_first, mid_first, attn_first, mlp_first)
    gathering.step(None, output_first, *swapped_first)
    input_mlp, active, moving = after(
        (mlp_first[1], mlp_first[2], output_first), *gathering.sent
    )
    swapped_first += [swap(input_mlp), swap(active)]
    moving = mine_first(moving.astype(jnp.bfloat16), place, 0)
    moving = moving.reshape(2, frame_part, place.row_count, groups, period, half)
    moving = moving.transpose(0, 2, 3, 1, 4, 5)
    moved = lax.all_to_all(moving, "row", split_axis=1, concat_axis=3, tiled=True)
    gathering.step(None, moved, *swapped_first[2:])
    moved = after(moved, *gathering.sent)
    moved = moved.reshape(2, -1, half)
    stream_second = mine_first(moved, place, 0).astype(jnp.float32)
    gathering.step(None)
    stream_second = after(stream_second, gathering.done[5][0])
    mid_second, *attn_second = attn_part(1, stream_second)
    mid_second, input_attn, heads = together(mid_second, attn_second[1], attn_second[3])
    swapped_second = [swap(input_attn), swap(heads)]
    gradient_blocks = trade(after(gradient_blocks, mid_second))
    output_second, *mlp_second = mlp_part(1, mid_second)
    saved_second = (stream_second, mid_second, attn_second, mlp_second)
    gradient_blocks, swapped_second, input_mlp, active, output_second = together(
        gradient_blocks, swapped_second, mlp_second[1], mlp_second[2], output_second
    )
    grad = entered(gradient_blocks)
    swapped_second += [swap(input_mlp), swap(active)]

    grad_mid, grad_mlp, grad_sent, grad_pre, small_mlp_second, hidden_sum_second = mlp_grads(
        1, grad, saved_second
    )
    grad_mid, grad_mlp, grad_sent, grad_pre, swapped_second, output_second = together(
        grad_mid, grad_mlp, grad_sent, grad_pre, swapped_second, output_second
    )
    received = swap(grad_sent)
    received, grad_pre = together(received, grad_pre)
    received_pre = swap(grad_pre)
    output_part = output_terms(saved_second, swapped_second, grad_mlp, received)
    output_part, received_pre, grad_mid = together(output_part, received_pre, grad_mid)
    output_part = scatter_corner(output_part)
    hidden_part = hidden_terms(saved_second, swapped_second, grad_pre, received_pre)
    hidden_part, grad_mid = together(hidden_part, grad_mid)
    hidden_part = scatter_corner(hidden_part)
    grad_second, grad_attn, grad_sent, grad_qkv, small_attn_second, qkv_sum_second = attn_grads(
        1, grad_mid, saved_second
    )
    grad_second, grad_attn, grad_sent, grad_qkv, output_part, output_second = together(
        grad_second, grad_attn, grad_sent, grad_qkv, output_part, output_second
    )
    received = [swap(grad_qkv), swap(grad_sent)]
    sides = scatter_sides(output_part)
    moving = mine_first(grad_second.astype(jnp.bfloat16), place, 0)
    moving = moving.reshape(2, 1, groups, frames, period, half)
    received, grad_attn, grad_qkv, sides, moving = together(
        received, grad_attn, grad_qkv, sides, moving
    )
    output_part = scatter_plane(output_part, sides)
    attn_blocks = attn_terms(saved_second, swapped_second, grad_attn, grad_qkv, received)
    attn_blocks, moving, hidden_part = together(attn_blocks, moving, hidden_part)
    moved = lax.all_to_all(moving, "row", split_axis=3, concat_axis=1, tiled=True)
    attn_part_second = scatter_corner(attn_blocks)
    result_blocks = leaving(after(output_second, *attn_blocks))
    sides = scatter_sides(hidden_part)
    output_total = add_blocks(output_part)
    moved, output_total, sides, result_blocks = together(
        moved, output_total, sides, result_blocks
    )
    hidden_part = scatter_plane(hidden_part, sides)
    moved = moved.transpose(0, 3, 1, 2, 4, 5).reshape(2, -1, half)
    returned = mine_first(moved, place, 0).astype(jnp.float32)
    output_pieces = over_depth(output_total, place)
    result_blocks = trade(after(result_blocks, output_total))
    grad_mid, grad_mlp, grad_sent, grad_pre, small_mlp_first, hidden_sum_first = mlp_grads(
        0, returned, saved_first
    )
    grad_mid, grad_mlp, grad_sent, grad_pre, output_pieces, hidden_part, result_blocks = together(
        grad_mid, grad_mlp, grad_sent, grad_pre, output_pieces, hidden_part, result_blocks
    )
    received = swap(grad_sent)
    hidden_total = add_blocks(hidden_part)
    received, hidden_total, grad_pre = together(received, hidden_total, grad_pre)
    hidden_pieces = over_depth(hidden_total, place)
    received_pre = swap(grad_pre)
    output_blocks = output_terms(saved_first, swapped_first, grad_mlp, received)
    output_blocks, received_pre = together(output_blocks, received_pre)
    output_part = scatter_corner(output_blocks)
    hidden_blocks = hidden_terms(saved_first, swapped_first, grad_pre, received_pre)
    hidden_blocks, grad_mid, attn_part_second = together(
        hidden_blocks, grad_mid, attn_part_second
    )
    sides = scatter_sides(attn_part_second)
    grad_mid, sides = together(grad_mid, sides)
    attn_part_second = scatter_plane(attn_part_second, sides)
    hidden_part = scatter_corner(hidden_blocks)
    grad_first, grad_attn, grad_sent, grad_qkv, small_attn_first, qkv_sum_first = attn_grads(
        0, grad_mid, saved_first
    )
    (
        grad_first,
        grad_attn,
        grad_sent,
        grad_qkv,
        output_part,
        attn_part_second,
        hidden_pieces,
    ) = together(
        grad_first, grad_attn, grad_sent, grad_qkv, output_part, attn_part_second, hidden_pieces
    )
    received = [swap(grad_qkv), swap(grad_sent)]
    sides = scatter_sides(output_part)
    attn_total = add_blocks(attn_part_second)
    received, sides, attn_total, grad_attn, grad_qkv = together(
        received, sides, attn_total, grad_attn, grad_qkv
    )
    output_part = scatter_plane(output_part, sides)
    attn_pieces = over_depth(attn_total, place)
    attn_blocks = attn_terms(saved_first, swapped_first, grad_attn, grad_qkv, received)
    def small_grads(small_attn, small_mlp, qkv_sum, hidden_sum):
        return (
            jnp.concatenate((small_attn[:, :3], small_mlp[:, :3]), 1),
            (qkv_sum[:, 0], small_attn[:, 3], hidden_sum[:, 0], small_mlp[:, 3]),
        )

    modgrad_first, biasgrad_first = small_grads(
        small_attn_first, small_mlp_first, qkv_sum_first, hidden_sum_first
    )
    modgrad_second, biasgrad_second = small_grads(
        small_attn_second, small_mlp_second, qkv_sum_second, hidden_sum_second
    )
    def by_block(halves):
        features = from_halves(halves, place)
        features = features.reshape(features.shape[:-1] + (place.col_count, col_width))
        return relative(jnp.moveaxis(features, -2, 0), place)

    modgrad = by_block(jnp.swapaxes(jnp.stack((modgrad_first, modgrad_second)), 1, 2))
    mixgrad = by_block(jnp.stack((biasgrad_first[1], biasgrad_second[1])))
    outgrad = by_block(jnp.stack((biasgrad_first[3], biasgrad_second[3])))
    sending = []
    for step in range(place.col_count):
        pieces = [modgrad[step].reshape(-1)]
        for grads in (biasgrad_first, biasgrad_second):
            pieces.append(grads[0][step][:col_width])
            pieces.append(grads[0][step][2 * col_width : 3 * col_width])
        for grads in (biasgrad_first, biasgrad_second):
            pieces.append(grads[2][step])
        pieces.append(mixgrad[step].reshape(-1))
        pieces.append(outgrad[step].reshape(-1))
        sending.append(jnp.concatenate(pieces))
    sending = [value.reshape(-1, LANES) for value in sending]
    attn_blocks, output_part, hidden_part, grad_first, result_blocks = together(
        attn_blocks, output_part, hidden_part, grad_first, result_blocks
    )
    attn_part_first = scatter_corner(attn_blocks)
    sides = scatter_sides(hidden_part)
    output_total = add_blocks(output_part)
    output_total, sides, grad_first, attn_pieces = together(
        output_total, sides, grad_first, attn_pieces
    )
    hidden_part = scatter_plane(hidden_part, sides)
    output_first_pieces = over_depth(output_total, place)
    gradient_blocks = leaving(grad_first)

    result = assembled(result_blocks, jnp.bfloat16)
    result = result.reshape(clip_count, groups, frames, period, col_width)
    result = jnp.swapaxes(result, 1, 2).reshape(clip_count, frames, place_part, col_width)
    result = close_tokens(result)
    attn_part_first, hidden_part, gradient_blocks, sending, result = together(
        attn_part_first, hidden_part, gradient_blocks, sending, result
    )
    sides = scatter_sides(attn_part_first)
    hidden_total = add_blocks(hidden_part)
    sides, hidden_total, sending, output_first_pieces = together(
        sides, hidden_total, sending, output_first_pieces
    )
    attn_part_first = scatter_plane(attn_part_first, sides)
    met = trade(sending)
    hidden_first_pieces = over_depth(hidden_total, place)
    met = [value.reshape(-1) for value in met]
    modgrad = jnp.concatenate([block[:cut] for block in met])
    biasgrad = sum(block[cut:] for block in met)
    small = jnp.concatenate((modgrad, biasgrad))
    small = small + swap(small)
    small, attn_part_first = together(small, attn_part_first)
    attn_total = add_blocks(attn_part_first)
    small, attn_total = together(small, attn_total)
    gradient_blocks = trade(gradient_blocks)
    for mask in place.depth_masks:
        small = small + exchange(small, "row", mask)
    sums = [add_all(pieces, place) for pieces in (attn_pieces, hidden_pieces, output_pieces)]
    gradient_blocks, hidden_first_pieces, attn_total, small, sums = together(
        gradient_blocks, hidden_first_pieces, attn_total, small, sums
    )
    attn_first_pieces = over_depth(attn_total, place)
    tokens_gradient = assembled(gradient_blocks, jnp.float32)
    tokens_gradient = tokens_gradient.reshape(clip_count, frame_part, places, col_width)
    first_sums = [
        add_all(pieces, place)
        for pieces in (attn_first_pieces, hidden_first_pieces, output_first_pieces)
    ]
    modgrad = small[: cut * clip_count].reshape(clip_count, layer_count, 6, col_width)
    modgrad = jnp.moveaxis(jnp.stack(relative(modgrad, place)), 1, 0)
    rest = small[cut * clip_count :]
    bias_grads = []
    for value in (attn_bias, hidden_bias, mixing_bias, output_bias):
        bias_grads.append(rest[: value.size].reshape(value.shape))
        rest = rest[value.size :]
    ada_bias_grad = jnp.sum(modgrad, 1)
    ada_weight_grad = jnp.einsum(
        "cr,lcsk->lrsk", cond_act.astype(jnp.float32), modgrad, precision=highest
    )
    cond_part = jnp.einsum(
        "lcsk,lrsk->cr", modgrad, ada_weight.astype(jnp.float32), precision=highest
    )
    for mask in (1, 2):
        cond_part = cond_part + exchange(cond_part, "col", mask)
    conditioning_gradient = jax.vjp(jax.nn.silu, conditioning)[1](cond_part)[0]

    attn_sums, hidden_sums, output_sums = (
        jnp.stack((first_sums[index], sums[index])) for index in range(3)
    )
    return (
        result,
        close_tokens(tokens_gradient),
        conditioning_gradient,
        close_weight(ada_weight_grad),
        ada_bias_grad,
        close_weight(attn_sums[:, :, : 3 * col_width]),
        bias_grads[0],
        close_weight(jnp.swapaxes(attn_sums[:, :, 3 * col_width :], 1, 2)),
        bias_grads[2],
        close_weight(hidden_sums),
        bias_grads[1],
        close_weight(jnp.swapaxes(output_sums, 1, 2)),
        bias_grads[3],
    )


def suits_tokens(mesh):
    rows, cols = (mesh.shape["row"], mesh.shape["col"])
    return cols == 4 and rows >= 2 and rows & (rows - 1) == 0


def solution(mesh):
    placed = (
        P(None, "row", "col", None),
        P(None, "row"),
        P(None, "row", "col", None),
        P(None, None, "col"),
        P(None, "row", "col", None),
        P(None, None, "col"),
        P(None, "col", "row", None),
        P(None, "col"),
        P(None, "row", "col", None),
        P(None, "col"),
        P(None, "col", "row", None),
        P(None, "col"),
        P(None, None, "col", "row"),
    )
    return jax.shard_map(
        token_parallel if suits_tokens(mesh) else tensor_parallel,
        mesh=mesh,
        in_specs=placed,
        out_specs=(
            P(None, None, "col", "row"),
            P(None, "row", "col", None),
            P(None, "row"),
            P(None, "row", "col", None),
            P(None, None, "col"),
            P(None, "row", "col", None),
            P(None, None, "col"),
            P(None, "col", "row", None),
            P(None, "col"),
            P(None, "row", "col", None),
            P(None, "col"),
            P(None, "col", "row", None),
            P(None, "col"),
        ),
        check_vma=False,
    )
```

```python
import functools

import jax
import jax.numpy as jnp
from jax import lax
from jax.experimental import pallas as pl
from jax.experimental.pallas import tpu as pltpu
from jax.sharding import PartitionSpec as P

HEAD_DIM = 72


epsilon = 1e-06
highest = lax.Precision.HIGHEST
spatial_forms = ("caqhe,cakhe->cahqk", "cahqk,cakhe->caqhe", "cahqk,caqhe->cakhe")
temporal_forms = ("cqbhe,ckbhe->cbhqk", "cbhqk,ckbhe->cqbhe", "cbhqk,cqbhe->ckbhe")


def matmul(pattern, left, right):
    return jnp.einsum(pattern, left, right, preferred_element_type=jnp.float32)


def split_heads(values):
    return values.reshape(values.shape[:-1] + (values.shape[-1] // HEAD_DIM, HEAD_DIM))


def merge_heads(values):
    return values.reshape(values.shape[:-2] + (values.shape[-2] * values.shape[-1],))


def gelu_tanh(values):
    return jax.nn.gelu(values, approximate=True)


def open_tokens(blocked, width):
    return blocked.reshape(blocked.shape[0], blocked.shape[1], blocked.shape[3] // width, width)


def close_tokens(plain_layout):
    return plain_layout.reshape(
        plain_layout.shape[0],
        plain_layout.shape[1],
        1,
        plain_layout.shape[2] * plain_layout.shape[3],
    )


def close_weight(plain_layout):
    return plain_layout.reshape(plain_layout.shape[0], 1, 1, -1)


def normalize(stream):
    feature_count = stream.shape[-1] * lax.axis_size("col")
    row_total, squares = lax.psum((jnp.sum(stream, -1), jnp.sum(stream * stream, -1)), "col")
    average = row_total / feature_count
    variance = squares / feature_count - average * average
    inverse = lax.rsqrt(variance + epsilon)
    return ((stream - average[..., None]) * inverse[..., None], inverse)


def normalize_back(grad_normed, normed, inverse):
    feature_count = grad_normed.shape[-1] * lax.axis_size("col")
    first, second = lax.psum((jnp.sum(grad_normed, -1), jnp.sum(grad_normed * normed, -1)), "col")
    return inverse[..., None] * (
        grad_normed - first[..., None] / feature_count - normed * second[..., None] / feature_count
    )


def spread(values):
    return lax.all_gather(values, "col", axis=3, tiled=True)


def collect(terms):
    return lax.psum_scatter(
        terms.astype(jnp.bfloat16), "col", scatter_dimension=3, tiled=True
    ).astype(jnp.float32)


def spread_grad(values):
    return lax.all_gather(values, "col", axis=3, tiled=True)


def collect_grad(terms):
    return lax.psum_scatter(
        terms.astype(jnp.bfloat16), "col", scatter_dimension=3, tiled=True
    ).astype(jnp.float32)


def fetch_weights(qkv_weight, mixing_weight, hidden_weight, output_weight, depth):
    return (
        lax.all_gather(qkv_weight[depth], "row", axis=0, tiled=True),
        lax.all_gather(mixing_weight[depth], "row", axis=1, tiled=True),
        lax.all_gather(hidden_weight[depth], "row", axis=0, tiled=True),
        lax.all_gather(output_weight[depth], "row", axis=1, tiled=True),
    )


def attend(queries, key_rows, value_rows, forms):
    softmax_scale = HEAD_DIM ** (-0.5)
    scores = matmul(forms[0], split_heads(queries), split_heads(key_rows)) * softmax_scale
    largest = jnp.max(scores, -1, keepdims=True)
    weights = jnp.exp(scores - largest)
    totals = jnp.sum(weights, -1, keepdims=True)
    probs = (weights / totals).astype(jnp.bfloat16)
    mixed = matmul(forms[1], probs, split_heads(value_rows))
    return (merge_heads(mixed).astype(jnp.bfloat16), largest + jnp.log(totals))


def attend_back(queries, key_rows, value_rows, grad_heads, log_totals, forms):
    softmax_scale = HEAD_DIM ** (-0.5)
    query_split = split_heads(queries)
    key_split = split_heads(key_rows)
    value_split = split_heads(value_rows)
    grad_split = split_heads(grad_heads)
    scores = matmul(forms[0], query_split, key_split) * softmax_scale
    probs = jnp.exp(scores - log_totals)
    grad_values = matmul(forms[2], probs.astype(jnp.bfloat16), grad_split)
    grad_probs = matmul(forms[0], grad_split, value_split)
    row_delta = jnp.sum(probs * grad_probs, -1, keepdims=True)
    grad_scores = (probs * (grad_probs - row_delta)).astype(jnp.bfloat16)
    grad_queries = matmul(forms[1], grad_scores, key_split) * softmax_scale
    grad_keys = matmul(forms[2], grad_scores, query_split) * softmax_scale
    return tuple(
        (
            merge_heads(part_grad).astype(jnp.bfloat16)
            for part_grad in (grad_queries, grad_keys, grad_values)
        )
    )


def residual_forward(stream, modulation, weights, biases, forms):
    qkv_full, mixing_full, hidden_full, output_full = weights
    attn_add, mixing_add, hidden_add, output_add = biases

    def piece_of(column):
        return modulation[:, column][:, None, None, :]

    normed_attn, inv_attn = normalize(stream)
    input_attn = spread((normed_attn * (1.0 + piece_of(1)) + piece_of(0)).astype(jnp.bfloat16))
    qkv_rows = matmul("cabd,dsk->cabsk", input_attn, qkv_full)
    queries = (qkv_rows[..., 0, :] + attn_add[0]).astype(jnp.bfloat16)
    key_rows = qkv_rows[..., 1, :].astype(jnp.bfloat16)
    value_rows = (qkv_rows[..., 2, :] + attn_add[1]).astype(jnp.bfloat16)
    heads_out, log_totals = attend(queries, key_rows, value_rows, forms)
    attn_out = collect(matmul("cabk,kd->cabd", heads_out, mixing_full)) + mixing_add
    stream_mid = stream + piece_of(2) * attn_out
    normed_mlp, inv_mlp = normalize(stream_mid)
    input_mlp = spread((normed_mlp * (1.0 + piece_of(4)) + piece_of(3)).astype(jnp.bfloat16))
    pre_gelu = matmul("cabd,df->cabf", input_mlp, hidden_full) + hidden_add
    activated = gelu_tanh(pre_gelu).astype(jnp.bfloat16)
    mlp_out = collect(matmul("cabf,fd->cabd", activated, output_full)) + output_add
    stream_out = stream_mid + piece_of(5) * mlp_out
    saved = (
        normed_attn,
        inv_attn,
        input_attn,
        queries,
        key_rows,
        value_rows,
        heads_out,
        log_totals,
        attn_out,
        normed_mlp,
        inv_mlp,
        input_mlp,
        pre_gelu,
        activated,
        mlp_out,
    )
    return (stream_out, saved)


def residual_backward(grad_stream, saved, modulation, weights, forms):
    (
        normed_attn,
        inv_attn,
        input_attn,
        queries,
        key_rows,
        value_rows,
        heads_out,
        log_totals,
        attn_out,
        normed_mlp,
        inv_mlp,
        input_mlp,
        pre_gelu,
        activated,
        mlp_out,
    ) = saved
    qkv_full, mixing_full, hidden_full, output_full = weights

    def piece_of(column):
        return modulation[:, column][:, None, None, :]

    grad_mlp = (grad_stream * piece_of(5)).astype(jnp.bfloat16)
    gate_mlp_grad = jnp.sum(grad_stream * mlp_out, (1, 2))
    grad_mlp_all = spread_grad(grad_mlp)
    output_weight_term = matmul("cabf,cabd->fd", activated, grad_mlp_all)
    grad_act = matmul("cabd,fd->cabf", grad_mlp_all, output_full)
    grad_pre = jax.vjp(gelu_tanh, pre_gelu)[1](grad_act)[0].astype(jnp.bfloat16)
    hidden_weight_term = matmul("cabd,cabf->df", input_mlp, grad_pre)
    grad_input_mlp = collect_grad(matmul("cabf,df->cabd", grad_pre, hidden_full))
    shift_mlp_grad = jnp.sum(grad_input_mlp, (1, 2))
    scale_mlp_grad = jnp.sum(grad_input_mlp * normed_mlp, (1, 2))
    grad_mid = grad_stream + normalize_back(
        grad_input_mlp * (1.0 + piece_of(4)), normed_mlp, inv_mlp
    )
    grad_attn = (grad_mid * piece_of(2)).astype(jnp.bfloat16)
    gate_attn_grad = jnp.sum(grad_mid * attn_out, (1, 2))
    grad_attn_all = spread_grad(grad_attn)
    mixing_weight_term = matmul("cabk,cabd->kd", heads_out, grad_attn_all)
    grad_heads = matmul("cabd,kd->cabk", grad_attn_all, mixing_full).astype(jnp.bfloat16)
    grad_queries, grad_keys, grad_values = attend_back(
        queries, key_rows, value_rows, grad_heads, log_totals, forms
    )
    grad_qkv = jnp.stack((grad_queries, grad_keys, grad_values), 3)
    qkv_weight_term = matmul("cabd,cabsk->dsk", input_attn, grad_qkv)
    grad_input_attn = collect_grad(matmul("cabsk,dsk->cabd", grad_qkv, qkv_full))
    shift_attn_grad = jnp.sum(grad_input_attn, (1, 2))
    scale_attn_grad = jnp.sum(grad_input_attn * normed_attn, (1, 2))
    grad_input = grad_mid + normalize_back(
        grad_input_attn * (1.0 + piece_of(1)), normed_attn, inv_attn
    )
    weight_terms = (
        lax.psum_scatter(
            qkv_weight_term.astype(jnp.bfloat16), "row", scatter_dimension=0, tiled=True
        ).astype(jnp.float32),
        lax.psum_scatter(
            mixing_weight_term.astype(jnp.bfloat16), "row", scatter_dimension=1, tiled=True
        ).astype(jnp.float32),
        lax.psum_scatter(
            hidden_weight_term.astype(jnp.bfloat16), "row", scatter_dimension=0, tiled=True
        ).astype(jnp.float32),
        lax.psum_scatter(
            output_weight_term.astype(jnp.bfloat16), "row", scatter_dimension=1, tiled=True
        ).astype(jnp.float32),
    )
    modulation_grad = jnp.stack(
        (
            shift_attn_grad,
            scale_attn_grad,
            gate_attn_grad,
            shift_mlp_grad,
            scale_mlp_grad,
            gate_mlp_grad,
        ),
        1,
    )
    attn_bias_term = jnp.stack(
        (
            jnp.sum(grad_queries.astype(jnp.float32), (0, 1, 2)),
            jnp.sum(grad_values.astype(jnp.float32), (0, 1, 2)),
        )
    )
    bias_terms = (
        attn_bias_term,
        jnp.sum(grad_attn.astype(jnp.float32), (0, 1, 2)),
        jnp.sum(grad_pre.astype(jnp.float32), (0, 1, 2)),
        jnp.sum(grad_mlp.astype(jnp.float32), (0, 1, 2)),
    )
    return (grad_input, weight_terms, modulation_grad, bias_terms)


def tensor_parallel(
    tokens,
    conditioning,
    ada_weight,
    ada_bias,
    qkv_weight,
    attn_bias,
    mixing_weight,
    mixing_bias,
    hidden_weight,
    hidden_bias,
    output_weight,
    output_bias,
    cotangent,
):
    col_width = ada_bias.shape[2]
    row_width = conditioning.shape[1]
    hidden_width = hidden_bias.shape[1]
    layer_count = ada_bias.shape[0]
    ada_weight = ada_weight.reshape(layer_count, row_width, 6, col_width)
    qkv_weight = qkv_weight.reshape(layer_count, row_width, 3, col_width)
    mixing_weight = mixing_weight.reshape(layer_count, col_width, row_width)
    hidden_weight = hidden_weight.reshape(layer_count, row_width, hidden_width)
    output_weight = output_weight.reshape(layer_count, hidden_width, row_width)
    tokens = open_tokens(tokens, col_width)
    cotangent = open_tokens(cotangent, col_width)
    cond_act = jax.nn.silu(conditioning).astype(jnp.bfloat16)
    modulation = lax.psum(
        (
            matmul("cr,rsk->csk", cond_act, ada_weight[0]),
            matmul("cr,rsk->csk", cond_act, ada_weight[1]),
        ),
        "row",
    )
    modulation = (modulation[0] + ada_bias[0][None], modulation[1] + ada_bias[1][None])

    def biases_of(depth):
        return (attn_bias[depth], mixing_bias[depth], hidden_bias[depth], output_bias[depth])

    stream_first = tokens.astype(jnp.float32)
    weights_first = fetch_weights(qkv_weight, mixing_weight, hidden_weight, output_weight, 0)
    output_first, saved_first = residual_forward(
        stream_first, modulation[0], weights_first, biases_of(0), spatial_forms
    )
    moved = lax.all_to_all(
        output_first.astype(jnp.bfloat16), "row", split_axis=2, concat_axis=1, tiled=True
    )
    stream_second = moved.astype(jnp.float32)
    weights_second = fetch_weights(qkv_weight, mixing_weight, hidden_weight, output_weight, 1)
    output_second, saved_second = residual_forward(
        stream_second, modulation[1], weights_second, biases_of(1), temporal_forms
    )
    result = output_second.astype(jnp.bfloat16)
    weights_second = fetch_weights(qkv_weight, mixing_weight, hidden_weight, output_weight, 1)
    saved_second = residual_forward(
        stream_second, modulation[1], weights_second, biases_of(1), temporal_forms
    )[1]
    grad_second, terms_second, modgrad_second, biasgrad_second = residual_backward(
        cotangent.astype(jnp.float32), saved_second, modulation[1], weights_second, temporal_forms
    )
    returned = lax.all_to_all(
        grad_second.astype(jnp.bfloat16), "row", split_axis=1, concat_axis=2, tiled=True
    )
    weights_first = fetch_weights(qkv_weight, mixing_weight, hidden_weight, output_weight, 0)
    saved_first = residual_forward(
        stream_first, modulation[0], weights_first, biases_of(0), spatial_forms
    )[1]
    grad_first, terms_first, modgrad_first, biasgrad_first = residual_backward(
        returned.astype(jnp.float32), saved_first, modulation[0], weights_first, spatial_forms
    )
    summed = (
        lax.psum(jnp.stack((modgrad_first, modgrad_second)).astype(jnp.bfloat16), "row").astype(
            jnp.float32
        ),
        lax.psum(
            jnp.stack((biasgrad_first[0], biasgrad_second[0])).astype(jnp.bfloat16), "row"
        ).astype(jnp.float32),
        lax.psum(
            jnp.stack((biasgrad_first[1], biasgrad_second[1])).astype(jnp.bfloat16), "row"
        ).astype(jnp.float32),
        lax.psum(
            jnp.stack((biasgrad_first[2], biasgrad_second[2])).astype(jnp.bfloat16), "row"
        ).astype(jnp.float32),
        lax.psum(
            jnp.stack((biasgrad_first[3], biasgrad_second[3])).astype(jnp.bfloat16), "row"
        ).astype(jnp.float32),
    )
    modulation_grad = summed[0]
    ada_bias_grad = jnp.sum(modulation_grad, 1)
    ada_weight_grad = jnp.einsum(
        "cr,lcsk->lrsk", cond_act.astype(jnp.float32), modulation_grad, precision=highest
    )
    cond_part = jnp.einsum(
        "lcsk,lrsk->cr", modulation_grad, ada_weight.astype(jnp.float32), precision=highest
    )
    cond_part = lax.psum(cond_part, "col")
    conditioning_gradient = jax.vjp(jax.nn.silu, conditioning)[1](cond_part)[0]
    qkv_weight_grad = jnp.stack((terms_first[0], terms_second[0]))
    mixing_weight_grad = jnp.stack((terms_first[1], terms_second[1]))
    hidden_weight_grad = jnp.stack((terms_first[2], terms_second[2]))
    output_weight_grad = jnp.stack((terms_first[3], terms_second[3]))
    return (
        close_tokens(result),
        close_tokens(grad_first),
        conditioning_gradient,
        close_weight(ada_weight_grad),
        ada_bias_grad,
        close_weight(qkv_weight_grad),
        summed[1],
        close_weight(mixing_weight_grad),
        summed[2],
        close_weight(hidden_weight_grad),
        summed[3],
        close_weight(output_weight_grad),
        summed[4],
    )


def exchange(values, axis, mask):
    count = lax.axis_size(axis)
    return lax.ppermute(values, axis, [(index, index ^ mask) for index in range(count)])


def add_low(first, second):
    return (first.astype(jnp.float32) + second.astype(jnp.float32)).astype(jnp.bfloat16)


def after(values, *others):
    return lax.optimization_barrier((values,) + others)[0]


def together(*values):
    return lax.optimization_barrier(values)


def over_depth(values, place):
    groups = [list(range(core, place.row_count, 2)) for core in range(2)]
    return lax.all_to_all(
        values, "row", split_axis=0, concat_axis=0, tiled=True, axis_index_groups=groups
    )


def swap(values):
    return exchange(values, "row", 1)


class Gathering:
    def __init__(self, place):
        self.place = place
        self.held = ()
        self.plane = ()
        self.corner = ()
        self.sent = ()
        self.done = []

    def step(self, shard, *gates):
        groups = (self.held, self.plane, self.corner)
        values = list(together(*[value for group in groups for value in group], *gates))
        held, plane, corner = [[values.pop(0) for _ in group] for group in groups]
        across, above = ([], [])
        if held:
            across.append(held[0])
            above.append(held[0])
        if plane:
            size = plane[0].shape[0]
            across.append(plane[2][size // 2 : size])
            above.append(plane[1][: size // 2])
        across = [jnp.concatenate(across, 0)] if across else []
        above = [jnp.concatenate(above, 0)] if above else []
        self.sent = tuple(across + above)
        self.held = ()
        if shard is not None:
            self.held = (over_depth(after(shard, *self.sent), self.place),)
        if corner:
            own = pack_blocks(after(corner, *self.sent))
            self.done.append((own, swap(own)))
        met = tuple(
            exchange(value[0], "col", mask) for mask, value in ((1, across), (2, above)) if value
        )
        self.corner = tuple(plane) + met if plane else ()
        self.plane = tuple(held) + met if held else ()


def scatter_corner(blocks):
    held, across_upper, across_first, above_first, above_lower = blocks
    return (
        held,
        across_upper,
        exchange(across_first, "col", 1),
        exchange(above_first, "col", 2),
        above_lower,
    )


def scatter_sides(blocks):
    held, across_upper, across_first, above_first, above_lower = blocks
    half = across_upper.shape[0]
    return (
        add_low(across_upper, above_first[half:]),
        add_low(above_lower, across_first[half:]),
    )


def scatter_plane(blocks, sides):
    held, _, across_first, above_first, _ = blocks
    across, above = sides
    return (held, exchange(across, "col", 1), across_first, above_first, exchange(above, "col", 2))


def add_all(pieces, place):
    count = place.row_count // 2
    pieces = pieces.reshape((count, -1) + pieces.shape[1:])
    return jnp.sum(pieces.astype(jnp.float32), 0)


class Place:
    def __init__(self):
        self.row = lax.axis_index("row")
        self.col = lax.axis_index("col")
        self.row_count = lax.axis_size("row")
        self.col_count = lax.axis_size("col")
        self.core = self.row & 1
        self.depth_masks = []
        mask = 2
        while mask < self.row_count:
            self.depth_masks.append(mask)
            mask *= 2


def mine_first(halves, place, axis):
    return jnp.where(place.core == 1, jnp.flip(halves, axis), halves)


def to_halves(features, place):
    width = features.shape[-1]
    lead = features.shape[:-1]
    split_up = features.reshape(lead + (place.row_count // 2, 2, width // place.row_count))
    halves = jnp.swapaxes(split_up, -3, -2).reshape(lead + (2, width // 2))
    return mine_first(halves, place, len(lead))


def from_halves(halves, place):
    lead = halves.shape[:-2]
    half = halves.shape[-1]
    halves = mine_first(halves, place, len(lead))
    split_up = halves.reshape(lead + (2, place.row_count // 2, half // (place.row_count // 2)))
    return jnp.swapaxes(split_up, -3, -2).reshape(lead + (2 * half,))


def relative(stacked, place):
    return [
        lax.dynamic_index_in_dim(stacked, place.col ^ step, 0, keepdims=False)
        for step in range(place.col_count)
    ]


def absolute(blocks, place):
    return jnp.stack(relative(jnp.stack(blocks), place))


def trade(blocks):
    return [
        block if step == 0 else exchange(block, "col", step) for step, block in enumerate(blocks)
    ]


PLAIN = ((1,), (0,))
TURNED = ((1,), (1,))
SUMMED = ((0,), (0,))
VMEM_BYTES = 58 * 1024 * 1024
LANES = 128
LOG2_E = 1.4426950408889634
IN_HBM = pl.BlockSpec(memory_space=pl.ANY)
SMALL_COST = pl.CostEstimate(flops=0, bytes_accessed=0, transcendentals=0)


def dot(left, right, dims):
    return lax.dot_general(left, right, (dims, ((), ())), preferred_element_type=jnp.float32)


def round_up(value):
    return -(-value // LANES) * LANES


def whole(shape):
    return pl.BlockSpec(shape, lambda step: (0,) * len(shape))


def stepped(shape):
    return pl.BlockSpec((1,) + shape, lambda step: (step,) + (0,) * len(shape))


def of(shape, dtype):
    return jax.ShapeDtypeStruct(shape, dtype)


def norm_parts(stream_ref):
    first, second = (stream_ref[0], stream_ref[1])
    count = 2 * first.shape[1]
    average = (jnp.sum(first, 1, keepdims=True) + jnp.sum(second, 1, keepdims=True)) / count
    first, second = (first - average, second - average)
    variance = (
        jnp.sum(first * first, 1, keepdims=True) + jnp.sum(second * second, 1, keepdims=True)
    ) / count
    inverse = lax.rsqrt(variance + epsilon)
    return (first * inverse, second * inverse, inverse)


def norm_grads(stream_ref, acc, mod_ref, scale_row, grad_ref, out_ref, small_ref):
    normed = norm_parts(stream_ref)
    inverse = normed[2]
    count = 2 * normed[0].shape[1]
    weighted = []
    for half in range(2):
        grad_input = acc[half]
        small_ref[half, 0:1, :] = jnp.sum(grad_input, 0, keepdims=True)
        small_ref[half, 1:2, :] = jnp.sum(grad_input * normed[half], 0, keepdims=True)
        weighted.append(grad_input * (1.0 + mod_ref[half, scale_row : scale_row + 1, :]))
    first = sum(jnp.sum(value, 1, keepdims=True) for value in weighted) / count
    second = (
        sum(jnp.sum(value * normed[half], 1, keepdims=True) for half, value in enumerate(weighted))
        / count
    )
    for half in range(2):
        out_ref[half] = grad_ref[half] + inverse * (
            weighted[half] - first - normed[half] * second
        )


def same_place(size, period):
    row = lax.broadcasted_iota(jnp.int32, (size, size), 0)
    column = lax.broadcasted_iota(jnp.int32, (size, size), 1)
    return (row % period) == (column % period)


def attention_kernel(size, period, steps, *refs):
    stream_ref, mod_ref, bias_ref, added_ref = refs[:4]
    weights = refs[4:6]
    mid_ref, mine_ref, other_ref, qkv_ref, heads_ref, log_ref, out_ref, acc, kept_ref = refs[6:]
    input_refs = (mine_ref, kept_ref)
    step = pl.program_id(0)
    tokens = stream_ref.shape[1]
    used = qkv_ref.shape[2]
    padded = heads_ref.shape[2]
    columns = weights[0].shape[2]
    width = columns // 4
    count = width // HEAD_DIM
    scale = HEAD_DIM ** (-0.5)
    binary = scale * LOG2_E

    @pl.when(step == 0)
    def _():
        normed = norm_parts(stream_ref)
        for half in range(2):
            input_refs[half][...] = (
                normed[half] * (1.0 + mod_ref[half, 1:2, :]) + mod_ref[half, 0:1, :]
            ).astype(jnp.bfloat16)
        other_ref[...] = kept_ref[...].T
        acc[...] = jnp.zeros_like(acc)

    rows = dot(input_refs[0][...], weights[0][0, :, :used], PLAIN)
    rows = rows + dot(input_refs[1][...], weights[1][0, :, :used], PLAIN) + bias_ref[0]
    lane = lax.broadcasted_iota(jnp.int32, rows.shape, 1)
    qkv_ref[0] = jnp.where(lane < 3 * width, rows, 0.0).astype(jnp.bfloat16)
    log_lane = lax.broadcasted_iota(jnp.int32, (size, LANES), 1)
    for group in range(tokens // size):
        block = qkv_ref[0, group * size : (group + 1) * size, :]
        outs = [jnp.zeros((size, padded - width), jnp.float32)]
        logs = jnp.zeros((size, LANES), jnp.float32)
        for head in range(count):
            start = head * HEAD_DIM
            query = block[:, start : start + HEAD_DIM]
            key = block[:, width + start : width + start + HEAD_DIM]
            value = block[:, 2 * width + start : 2 * width + start + HEAD_DIM]
            scores = dot(query, key, TURNED) * binary
            if period:
                scores = jnp.where(same_place(size, period), scores, -1e30)
            largest = jnp.max(scores, 1, keepdims=True)
            weight = jnp.exp2(scores - largest)
            total = jnp.sum(weight, 1, keepdims=True)
            probs = (weight * (1.0 / total)).astype(jnp.bfloat16)
            outs.append(dot(probs, value, PLAIN))
            logs = jnp.where(log_lane == head, largest + jnp.log(total) * LOG2_E, logs)
        heads_ref[0, group * size : (group + 1) * size, :] = jnp.concatenate(outs, 1).astype(
            jnp.bfloat16
        )
        log_ref[0, group * size : (group + 1) * size, :] = logs
    for half in range(2):
        acc[half] += dot(heads_ref[0], weights[half][0, :, columns - padded :], TURNED)

    @pl.when(step == steps - 1)
    def _():
        for half in range(2):
            total = acc[half] + added_ref[half]
            out_ref[half] = total.astype(jnp.bfloat16)
            mid_ref[half] = stream_ref[half] + mod_ref[half, 2:3, :] * total


def attention_forward(stream, modulation, weights, bias, added, size, period):
    steps = weights[0].shape[0]
    _, tokens, half = stream.shape
    columns = weights[0].shape[2]
    used = round_up(3 * columns // 4)
    padded = columns - (3 * columns // 4) // LANES * LANES
    bf16, f32 = (jnp.bfloat16, jnp.float32)
    return pl.pallas_call(
        functools.partial(attention_kernel, size, period, steps),
        grid=(steps,),
        in_specs=[
            whole(stream.shape),
            whole(modulation.shape),
            stepped((1, used)),
            whole(added.shape),
        ]
        + [stepped((half, columns))] * 2,
        out_specs=[
            whole(stream.shape),
            whole((tokens, half)),
            whole((half, tokens)),
            stepped((tokens, used)),
            stepped((tokens, padded)),
            stepped((tokens, LANES)),
            whole(stream.shape),
        ],
        out_shape=[
            of(stream.shape, f32),
            of((tokens, half), bf16),
            of((half, tokens), bf16),
            of((steps, tokens, used), bf16),
            of((steps, tokens, padded), bf16),
            of((steps, tokens, LANES), f32),
            of(stream.shape, bf16),
        ],
        scratch_shapes=[
            pltpu.VMEM(stream.shape, f32),
            pltpu.VMEM((tokens, half), bf16),
        ],
        compiler_params=pltpu.CompilerParams(vmem_limit_bytes=VMEM_BYTES),
        cost_estimate=SMALL_COST,
        name="attention_forward",
    )(stream, modulation, bias, added, *weights)


def mlp_kernel(steps, *refs):
    mid_ref, mod_ref, bias_ref, added_ref = refs[:4]
    hidden, output = (refs[4:6], refs[6:8])
    stream_ref, mine_ref, other_ref, active_ref, slope_ref, out_ref, acc, kept_ref = refs[8:]
    input_refs = (mine_ref, kept_ref)
    step = pl.program_id(0)

    @pl.when(step == 0)
    def _():
        normed = norm_parts(mid_ref)
        for half in range(2):
            input_refs[half][...] = (
                normed[half] * (1.0 + mod_ref[half, 4:5, :]) + mod_ref[half, 3:4, :]
            ).astype(jnp.bfloat16)
        other_ref[...] = kept_ref[...].T
        acc[...] = jnp.zeros_like(acc)

    pre = dot(input_refs[0][...], hidden[0][0], PLAIN)
    pre = pre + dot(input_refs[1][...], hidden[1][0], PLAIN) + bias_ref[0]
    root = (2.0 / jnp.pi) ** 0.5
    square = pre * pre
    bend = jnp.tanh(pre * (root + root * 0.044715 * square))
    active_ref[0] = (0.5 * pre * (1.0 + bend)).astype(jnp.bfloat16)
    slope_ref[0] = (
        0.5 * (1.0 + bend)
        + 0.5 * pre * (1.0 - bend * bend) * (root + 3.0 * root * 0.044715 * square)
    ).astype(jnp.bfloat16)
    for half in range(2):
        acc[half] += dot(active_ref[0], output[half][0], TURNED)

    @pl.when(step == steps - 1)
    def _():
        for half in range(2):
            total = acc[half] + added_ref[half]
            out_ref[half] = total.astype(jnp.bfloat16)
            stream_ref[half] = mid_ref[half] + mod_ref[half, 5:6, :] * total


def mlp_forward(mid, modulation, hidden, output, bias, added):
    steps = hidden[0].shape[0]
    _, tokens, half = mid.shape
    columns = hidden[0].shape[2]
    bf16, f32 = (jnp.bfloat16, jnp.float32)
    return pl.pallas_call(
        functools.partial(mlp_kernel, steps),
        grid=(steps,),
        in_specs=[
            whole(mid.shape),
            whole(modulation.shape),
            stepped((1, columns)),
            whole(added.shape),
        ]
        + [stepped((half, columns))] * 4,
        out_specs=[
            whole(mid.shape),
            whole((tokens, half)),
            whole((half, tokens)),
            stepped((tokens, columns)),
            stepped((tokens, columns)),
            whole(mid.shape),
        ],
        out_shape=[
            of(mid.shape, f32),
            of((tokens, half), bf16),
            of((half, tokens), bf16),
            of((steps, tokens, columns), bf16),
            of((steps, tokens, columns), bf16),
            of(mid.shape, bf16),
        ],
        scratch_shapes=[
            pltpu.VMEM(mid.shape, f32),
            pltpu.VMEM((tokens, half), bf16),
        ],
        compiler_params=pltpu.CompilerParams(vmem_limit_bytes=VMEM_BYTES),
        cost_estimate=SMALL_COST,
        name="mlp_forward",
    )(mid, modulation, bias, added, *hidden, *output)


def mlp_back_kernel(steps, *refs):
    grad_ref, mid_ref, out_ref, slope_ref, mod_ref = refs[:5]
    hidden, output = (refs[5:7], refs[7:9])
    grad_mid_ref, mine_ref, other_ref, grad_pre_ref, small_ref, sum_ref, acc, kept_ref = refs[9:]
    grad_mlp_refs = (mine_ref, kept_ref)
    step = pl.program_id(0)

    @pl.when(step == 0)
    def _():
        for half in range(2):
            grad = grad_ref[half]
            scaled = (grad * mod_ref[half, 5:6, :]).astype(jnp.bfloat16)
            grad_mlp_refs[half][...] = scaled
            small_ref[half, 2:3, :] = jnp.sum(
                grad * out_ref[half].astype(jnp.float32), 0, keepdims=True
            )
            small_ref[half, 3:4, :] = jnp.sum(scaled.astype(jnp.float32), 0, keepdims=True)
        other_ref[...] = kept_ref[...].T
        acc[...] = jnp.zeros_like(acc)

    grad_act = dot(grad_mlp_refs[0][...], output[0][0], PLAIN)
    grad_act = grad_act + dot(grad_mlp_refs[1][...], output[1][0], PLAIN)
    grad_pre = (grad_act * slope_ref[0].astype(jnp.float32)).astype(jnp.bfloat16)
    grad_pre_ref[0] = grad_pre
    sum_ref[0] = jnp.sum(grad_pre.astype(jnp.float32), 0, keepdims=True)
    for half in range(2):
        acc[half] += dot(grad_pre, hidden[half][0], TURNED)

    @pl.when(step == steps - 1)
    def _():
        norm_grads(mid_ref, acc, mod_ref, 4, grad_ref, grad_mid_ref, small_ref)


def mlp_backward(grad, mid, out, slope, modulation, hidden, output):
    steps = hidden[0].shape[0]
    _, tokens, half = mid.shape
    columns = hidden[0].shape[2]
    bf16, f32 = (jnp.bfloat16, jnp.float32)
    return pl.pallas_call(
        functools.partial(mlp_back_kernel, steps),
        grid=(steps,),
        in_specs=[
            whole(mid.shape),
            whole(mid.shape),
            whole(mid.shape),
            stepped((tokens, columns)),
            whole(modulation.shape),
        ]
        + [stepped((half, columns))] * 4,
        out_specs=[
            whole(mid.shape),
            whole((tokens, half)),
            whole((half, tokens)),
            stepped((tokens, columns)),
            whole((2, 8, half)),
            stepped((1, columns)),
        ],
        out_shape=[
            of(mid.shape, f32),
            of((tokens, half), bf16),
            of((half, tokens), bf16),
            of((steps, tokens, columns), bf16),
            of((2, 8, half), f32),
            of((steps, 1, columns), f32),
        ],
        scratch_shapes=[
            pltpu.VMEM(mid.shape, f32),
            pltpu.VMEM((tokens, half), bf16),
        ],
        compiler_params=pltpu.CompilerParams(vmem_limit_bytes=VMEM_BYTES),
        cost_estimate=SMALL_COST,
        name="mlp_backward",
    )(grad, mid, out, slope, modulation, *hidden, *output)


def attention_back_kernel(size, period, steps, *refs):
    grad_ref, stream_ref, out_ref, qkv_ref, log_ref, mod_ref = refs[:6]
    weights = refs[6:8]
    grad_in_ref, mine_ref, other_ref, grad_qkv_ref, small_ref, sum_ref, acc, kept_ref = refs[8:]
    grad_attn_refs = (mine_ref, kept_ref)
    step = pl.program_id(0)
    tokens = stream_ref.shape[1]
    used = qkv_ref.shape[2]
    columns = weights[0].shape[2]
    width = columns // 4
    padded = columns - (3 * width) // LANES * LANES
    count = width // HEAD_DIM
    scale = HEAD_DIM ** (-0.5)
    binary = scale * LOG2_E

    @pl.when(step == 0)
    def _():
        for half in range(2):
            grad = grad_ref[half]
            scaled = (grad * mod_ref[half, 2:3, :]).astype(jnp.bfloat16)
            grad_attn_refs[half][...] = scaled
            small_ref[half, 2:3, :] = jnp.sum(
                grad * out_ref[half].astype(jnp.float32), 0, keepdims=True
            )
            small_ref[half, 3:4, :] = jnp.sum(scaled.astype(jnp.float32), 0, keepdims=True)
        other_ref[...] = kept_ref[...].T
        acc[...] = jnp.zeros_like(acc)

    grad_heads = dot(grad_attn_refs[0][...], weights[0][0, :, columns - padded :], PLAIN)
    grad_heads = grad_heads + dot(grad_attn_refs[1][...], weights[1][0, :, columns - padded :], PLAIN)
    grad_heads = grad_heads.astype(jnp.bfloat16)
    total = jnp.zeros((1, used), jnp.float32)
    for group in range(tokens // size):
        rows = slice(group * size, (group + 1) * size)
        block = qkv_ref[0, rows, :]
        logs = log_ref[0, rows, :]
        grad_queries, grad_keys, grad_values = ([], [], [])
        for head in range(count):
            start = head * HEAD_DIM
            query = block[:, start : start + HEAD_DIM]
            key = block[:, width + start : width + start + HEAD_DIM]
            value = block[:, 2 * width + start : 2 * width + start + HEAD_DIM]
            start = padded - width + head * HEAD_DIM
            grad_out = grad_heads[rows, start : start + HEAD_DIM]
            scores = dot(query, key, TURNED) * binary - logs[:, head : head + 1]
            if period:
                scores = jnp.where(same_place(size, period), scores, -1e30)
            probs = jnp.exp2(scores)
            grad_probs = dot(grad_out, value, TURNED)
            delta = jnp.sum(probs * grad_probs, 1, keepdims=True)
            grad_scores = (probs * (grad_probs - delta)).astype(jnp.bfloat16)
            grad_values.append(dot(probs.astype(jnp.bfloat16), grad_out, SUMMED))
            grad_queries.append(dot(grad_scores, key, PLAIN) * scale)
            grad_keys.append(dot(grad_scores, query, SUMMED) * scale)
        rest = [jnp.zeros((size, used - 3 * width), jnp.float32)]
        joined = jnp.concatenate(grad_queries + grad_keys + grad_values + rest, 1)
        joined = joined.astype(jnp.bfloat16)
        grad_qkv_ref[0, rows, :] = joined
        total = total + jnp.sum(joined.astype(jnp.float32), 0, keepdims=True)
    sum_ref[0] = total
    for half in range(2):
        acc[half] += dot(grad_qkv_ref[0], weights[half][0, :, :used], TURNED)

    @pl.when(step == steps - 1)
    def _():
        norm_grads(stream_ref, acc, mod_ref, 1, grad_ref, grad_in_ref, small_ref)


def attention_backward(grad, stream, out, qkv, logs, modulation, weights, size, period):
    steps = weights[0].shape[0]
    _, tokens, half = stream.shape
    columns = weights[0].shape[2]
    used = qkv.shape[2]
    bf16, f32 = (jnp.bfloat16, jnp.float32)
    return pl.pallas_call(
        functools.partial(attention_back_kernel, size, period, steps),
        grid=(steps,),
        in_specs=[
            whole(stream.shape),
            whole(stream.shape),
            whole(stream.shape),
            stepped((tokens, used)),
            stepped((tokens, LANES)),
            whole(modulation.shape),
        ]
        + [stepped((half, columns))] * 2,
        out_specs=[
            whole(stream.shape),
            whole((tokens, half)),
            whole((half, tokens)),
            stepped((tokens, used)),
            whole((2, 8, half)),
            stepped((1, used)),
        ],
        out_shape=[
            of(stream.shape, f32),
            of((tokens, half), bf16),
            of((half, tokens), bf16),
            of((steps, tokens, used), bf16),
            of((2, 8, half), f32),
            of((steps, 1, used), f32),
        ],
        scratch_shapes=[
            pltpu.VMEM(stream.shape, f32),
            pltpu.VMEM((tokens, half), bf16),
        ],
        compiler_params=pltpu.CompilerParams(vmem_limit_bytes=VMEM_BYTES),
        cost_estimate=SMALL_COST,
        name="attention_backward",
    )(grad, stream, out, qkv, logs, modulation, *weights)


def weight_kernel(pairs, overlap, steps, *refs):
    inputs = refs[: 4 * pairs]
    outs = refs[4 * pairs : 4 * pairs + 5]
    turned = refs[4 * pairs + 5 : 5 * pairs + 5]
    buffer, sems = refs[5 * pairs + 5 :]
    step = pl.program_id(0)
    slot = step % 2
    for pair in range(pairs):
        mine = inputs[4 * pair]

        @pl.when(step == 0)
        def _():
            turned[pair][...] = mine[...].T

    @pl.when(step >= 2)
    def _():
        pltpu.make_async_copy(buffer.at[slot], outs[0], sems.at[slot]).wait()

    sums = []
    for pair in range(pairs):
        _, rows, mine, theirs = inputs[4 * pair : 4 * pair + 4]
        total = dot(turned[pair][...], mine[0], PLAIN)
        sums.append(total + dot(rows[...], theirs[0], PLAIN))
    if pairs == 1:
        buffer[slot] = sums[0].astype(jnp.bfloat16)
    else:
        first = sums[0].shape[1] - overlap
        buffer[slot, :, :first] = sums[0][:, :first].astype(jnp.bfloat16)
        buffer[slot, :, first : first + overlap] = (
            sums[0][:, first:] + sums[1][:, :overlap]
        ).astype(jnp.bfloat16)
        buffer[slot, :, first + overlap :] = sums[1][:, overlap:].astype(jnp.bfloat16)
    for index in range(steps):

        @pl.when(step == index)
        def _():
            source = buffer.at[index % 2]
            sem = sems.at[index % 2]
            if index == 0:
                pltpu.make_async_copy(source, outs[0], sem).start()
            else:
                rows = outs[1].shape[0]
                upper, lower = (
                    (outs[1], outs[2].at[:rows]),
                    (outs[3].at[:rows], outs[4]),
                    (outs[3].at[rows:], outs[2].at[rows:]),
                )[index - 1]
                pltpu.make_async_copy(source.at[:rows], upper, sem).start()
                pltpu.make_async_copy(source.at[rows:], lower, sem).start()

    @pl.when(step == steps - 1)
    def _():
        for index in range(2):
            pltpu.make_async_copy(buffer.at[index], outs[0], sems.at[index]).wait()


def weight_grads(columns, overlap, *pairs, flops=0):
    steps, tokens, _ = pairs[0][2].shape
    half = pairs[0][1].shape[0]
    bf16 = jnp.bfloat16
    specs, values, turned = ([], [], [])
    for mine, theirs, blocks, their_blocks in pairs:
        specs += [
            whole(mine.shape),
            whole(theirs.shape),
            stepped(blocks.shape[1:]),
            stepped(blocks.shape[1:]),
        ]
        values += [mine, theirs, blocks, their_blocks]
        turned.append(pltpu.VMEM((half, tokens), bf16))
    return pl.pallas_call(
        functools.partial(weight_kernel, len(pairs), overlap, steps),
        grid=(steps,),
        in_specs=specs,
        out_specs=[IN_HBM] * 5,
        out_shape=[
            of((rows, columns), bf16) for rows in (half, half // 2, half, half, half // 2)
        ],
        scratch_shapes=turned
        + [pltpu.VMEM((2, half, columns), bf16), pltpu.SemaphoreType.DMA((2,))],
        compiler_params=pltpu.CompilerParams(vmem_limit_bytes=VMEM_BYTES),
        cost_estimate=pl.CostEstimate(flops=flops, bytes_accessed=0, transcendentals=0),
        name="weight_grads",
    )(*values)


def pack_kernel(held, across, above, lower, upper, out, buffer, sems):
    size = held.shape[0]
    half = size // 2
    corner = pl.ds(lower.shape[0] - half, half)
    incoming = [
        pltpu.make_async_copy(source, target, sems.at[index])
        for index, (source, target) in enumerate(
            (
                (held, buffer.at[0]),
                (across.at[:size], buffer.at[1]),
                (above.at[:size], buffer.at[2]),
                (upper.at[corner], buffer.at[3, :half]),
                (lower.at[corner], buffer.at[3, half:]),
            )
        )
    ]
    outgoing = [
        pltpu.make_async_copy(buffer.at[index], out.at[index], sems.at[5 + index])
        for index in range(4)
    ]
    for copy in incoming:
        copy.start()
    for index in range(3):
        incoming[index].wait()
        outgoing[index].start()
    incoming[3].wait()
    incoming[4].wait()
    outgoing[3].start()
    for copy in outgoing:
        copy.wait()


def pack_blocks(blocks):
    shape = (4,) + blocks[0].shape
    return pl.pallas_call(
        pack_kernel,
        in_specs=[IN_HBM] * 5,
        out_specs=IN_HBM,
        out_shape=of(shape, jnp.bfloat16),
        scratch_shapes=[pltpu.VMEM(shape, jnp.bfloat16), pltpu.SemaphoreType.DMA((9,))],
        compiler_params=pltpu.CompilerParams(vmem_limit_bytes=VMEM_BYTES // 4),
        cost_estimate=SMALL_COST,
        name="pack_blocks",
    )(*blocks)


def placing_matrix(core, part, block, half, shape):
    feature = lax.broadcasted_iota(jnp.int32, shape, 0) + block * shape[0]
    target = lax.broadcasted_iota(jnp.int32, shape, 1)
    row = feature // part
    match = (row & 1) == (core ^ half)
    match &= (row // 2) * part + (feature - row * part) == target
    return jnp.where(match, 1.0, 0.0).astype(jnp.bfloat16)


def enter_kernel(part, where_ref, *refs):
    *blocks, out_ref = refs
    shape = (blocks[0].shape[1], out_ref.shape[2])
    for half in range(2):
        total = None
        for step, block in enumerate(blocks):
            matrix = placing_matrix(where_ref[0], part, where_ref[1] ^ step, half, shape)
            term = dot(block[...], matrix, PLAIN)
            total = term if total is None else total + term
        out_ref[half] = total


def leave_kernel(part, where_ref, halves_ref, *outs):
    shape = (outs[0].shape[1], halves_ref.shape[2])
    halves = [halves_ref[half].astype(jnp.bfloat16) for half in range(2)]
    for step, out in enumerate(outs):
        total = None
        for half in range(2):
            matrix = placing_matrix(where_ref[0], part, where_ref[1] ^ step, half, shape)
            term = dot(halves[half], matrix, TURNED)
            total = term if total is None else total + term
        out[...] = total.astype(jnp.bfloat16)


def assemble_kernel(where_ref, *refs):
    *blocks, out_ref = refs
    for step, block in enumerate(blocks):
        out_ref[where_ref[1] ^ step] = block[...].astype(out_ref.dtype)


def reorder(kernel, values, outs, place):
    in_vmem = pl.BlockSpec(memory_space=pltpu.VMEM)
    where = jnp.stack((place.core, place.col)).astype(jnp.int32)
    return pl.pallas_call(
        kernel,
        in_specs=[pl.BlockSpec(memory_space=pltpu.SMEM)] + [in_vmem] * len(values),
        out_specs=[in_vmem] * len(outs),
        out_shape=outs,
        compiler_params=pltpu.CompilerParams(vmem_limit_bytes=VMEM_BYTES // 2),
        cost_estimate=SMALL_COST,
        name="reorder",
    )(where, *values)


def add_kernel(held, across_upper, across_first, above_first, above_lower, out):
    rows = across_upper.shape[0]
    for start, pair in ((0, (across_upper, above_first)), (rows, (across_first, above_lower))):
        total = held[start : start + rows].astype(jnp.float32)
        for value in pair:
            total += value[:rows].astype(jnp.float32)
        out[start : start + rows] = total.astype(jnp.bfloat16)


def add_blocks(blocks):
    in_vmem = pl.BlockSpec(memory_space=pltpu.VMEM)
    return pl.pallas_call(
        add_kernel,
        in_specs=[in_vmem] * 5,
        out_specs=in_vmem,
        out_shape=of(blocks[0].shape, jnp.bfloat16),
        compiler_params=pltpu.CompilerParams(vmem_limit_bytes=VMEM_BYTES // 2),
        cost_estimate=SMALL_COST,
        name="add_blocks",
    )(*blocks)


def token_parallel(
    tokens,
    conditioning,
    ada_weight,
    ada_bias,
    qkv_weight,
    attn_bias,
    mixing_weight,
    mixing_bias,
    hidden_weight,
    hidden_bias,
    output_weight,
    output_bias,
    cotangent,
):
    place = Place()
    col_width = ada_bias.shape[2]
    row_width = conditioning.shape[1]
    hidden_width = hidden_bias.shape[1]
    layer_count = ada_bias.shape[0]
    clip_count = conditioning.shape[0]
    width = col_width * place.col_count

    copies = (place.row_count // 2, 1)

    def attn_shards(*gate):
        first, second = together(qkv_weight, mixing_weight, *gate)[:2]
        return [
            jnp.tile(
                jnp.concatenate(
                    (
                        first[depth].reshape(row_width, 3 * col_width),
                        second[depth].reshape(col_width, row_width).T,
                    ),
                    1,
                ),
                copies,
            )
            for depth in range(layer_count)
        ]

    def hidden_shards(*gate):
        value = after(hidden_weight, *gate)
        return [
            jnp.tile(value[depth].reshape(row_width, hidden_width), copies)
            for depth in range(layer_count)
        ]

    def output_shards(*gate):
        value = after(output_weight, *gate)
        return [
            jnp.tile(value[depth].reshape(hidden_width, row_width).T, copies)
            for depth in range(layer_count)
        ]

    def arriving(held):
        return trade(relative(held.reshape(clip_count, -1, col_width), place))

    def entered(blocks):
        outs = [of((2, blocks[0].shape[0], width // 2), jnp.float32)]
        return reorder(functools.partial(enter_kernel, row_width), blocks, outs, place)[0]

    gathering = Gathering(place)
    attn_ready = attn_shards()
    tokens = after(open_tokens(tokens, col_width), attn_ready[0])
    cotangent = open_tokens(cotangent, col_width)
    frame_part, places = tokens.shape[1:3]
    frames, place_part = cotangent.shape[1:3]
    period = 16 if place_part % 16 == 0 else place_part
    groups = place_part // period
    first_size = places
    second_size = frames * period
    gathering.step(attn_ready[0])
    token_blocks = arriving(tokens)
    hidden_ready = hidden_shards(attn_ready[0])
    hidden_ready, attn_ready, token_blocks = together(hidden_ready, attn_ready, token_blocks)
    gathering.step(hidden_ready[0], *token_blocks)
    conditioning, ada_weight, attn_bias, token_blocks, output_gate = after(
        (conditioning, ada_weight, attn_bias, token_blocks, output_weight), *gathering.sent
    )
    output_weight = output_gate
    output_ready = output_shards()
    stream_first = entered(token_blocks)
    ada_weight = ada_weight.reshape(layer_count, row_width, 6, col_width)

    half = width // 2

    def leaving(halves):
        outs = [of((halves.shape[1], col_width), jnp.bfloat16)] * place.col_count
        return reorder(functools.partial(leave_kernel, row_width), [halves], outs, place)

    def assembled(blocks, dtype):
        outs = [of((len(blocks),) + blocks[0].shape, dtype)]
        return reorder(assemble_kernel, blocks, outs, place)[0]

    cond_act = jax.nn.silu(conditioning).astype(jnp.bfloat16)
    modulation = matmul("cr,lrsk->clsk", cond_act, ada_weight)
    modulation = modulation.reshape(clip_count, -1)
    cut = modulation.shape[1]
    own = [modulation] + [
        value.reshape(clip_count, -1)
        for value in (attn_bias, hidden_bias, mixing_bias, output_bias, ada_bias)
    ]
    met = lax.all_gather(jnp.concatenate(own, 1), ("row", "col"), axis=0)
    met = met.reshape(place.row_count, place.col_count, clip_count, -1)
    modulation = lax.dynamic_index_in_dim(met, place.col, 2, keepdims=False)[:, :, :cut]
    modulation = jnp.sum(modulation, 0).reshape(-1, layer_count, 6, col_width)
    rest = met[0, :, :, cut:]
    vectors = []
    for value in (attn_bias, hidden_bias, mixing_bias, output_bias, ada_bias):
        size = value.size // clip_count
        vectors.append(rest[:, :, :size].reshape((place.col_count,) + value.shape))
        rest = rest[:, :, size:]
    modulation = modulation + vectors.pop()
    modulation = jnp.moveaxis(modulation, 0, 2).reshape(layer_count, 6, width)
    modulation = jnp.swapaxes(to_halves(modulation, place), 1, 2)
    attn_add, hidden_add, mixing_add, output_add = vectors
    attn_add, hidden_add = (relative(value, place) for value in (attn_add, hidden_add))

    def whole_vector(blocks):
        joined = jnp.moveaxis(blocks, 0, 1).reshape(layer_count, width)
        return to_halves(joined, place)

    mixing_add = whole_vector(mixing_add)
    output_add = whole_vector(output_add)

    blank = jnp.zeros((round_up(3 * col_width) - 3 * col_width,), jnp.float32)

    def biases_of(depth):
        attn_rows = [
            jnp.concatenate((block[depth, 0], jnp.zeros_like(block[depth, 0]), block[depth, 1], blank))
            for block in attn_add
        ]
        return (
            jnp.stack(attn_rows)[:, None, :],
            mixing_add[depth][:, None, :],
            jnp.stack([block[depth] for block in hidden_add])[:, None, :],
            output_add[depth][:, None, :],
        )

    attn_biases, mixing_biases, hidden_biases, output_biases = zip(biases_of(0), biases_of(1))
    sizes = (first_size, second_size)
    periods = (0, period)

    def attn_part(depth, stream):
        return attention_forward(
            stream,
            modulation[depth],
            gathering.done[3 * depth],
            attn_biases[depth],
            mixing_biases[depth],
            sizes[depth],
            periods[depth],
        )

    def mlp_part(depth, mid):
        return mlp_forward(
            mid,
            modulation[depth],
            gathering.done[3 * depth + 1],
            gathering.done[3 * depth + 2],
            hidden_biases[depth],
            output_biases[depth],
        )

    def mlp_grads(depth, grad, saved):
        _, mid, _, (_, _, _, slope, mlp_out) = saved
        return mlp_backward(
            grad, mid, mlp_out, slope, modulation[depth], *gathering.done[3 * depth + 1 : 3 * depth + 3]
        )

    def attn_grads(depth, grad_mid, saved):
        stream, _, (_, _, qkv, _, logs, attn_out), _ = saved
        return attention_backward(
            grad_mid,
            stream,
            attn_out,
            qkv,
            logs,
            modulation[depth],
            gathering.done[3 * depth],
            sizes[depth],
            periods[depth],
        )

    def attn_terms(saved, swapped, grad_attn, grad_qkv, received, flops=0):
        input_attn, _, _, heads, _, _ = saved[2]
        columns = 4 * col_width
        return weight_grads(
            columns,
            grad_qkv.shape[2] + heads.shape[2] - columns,
            (input_attn, swapped[0], grad_qkv, received[0]),
            (grad_attn, received[1], heads, swapped[1]),
            flops=flops,
        )

    def output_terms(saved, swapped, grad_mlp, received):
        active = saved[3][2]
        return weight_grads(active.shape[2], 0, (grad_mlp, received, active, swapped[3]))

    def hidden_terms(saved, swapped, grad_pre, received):
        return weight_grads(
            grad_pre.shape[2], 0, (saved[3][0], swapped[2], grad_pre, received)
        )

    gathering.step(output_ready[0], stream_first, *output_ready)
    gathering.step(attn_ready[1], modulation)
    mid_first, *attn_first = attn_part(0, after(stream_first, *gathering.sent))
    gathering.step(hidden_ready[1], mid_first)
    cotangent = after(cotangent, *gathering.sent)
    cotangent = cotangent.reshape(clip_count, frames, groups, period, col_width)
    gradient_blocks = relative(
        jnp.swapaxes(cotangent, 1, 2).reshape(clip_count, -1, col_width), place
    )
    gathering.step(output_ready[1], *gradient_blocks)
    input_attn, heads = after((attn_first[1], attn_first[3]), *gathering.sent)
    swapped_first = [swap(input_attn), swap(heads)]
    output_first, *mlp_first = mlp_part(0, after(mid_first, *gathering.sent))
    saved_first = (stream_first, mid_first, attn_first, mlp_first)
    gathering.step(None, output_first, *swapped_first)
    input_mlp, active, moving = after(
        (mlp_first[1], mlp_first[2], output_first), *gathering.sent
    )
    swapped_first += [swap(input_mlp), swap(active)]
    moving = mine_first(moving.astype(jnp.bfloat16), place, 0)
    moving = moving.reshape(2, frame_part, place.row_count, groups, period, half)
    moving = moving.transpose(0, 2, 3, 1, 4, 5)
    moved = lax.all_to_all(moving, "row", split_axis=1, concat_axis=3, tiled=True)
    gathering.step(None, moved, *swapped_first[2:])
    moved = after(moved, *gathering.sent)
    moved = moved.reshape(2, -1, half)
    stream_second = mine_first(moved, place, 0).astype(jnp.float32)
    gathering.step(None)
    stream_second = after(stream_second, gathering.done[5][0])
    mid_second, *attn_second = attn_part(1, stream_second)
    mid_second, input_attn, heads = together(mid_second, attn_second[1], attn_second[3])
    swapped_second = [swap(input_attn), swap(heads)]
    gradient_blocks = trade(after(gradient_blocks, mid_second))
    output_second, *mlp_second = mlp_part(1, mid_second)
    saved_second = (stream_second, mid_second, attn_second, mlp_second)
    gradient_blocks, swapped_second, input_mlp, active, output_second = together(
        gradient_blocks, swapped_second, mlp_second[1], mlp_second[2], output_second
    )
    grad = entered(gradient_blocks)
    swapped_second += [swap(input_mlp), swap(active)]

    grad_mid, grad_mlp, grad_sent, grad_pre, small_mlp_second, hidden_sum_second = mlp_grads(
        1, grad, saved_second
    )
    grad_mid, grad_mlp, grad_sent, grad_pre, swapped_second, output_second = together(
        grad_mid, grad_mlp, grad_sent, grad_pre, swapped_second, output_second
    )
    received = swap(grad_sent)
    received, grad_pre = together(received, grad_pre)
    received_pre = swap(grad_pre)
    output_part = output_terms(saved_second, swapped_second, grad_mlp, received)
    output_part, received_pre, grad_mid = together(output_part, received_pre, grad_mid)
    output_part = scatter_corner(output_part)
    hidden_part = hidden_terms(saved_second, swapped_second, grad_pre, received_pre)
    hidden_part, grad_mid = together(hidden_part, grad_mid)
    hidden_part = scatter_corner(hidden_part)
    grad_second, grad_attn, grad_sent, grad_qkv, small_attn_second, qkv_sum_second = attn_grads(
        1, grad_mid, saved_second
    )
    grad_second, grad_attn, grad_sent, grad_qkv, output_part, output_second = together(
        grad_second, grad_attn, grad_sent, grad_qkv, output_part, output_second
    )
    received = [swap(grad_qkv), swap(grad_sent)]
    sides = scatter_sides(output_part)
    moving = mine_first(grad_second.astype(jnp.bfloat16), place, 0)
    moving = moving.reshape(2, 1, groups, frames, period, half)
    received, grad_attn, grad_qkv, sides, moving = together(
        received, grad_attn, grad_qkv, sides, moving
    )
    output_part = scatter_plane(output_part, sides)
    attn_blocks = attn_terms(saved_second, swapped_second, grad_attn, grad_qkv, received)
    attn_blocks, moving, hidden_part = together(attn_blocks, moving, hidden_part)
    moved = lax.all_to_all(moving, "row", split_axis=3, concat_axis=1, tiled=True)
    attn_part_second = scatter_corner(attn_blocks)
    result_blocks = leaving(after(output_second, *attn_blocks))
    sides = scatter_sides(hidden_part)
    output_total = add_blocks(output_part)
    moved, output_total, sides, result_blocks = together(
        moved, output_total, sides, result_blocks
    )
    hidden_part = scatter_plane(hidden_part, sides)
    moved = moved.transpose(0, 3, 1, 2, 4, 5).reshape(2, -1, half)
    returned = mine_first(moved, place, 0).astype(jnp.float32)
    output_pieces = over_depth(output_total, place)
    result_blocks = trade(after(result_blocks, output_total))
    grad_mid, grad_mlp, grad_sent, grad_pre, small_mlp_first, hidden_sum_first = mlp_grads(
        0, returned, saved_first
    )
    grad_mid, grad_mlp, grad_sent, grad_pre, output_pieces, hidden_part, result_blocks = together(
        grad_mid, grad_mlp, grad_sent, grad_pre, output_pieces, hidden_part, result_blocks
    )
    received = swap(grad_sent)
    hidden_total = add_blocks(hidden_part)
    received, hidden_total, grad_pre = together(received, hidden_total, grad_pre)
    hidden_pieces = over_depth(hidden_total, place)
    received_pre = swap(grad_pre)
    output_blocks = output_terms(saved_first, swapped_first, grad_mlp, received)
    output_blocks, received_pre = together(output_blocks, received_pre)
    output_part = scatter_corner(output_blocks)
    hidden_blocks = hidden_terms(saved_first, swapped_first, grad_pre, received_pre)
    hidden_blocks, grad_mid, attn_part_second = together(
        hidden_blocks, grad_mid, attn_part_second
    )
    sides = scatter_sides(attn_part_second)
    grad_mid, sides = together(grad_mid, sides)
    attn_part_second = scatter_plane(attn_part_second, sides)
    hidden_part = scatter_corner(hidden_blocks)
    grad_first, grad_attn, grad_sent, grad_qkv, small_attn_first, qkv_sum_first = attn_grads(
        0, grad_mid, saved_first
    )
    (
        grad_first,
        grad_attn,
        grad_sent,
        grad_qkv,
        output_part,
        attn_part_second,
        hidden_pieces,
    ) = together(
        grad_first, grad_attn, grad_sent, grad_qkv, output_part, attn_part_second, hidden_pieces
    )
    received = [swap(grad_qkv), swap(grad_sent)]
    sides = scatter_sides(output_part)
    attn_total = add_blocks(attn_part_second)
    received, sides, attn_total, grad_attn, grad_qkv = together(
        received, sides, attn_total, grad_attn, grad_qkv
    )
    output_part = scatter_plane(output_part, sides)
    attn_pieces = over_depth(attn_total, place)
    attn_blocks = attn_terms(saved_first, swapped_first, grad_attn, grad_qkv, received)
    def small_grads(small_attn, small_mlp, qkv_sum, hidden_sum):
        return (
            jnp.concatenate((small_attn[:, :3], small_mlp[:, :3]), 1),
            (qkv_sum[:, 0], small_attn[:, 3], hidden_sum[:, 0], small_mlp[:, 3]),
        )

    modgrad_first, biasgrad_first = small_grads(
        small_attn_first, small_mlp_first, qkv_sum_first, hidden_sum_first
    )
    modgrad_second, biasgrad_second = small_grads(
        small_attn_second, small_mlp_second, qkv_sum_second, hidden_sum_second
    )
    def by_block(halves):
        features = from_halves(halves, place)
        features = features.reshape(features.shape[:-1] + (place.col_count, col_width))
        return relative(jnp.moveaxis(features, -2, 0), place)

    modgrad = by_block(jnp.swapaxes(jnp.stack((modgrad_first, modgrad_second)), 1, 2))
    mixgrad = by_block(jnp.stack((biasgrad_first[1], biasgrad_second[1])))
    outgrad = by_block(jnp.stack((biasgrad_first[3], biasgrad_second[3])))
    sending = []
    for step in range(place.col_count):
        pieces = [modgrad[step].reshape(-1)]
        for grads in (biasgrad_first, biasgrad_second):
            pieces.append(grads[0][step][:col_width])
            pieces.append(grads[0][step][2 * col_width : 3 * col_width])
        for grads in (biasgrad_first, biasgrad_second):
            pieces.append(grads[2][step])
        pieces.append(mixgrad[step].reshape(-1))
        pieces.append(outgrad[step].reshape(-1))
        sending.append(jnp.concatenate(pieces))
    sending = [value.reshape(-1, LANES) for value in sending]
    attn_blocks, output_part, hidden_part, grad_first, result_blocks = together(
        attn_blocks, output_part, hidden_part, grad_first, result_blocks
    )
    attn_part_first = scatter_corner(attn_blocks)
    sides = scatter_sides(hidden_part)
    output_total = add_blocks(output_part)
    output_total, sides, grad_first, attn_pieces = together(
        output_total, sides, grad_first, attn_pieces
    )
    hidden_part = scatter_plane(hidden_part, sides)
    output_first_pieces = over_depth(output_total, place)
    gradient_blocks = leaving(grad_first)

    result = assembled(result_blocks, jnp.bfloat16)
    result = result.reshape(clip_count, groups, frames, period, col_width)
    result = jnp.swapaxes(result, 1, 2).reshape(clip_count, frames, place_part, col_width)
    result = close_tokens(result)
    attn_part_first, hidden_part, gradient_blocks, sending, result = together(
        attn_part_first, hidden_part, gradient_blocks, sending, result
    )
    sides = scatter_sides(attn_part_first)
    hidden_total = add_blocks(hidden_part)
    sides, hidden_total, sending, output_first_pieces = together(
        sides, hidden_total, sending, output_first_pieces
    )
    attn_part_first = scatter_plane(attn_part_first, sides)
    met = trade(sending)
    hidden_first_pieces = over_depth(hidden_total, place)
    met = [value.reshape(-1) for value in met]
    modgrad = jnp.concatenate([block[:cut] for block in met])
    biasgrad = sum(block[cut:] for block in met)
    small = jnp.concatenate((modgrad, biasgrad))
    small = small + swap(small)
    small, attn_part_first = together(small, attn_part_first)
    attn_total = add_blocks(attn_part_first)
    small, attn_total = together(small, attn_total)
    gradient_blocks = trade(gradient_blocks)
    for mask in place.depth_masks:
        small = small + exchange(small, "row", mask)
    sums = [add_all(pieces, place) for pieces in (attn_pieces, hidden_pieces, output_pieces)]
    gradient_blocks, hidden_first_pieces, attn_total, small, sums = together(
        gradient_blocks, hidden_first_pieces, attn_total, small, sums
    )
    attn_first_pieces = over_depth(attn_total, place)
    tokens_gradient = assembled(gradient_blocks, jnp.float32)
    tokens_gradient = tokens_gradient.reshape(clip_count, frame_part, places, col_width)
    first_sums = [
        add_all(pieces, place)
        for pieces in (attn_first_pieces, hidden_first_pieces, output_first_pieces)
    ]
    modgrad = small[: cut * clip_count].reshape(clip_count, layer_count, 6, col_width)
    modgrad = jnp.moveaxis(jnp.stack(relative(modgrad, place)), 1, 0)
    rest = small[cut * clip_count :]
    bias_grads = []
    for value in (attn_bias, hidden_bias, mixing_bias, output_bias):
        bias_grads.append(rest[: value.size].reshape(value.shape))
        rest = rest[value.size :]
    ada_bias_grad = jnp.sum(modgrad, 1)
    ada_weight_grad = jnp.einsum(
        "cr,lcsk->lrsk", cond_act.astype(jnp.float32), modgrad, precision=highest
    )
    cond_part = jnp.einsum(
        "lcsk,lrsk->cr", modgrad, ada_weight.astype(jnp.float32), precision=highest
    )
    for mask in (1, 2):
        cond_part = cond_part + exchange(cond_part, "col", mask)
    conditioning_gradient = jax.vjp(jax.nn.silu, conditioning)[1](cond_part)[0]

    attn_sums, hidden_sums, output_sums = (
        jnp.stack((first_sums[index], sums[index])) for index in range(3)
    )
    return (
        result,
        close_tokens(tokens_gradient),
        conditioning_gradient,
        close_weight(ada_weight_grad),
        ada_bias_grad,
        close_weight(attn_sums[:, :, : 3 * col_width]),
        bias_grads[0],
        close_weight(jnp.swapaxes(attn_sums[:, :, 3 * col_width :], 1, 2)),
        bias_grads[2],
        close_weight(hidden_sums),
        bias_grads[1],
        close_weight(jnp.swapaxes(output_sums, 1, 2)),
        bias_grads[3],
    )


def suits_tokens(mesh):
    rows, cols = (mesh.shape["row"], mesh.shape["col"])
    return cols == 4 and rows >= 2 and rows & (rows - 1) == 0


def solution(mesh):
    placed = (
        P(None, "row", "col", None),
        P(None, "row"),
        P(None, "row", "col", None),
        P(None, None, "col"),
        P(None, "row", "col", None),
        P(None, None, "col"),
        P(None, "col", "row", None),
        P(None, "col"),
        P(None, "row", "col", None),
        P(None, "col"),
        P(None, "col", "row", None),
        P(None, "col"),
        P(None, None, "col", "row"),
    )
    return jax.shard_map(
        token_parallel if suits_tokens(mesh) else tensor_parallel,
        mesh=mesh,
        in_specs=placed,
        out_specs=(
            P(None, None, "col", "row"),
            P(None, "row", "col", None),
            P(None, "row"),
            P(None, "row", "col", None),
            P(None, None, "col"),
            P(None, "row", "col", None),
            P(None, None, "col"),
            P(None, "col", "row", None),
            P(None, "col"),
            P(None, "row", "col", None),
            P(None, "col"),
            P(None, "col", "row", None),
            P(None, "col"),
        ),
        check_vma=False,
    )
```
